128 devices in a mesh: gy: 8 (over x, core), gx: 8 (over z, y_lo), ctx: 2 (over y_hi).
Axes of the slice: x: 4, y: 4 (y_hi: 2, y_lo: 2; y = y_hi * 2 + y_lo), z: 4, core: 2. Of those that a mesh axis runs over, the one named last changes fastest.
Arguments:
- fine: bfloat16 [256, 256, 128], P(('gy', 'ctx'), 'gx'), may hold values from -6 to 6
- context: bfloat16 [64, 64, 512], P('gy', 'gx', 'ctx'), may hold values from -6 to 6
- interp_rows: bfloat16 [34, 10], replicated, may hold values from -2 to 2
- interp_cols: bfloat16 [34, 10], replicated, may hold values from -2 to 2
- fine_weight: bfloat16 [3, 3, 128, 128], replicated, may hold values from -0.078125 to 0.078125
- ctx_weight: bfloat16 [3, 3, 512, 128], replicated, may hold values from -0.09375 to 0.09375
- conv_weight: bfloat16 [3, 3, 128, 128], replicated, may hold values from -0.1875 to 0.1875
- hidden_weight: bfloat16 [128, 1024], replicated, may hold values from -0.5 to 0.5
- bin_weight: bfloat16 [1024, 512], replicated, may hold values from -0.75 to 0.75
- cell_index: int32 [16, 8, 256], P(('gy', 'ctx'), 'gx'), may hold values from 0 to 511, as said below
- counts: int32 [16, 8], P(('gy', 'ctx'), 'gx'), may hold values from 0 to 256, as said below
- labels: int32 [16, 8, 256], P(('gy', 'ctx'), 'gx'), may hold values from 0 to 511
Outputs:
- loss: float32 [], replicated
- grad_fine_weight: float32 [3, 3, 128, 128], replicated
- grad_ctx_weight: float32 [3, 3, 512, 128], P(None, None, 'ctx')
- grad_conv_weight: float32 [3, 3, 128, 128], replicated
- grad_hidden_weight: float32 [128, 1024], replicated
- grad_bin_weight: float32 [1024, 512], replicated
The draws below stay inside these ranges and needn't reach their ends.
Inputs may be any that keep to these rules, and one draw needn't show every extreme that they name: `cell_index`: within one device's slots the indices are distinct; slots at or past the count also hold valid indices. `counts`: some device has all 256 slots live in every draw.
All inputs are finite; a program needn't handle non-finite values.
Results may differ from the reference program's by a relative error of at most 0.01.
Values may be sent and summed in bfloat16 or wider, within the bound.
No kernel may reach another device: no remote copies, remote signals or barrier semaphores. Data moves between devices by JAX's collectives and lax.ppermute only.
A program may use at most 64 MiB of HBM per device.

```python
import jax
import jax.numpy as jnp
from jax import lax

C = 128
K = 512
HID = 1024
BINS = 512
ROWS_DEV = 16
COLS_DEV = 32
TILE_ROWS = 32
COARSE_ROWS = 8
COARSE_COLS = 8
CELLS = 512
CAP = 256
ROW_BLOCKS = 16
NY = 256
NX = 256
MY = 64
MX = 64
N_GY = 8
N_GX = 8


def draw_counts(key, part):
    key = jax.random.fold_in(key, 1)
    level = jax.random.randint(key, (ROW_BLOCKS * N_GX,), 1, 9)
    filled = CAP * level * level // 64
    pick = jax.random.randint(jax.random.fold_in(key, 5), (), 0, ROW_BLOCKS * N_GX)
    filled = jnp.where(jnp.arange(ROW_BLOCKS * N_GX) == pick, CAP, filled)
    return filled.reshape(ROW_BLOCKS, N_GX).astype(jnp.int32)


def draw_cell_index(key, part):
    key = jax.random.fold_in(key, 2)
    keys = jax.random.split(key, ROW_BLOCKS * N_GX)
    picks = jax.vmap(lambda k: jax.random.permutation(k, CELLS)[:CAP])(keys)
    return picks.reshape(ROW_BLOCKS, N_GX, CAP).astype(jnp.int32)


def place_ends(entries, own_key, smallest, high):
    spot = [jax.random.randint(jax.random.fold_in(own_key, axis), (), 0, length) for axis, length in enumerate(entries.shape)]
    main_axis = entries.shape.index(max(entries.shape))
    next_to = spot[:main_axis] + [(spot[main_axis] + 1) % entries.shape[main_axis]] + spot[main_axis + 1:]
    return entries.at[tuple(spot)].set(smallest).at[tuple(next_to)].set(high)


def block_scale(key, shape, cuts, least, top_value):
    loudness, own = 1.0, jax.random.fold_in(key, 6)
    for position, shards_of in cuts:
        heights = jnp.exp(jax.random.uniform(jax.random.fold_in(own, position), (shards_of,), jnp.float32, least / len(cuts), top_value / len(cuts)))
        loudness = loudness * jnp.repeat(heights, shape[position] // shards_of).reshape([-1 if axis == position else 1 for axis in range(len(shape))])
    return loudness


def noise(stream_key, shape, deviation, bound, cuts=(), kind=jnp.bfloat16):
    array = jax.random.normal(stream_key, shape, jnp.float32) * deviation
    if len(cuts) > 0:
        array = block_scale(stream_key, shape, cuts, -0.22, 0.18) * array
    return jnp.clip(array, min=-bound, max=bound).astype(kind)


def setup_inputs(seed: int = 0) -> dict:
    key_of = jax.random.split(jax.random.key(seed), 13)
    fine = noise(key_of[0], (NY, NX, C), 1.0, 6.0, ((0, 16), (1, 8)))
    context = noise(key_of[1], (MY, MX, K), 1.0, 6.0, ((0, 8), (1, 8), (2, 2)))
    interp_rows = noise(key_of[2], (TILE_ROWS + 2, COARSE_ROWS + 2), (COARSE_ROWS + 2) ** -0.5, 2.0)
    interp_cols = noise(key_of[3], (COLS_DEV + 2, COARSE_COLS + 2), (COARSE_COLS + 2) ** -0.5, 2.0)
    fine_weight = noise(key_of[4], (3, 3, C, C), (9 * (C + K)) ** -0.5, 0.078125)
    ctx_weight = noise(key_of[5], (3, 3, K, C), (9 * K) ** -0.5, 0.09375)
    conv_weight = noise(key_of[6], (3, 3, C, C), (9 * C) ** -0.5, 0.1875)
    hidden_weight = noise(key_of[7], (C, HID), C ** -0.5, 0.5)
    bin_weight = noise(key_of[8], (HID, BINS), (HID // 16) ** -0.5, 0.75)
    cell_index = draw_cell_index(jax.random.fold_in(key_of[12], 71), 0)
    counts = draw_counts(jax.random.fold_in(key_of[12], 71), 0)
    labels = place_ends(jax.random.randint(key_of[11], (ROW_BLOCKS, N_GX, CAP), 0, BINS), jax.random.fold_in(key_of[11], 1), 0, BINS - 1).astype(jnp.int32)
    return {"fine": fine, "context": context, "interp_rows": interp_rows, "interp_cols": interp_cols, "fine_weight": fine_weight, "ctx_weight": ctx_weight, "conv_weight": conv_weight, "hidden_weight": hidden_weight, "bin_weight": bin_weight, "cell_index": cell_index, "counts": counts, "labels": labels}


def silu_grad(v):
    s = jax.nn.sigmoid(v)
    return s * (1.0 + v * (1.0 - s))

def conv_rows(padded, weight, rows, cols):
    total = None
    for dy in range(3):
        for dx in range(3):
            patch = padded[dy:dy + rows, dx:dx + cols, :].reshape(rows * cols, -1)
            term = jnp.dot(patch, weight[dy, dx], preferred_element_type=jnp.float32)
            total = term if total is None else total + term
    return total.reshape(rows, cols, -1)

def weight_grad(padded, grad, rows, cols):
    flat_grad = grad.reshape(rows * cols, -1)
    parts = []
    for dy in range(3):
        for dx in range(3):
            patch = padded[dy:dy + rows, dx:dx + cols, :].reshape(rows * cols, -1)
            parts.append(lax.dot_general(patch, flat_grad, (((0,), (0,)), ((), ())), preferred_element_type=jnp.float32))
    return jnp.stack(parts).reshape(3, 3, padded.shape[2], flat_grad.shape[1])

def conv_back(gpad, weight, rows, cols):
    total = None
    for dy in range(3):
        for dx in range(3):
            patch = gpad[2 - dy:2 - dy + rows, 2 - dx:2 - dx + cols, :].reshape(rows * cols, -1)
            term = lax.dot_general(patch, weight[dy, dx], (((1,), (1,)), ((), ())), preferred_element_type=jnp.float32)
            total = term if total is None else total + term
    return total.reshape(rows, cols, -1)

def context_field(block, row_mat, col_mat, row_start, col_start):
    mid = jnp.einsum('ia,abk->ibk', row_mat.astype(jnp.float32), block.astype(jnp.float32)).astype(jnp.bfloat16)
    wide = jnp.einsum('jb,ibk->ijk', col_mat.astype(jnp.float32), mid.astype(jnp.float32))
    grow = row_start + jnp.arange(row_mat.shape[0], dtype=jnp.int32) - 1
    gcol = col_start + jnp.arange(col_mat.shape[0], dtype=jnp.int32) - 1
    keep = ((grow >= 0) & (grow < NY))[:, None] & ((gcol >= 0) & (gcol < NX))[None, :]
    return (wide * keep[:, :, None].astype(jnp.float32)).astype(jnp.bfloat16)

def head_rows(rows, lab, weight, hidden_weight, bin_weight):
    z = jnp.dot(rows, hidden_weight, preferred_element_type=jnp.float32)
    act = jax.nn.silu(z).astype(jnp.bfloat16)
    logits = jnp.dot(act, bin_weight, preferred_element_type=jnp.float32)
    top = jax.nn.logsumexp(logits, axis=1)
    onehot = (lab[:, None] == jnp.arange(logits.shape[1], dtype=jnp.int32)[None, :]).astype(jnp.float32)
    picked = lax.optimization_barrier(jnp.sum(logits * onehot, axis=1))
    loss = jnp.sum(weight * (top - picked))
    probs = jnp.exp(logits - top[:, None])
    dlogits = ((probs - onehot) * weight[:, None]).astype(jnp.bfloat16)
    gbin = lax.dot_general(act, dlogits, (((0,), (0,)), ((), ())), preferred_element_type=jnp.float32)
    dact = lax.dot_general(dlogits, bin_weight, (((1,), (1,)), ((), ())), preferred_element_type=jnp.float32)
    dz = (dact * silu_grad(z)).astype(jnp.bfloat16)
    ghid = lax.dot_general(rows, dz, (((0,), (0,)), ((), ())), preferred_element_type=jnp.float32)
    drows = lax.dot_general(dz, hidden_weight, (((1,), (1,)), ((), ())), preferred_element_type=jnp.float32)
    return (loss, ghid, gbin, drows)

def tile_place(t):
    ty = (t // N_GX).astype(jnp.int32)
    tx = (t % N_GX).astype(jnp.int32)
    return (ty, tx)

def reference(fine, context, interp_rows, interp_cols, fine_weight, ctx_weight, conv_weight, hidden_weight, bin_weight, cell_index, counts, labels):
    tiles = N_GY * N_GX
    zero = jnp.zeros((), jnp.int32)
    fine_pad = jnp.pad(fine, ((1, 1), (1, 1), (0, 0)))
    pre_one = conv_rows(fine_pad, fine_weight, NY, NX)
    coarse_pad = jnp.pad(context, ((1, 1), (1, 1), (0, 0)))

    def tile_field(t):
        ty, tx = tile_place(t)
        row_at = (ty * COARSE_ROWS).astype(jnp.int32)
        col_at = (tx * COARSE_COLS).astype(jnp.int32)
        block = lax.dynamic_slice(coarse_pad, (row_at, col_at, zero), (COARSE_ROWS + 2, COARSE_COLS + 2, K))
        fine_row = (ty * TILE_ROWS).astype(jnp.int32)
        fine_col = (tx * COLS_DEV).astype(jnp.int32)
        return (context_field(block, interp_rows, interp_cols, fine_row, fine_col), fine_row, fine_col)

    def add_tile(acc, t):
        field, fine_row, fine_col = tile_field(t)
        term = conv_rows(field, ctx_weight, TILE_ROWS, COLS_DEV)
        place = lax.dynamic_slice(acc, (fine_row, fine_col, zero), (TILE_ROWS, COLS_DEV, C))
        return (lax.dynamic_update_slice(acc, place + term, (fine_row, fine_col, zero)), None)
    pre_one, _ = lax.scan(add_tile, pre_one, jnp.arange(tiles, dtype=jnp.int32))
    h_one = jax.nn.silu(pre_one).astype(jnp.bfloat16)
    h_one_pad = jnp.pad(h_one, ((1, 1), (1, 1), (0, 0)))
    pre_two = conv_rows(h_one_pad, conv_weight, NY, NX)
    h_two = jax.nn.silu(pre_two).astype(jnp.bfloat16)
    blocks = ROW_BLOCKS * N_GX
    h_blocks = h_two.reshape(ROW_BLOCKS, ROWS_DEV, N_GX, COLS_DEV, C).transpose(0, 2, 1, 3, 4).reshape(blocks, CELLS, C)
    idx = cell_index.reshape(blocks, CAP).astype(jnp.int32)
    labs = labels.reshape(blocks, CAP).astype(jnp.int32)
    nums = counts.reshape(blocks).astype(jnp.int32)
    total = jnp.sum(nums.astype(jnp.float32))

    def head_block(carry, xs):
        cells, ids, lab, num = xs
        weight = (jnp.arange(CAP, dtype=jnp.int32) < num).astype(jnp.float32) / total
        loss, ghid, gbin, drows = head_rows(cells[ids], lab, weight, hidden_weight, bin_weight)
        grad_cells = jnp.zeros((CELLS, C), jnp.float32).at[ids].add(drows)
        return ((carry[0] + loss, carry[1] + ghid, carry[2] + gbin), grad_cells)
    init = (jnp.zeros((), jnp.float32), jnp.zeros((C, HID), jnp.float32), jnp.zeros((HID, BINS), jnp.float32))
    (loss, ghid, gbin), grad_blocks = lax.scan(head_block, init, (h_blocks, idx, labs, nums))
    dh_two = grad_blocks.reshape(ROW_BLOCKS, N_GX, ROWS_DEV, COLS_DEV, C).transpose(0, 2, 1, 3, 4).reshape(NY, NX, C)
    g_two = (dh_two * silu_grad(pre_two)).astype(jnp.bfloat16)
    gconv = weight_grad(h_one_pad, g_two, NY, NX)
    g_two_pad = jnp.pad(g_two, ((1, 1), (1, 1), (0, 0)))
    g_one = (conv_back(g_two_pad, conv_weight, NY, NX) * silu_grad(pre_one)).astype(jnp.bfloat16)
    gfine = weight_grad(fine_pad, g_one, NY, NX)

    def grad_tile(acc, t):
        field, fine_row, fine_col = tile_field(t)
        gtile = lax.dynamic_slice(g_one, (fine_row, fine_col, zero), (TILE_ROWS, COLS_DEV, C))
        return (acc + weight_grad(field, gtile, TILE_ROWS, COLS_DEV), None)
    gctx, _ = lax.scan(grad_tile, jnp.zeros((3, 3, K, C), jnp.float32), jnp.arange(tiles, dtype=jnp.int32))
    return (loss, gfine, gctx, gconv, ghid, gbin)
```

```python
import jax
import jax.numpy as jnp
import numpy as np
from jax import lax
from jax.sharding import Mesh
from jax.sharding import PartitionSpec as P

HID = 1024
BINS = 512
CAP = 256
ROWS = 16
COLS = 32
C = 128
K = 512
HALF = 256
SHARD = 96
PEERS = 64
BODY = 12032

GY = ("x", "core")
GX = ("z", "yl")
TALL = ("x", "core", "yh")
PLANE = ("x", "z", "yl", "yh")

BF = jnp.bfloat16
F32 = jnp.float32


def silu_grad(v):
    s = jax.nn.sigmoid(v)
    return s * (1.0 + v * (1.0 - s))


def conv_rows(padded, weight, rows, cols):
    total = None
    for dy in range(3):
        for dx in range(3):
            patch = padded[dy : dy + rows, dx : dx + cols, :].reshape(rows * cols, -1)
            term = jnp.dot(patch, weight[dy, dx], preferred_element_type=F32)
            total = term if total is None else total + term
    return total.reshape(rows, cols, -1)


def weight_grad(padded, grad, rows, cols):
    flat_grad = grad.reshape(rows * cols, -1)
    parts = []
    for dy in range(3):
        for dx in range(3):
            patch = padded[dy : dy + rows, dx : dx + cols, :].reshape(rows * cols, -1)
            parts.append(
                lax.dot_general(
                    patch, flat_grad, (((0,), (0,)), ((), ())), preferred_element_type=F32
                )
            )
    return jnp.stack(parts)


def conv_back(gpad, weight, rows, cols):
    total = None
    for dy in range(3):
        for dx in range(3):
            patch = gpad[2 - dy : 2 - dy + rows, 2 - dx : 2 - dx + cols, :].reshape(rows * cols, -1)
            term = lax.dot_general(
                patch, weight[dy, dx], (((1,), (1,)), ((), ())), preferred_element_type=F32
            )
            total = term if total is None else total + term
    return total.reshape(rows, cols, -1)


def shift(x, axis, count, step):
    pairs = [(i, i + step) for i in range(count) if 0 <= i + step < count]
    return lax.ppermute(x, axis, pairs)


def side_swap(x):
    own = [(2 * t + c, 2 * t + 1 - c) for t in range(8) for c in range(2)]
    return lax.ppermute(x, TALL, own)


def outer_swap(x):
    pairs = []
    for t in range(7):
        pairs += [(2 * t + 1, 2 * t + 2), (2 * t + 2, 2 * t + 1)]
    return lax.ppermute(x, TALL, pairs)


def context_field(block, row_mat, col_mat, row_start, col_start):
    mid = jnp.einsum("ia,abk->ibk", row_mat, block, preferred_element_type=F32).astype(BF)
    wide = jnp.einsum("jb,ibk->ijk", col_mat, mid, preferred_element_type=F32)
    grow = row_start + jnp.arange(row_mat.shape[0], dtype=jnp.int32) - 1
    gcol = col_start + jnp.arange(col_mat.shape[0], dtype=jnp.int32) - 1
    keep = ((grow >= 0) & (grow < 256))[:, None] & ((gcol >= 0) & (gcol < 256))[None, :]
    return (wide * keep[:, :, None].astype(F32)).astype(BF)


def split3(v):
    hi = v.astype(BF)
    rest = v - hi.astype(F32)
    mid = rest.astype(BF)
    low = (rest - mid.astype(F32)).astype(BF)
    return [hi, mid, low]


def head(rows, lab, weight, hidden_weight, bin_weight):
    z = jnp.dot(rows, hidden_weight, preferred_element_type=F32)
    act = jax.nn.silu(z).astype(BF)
    logits = jnp.dot(act, bin_weight, preferred_element_type=F32)
    top = jax.nn.logsumexp(logits, axis=1)
    onehot = (lab[:, None] == jnp.arange(BINS, dtype=jnp.int32)[None, :]).astype(F32)
    picked = jnp.sum(logits * onehot, axis=1)
    loss = jnp.sum((weight * (top - picked))[:CAP])
    probs = jnp.exp(logits - top[:, None])
    dlogits = ((probs - onehot) * weight[:, None]).astype(BF)
    gbin = lax.dot_general(
        act[:CAP], dlogits[:CAP], (((0,), (0,)), ((), ())), preferred_element_type=F32
    )
    dact = lax.dot_general(
        dlogits, bin_weight, (((1,), (1,)), ((), ())), preferred_element_type=F32
    )
    dz = (dact * silu_grad(z)).astype(BF)
    ghid = lax.dot_general(
        rows[:CAP], dz[:CAP], (((0,), (0,)), ((), ())), preferred_element_type=F32
    )
    drows = lax.dot_general(
        dz, hidden_weight, (((1,), (1,)), ((), ())), preferred_element_type=F32
    )
    return loss, ghid, gbin, drows


def local(
    fine,
    context,
    interp_rows,
    interp_cols,
    fine_weight,
    ctx_weight,
    conv_weight,
    hidden_weight,
    bin_weight,
    cell_index,
    counts,
    labels,
):
    core = lax.axis_index("core")
    half = lax.axis_index("yh")
    gy = lax.axis_index(GY)
    gx = lax.axis_index(GX)
    lower = half == 1

    own_idx = cell_index[0, 0]
    own_lab = labels[0, 0]
    own_num = counts[0, 0]
    live = jnp.arange(CAP, dtype=jnp.int32) < own_num

    spot = own_idx[:, None] == jnp.arange(ROWS * COLS, dtype=jnp.int32)[None, :]
    code = jnp.sum(
        jnp.where(spot & live[:, None], own_lab[:, None] + 1, 0), axis=0, dtype=jnp.int32
    )
    digits = jnp.stack([code // 32, code % 32], axis=1).astype(BF).reshape(ROWS, COLS, 2)

    fine_dig = jnp.concatenate([fine, jnp.pad(digits, ((0, 0), (0, 0), (0, 126)))], axis=0)

    def pack_cols(col):
        return jnp.concatenate([fine_dig[:, col], context[:, min(col, 7)].reshape(16, C)], axis=0)

    west = shift(pack_cols(COLS - 1), GX, 8, 1)
    east = shift(pack_cols(0), GX, 8, -1)
    wide = jnp.concatenate([west[:32, None], fine_dig, east[:32, None]], axis=1)
    fine_w, dig_w = wide[:ROWS], wide[ROWS:]
    ctx_w = jnp.concatenate(
        [west[32:].reshape(8, 1, HALF), context, east[32:].reshape(8, 1, HALF)], axis=1
    )
    edge = lambda v, last: lax.dynamic_slice_in_dim(v, jnp.where(last, v.shape[0] - 1, 0), 1, 0)
    inner = jnp.concatenate([edge(fine_w, ~lower), edge(dig_w, ~lower)], axis=0).reshape(68, C)
    outer = jnp.concatenate([edge(fine_w, lower), edge(dig_w, lower)], axis=0).reshape(68, C)
    inner = side_swap(jnp.concatenate([inner, ctx_w.reshape(160, C)], axis=0))
    outer = outer_swap(outer)
    inner_edge = inner[:68].reshape(2, 34, C)
    outer_edge = outer.reshape(2, 34, C)
    before = jnp.where(lower, inner_edge, outer_edge)
    after = jnp.where(lower, outer_edge, inner_edge)
    fine_pad = jnp.concatenate([before[:1], fine_w, after[:1]], axis=0)
    dig_pad = jnp.concatenate([before[1:], dig_w, after[1:]], axis=0)[:, :, :2]
    ctx_o = inner[68:].reshape(8, 10, HALF)
    ctx_all = jnp.where(
        lower,
        jnp.concatenate([ctx_o, ctx_w], axis=2),
        jnp.concatenate([ctx_w, ctx_o], axis=2),
    )
    north = shift(ctx_all[7:8], GY, 8, 1)
    south = shift(ctx_all[0:1], GY, 8, -1)
    block = jnp.concatenate([north, ctx_all, south], axis=0)

    row_anchor = gy * 32 + half * ROWS
    col_anchor = gx * COLS
    row_mat = lax.dynamic_slice_in_dim(interp_rows, half * ROWS, ROWS + 2, 0)
    field = context_field(block, row_mat, interp_cols, row_anchor, col_anchor)
    pre_one = conv_rows(fine_pad, fine_weight, ROWS, COLS) + conv_rows(field, ctx_weight, ROWS, COLS)
    h_one = jax.nn.silu(pre_one).astype(BF)

    west = shift(h_one[:, COLS - 2 :].reshape(32, C), GX, 8, 1)
    east = shift(h_one[:, :2].reshape(32, C), GX, 8, -1)
    wide = jnp.concatenate([west.reshape(ROWS, 2, C), h_one, east.reshape(ROWS, 2, C)], axis=1)
    two = lambda v, last: lax.dynamic_slice_in_dim(v, jnp.where(last, ROWS - 2, 0), 2, 0)
    inner = side_swap(two(wide, ~lower).reshape(72, C)).reshape(2, 36, C)
    outer = outer_swap(two(wide, lower).reshape(72, C)).reshape(2, 36, C)
    h_pad = jnp.concatenate(
        [jnp.where(lower, inner, outer), wide, jnp.where(lower, outer, inner)], axis=0
    )
    pre_two = conv_rows(h_pad, conv_weight, ROWS + 2, COLS + 2)
    h_two = jax.nn.silu(pre_two).astype(BF)

    own_rows = h_two[1 : 1 + ROWS, 1 : 1 + COLS].reshape(ROWS * COLS, C)[own_idx]

    def ring(v):
        parts = [v[0], v[ROWS + 1], v[1 : 1 + ROWS, 0], v[1 : 1 + ROWS, COLS + 1]]
        return jnp.concatenate(parts, axis=0)

    ring_code = jnp.sum(ring(dig_pad).astype(jnp.int32) * jnp.array([32, 1], jnp.int32), axis=1)
    rows = jnp.concatenate([own_rows, ring(h_two)], axis=0)
    lab = jnp.concatenate([own_lab, ring_code - 1])
    weight = jnp.concatenate([live, ring_code > 0]).astype(F32)
    loss, ghid, gbin, drows = head(rows, lab, weight, hidden_weight, bin_weight)
    inside = (
        jnp.zeros((ROWS * COLS, C), F32).at[own_idx].add(drows[:CAP]).reshape(ROWS, COLS, C)
    )
    round_ = drows[CAP:]
    cells = jnp.concatenate(
        [
            round_[68:84].reshape(ROWS, 1, C),
            inside,
            round_[84:100].reshape(ROWS, 1, C),
        ],
        axis=1,
    )
    dh_two = jnp.concatenate(
        [round_[0:34].reshape(1, 34, C), cells, round_[34:68].reshape(1, 34, C)], axis=0
    )
    g_two = (dh_two * silu_grad(pre_two)).astype(BF)
    gconv = weight_grad(h_pad[1 : 3 + ROWS, 1 : 3 + COLS], g_two[1 : 1 + ROWS, 1 : 1 + COLS], ROWS, COLS)
    g_one = (conv_back(g_two, conv_weight, ROWS, COLS) * silu_grad(pre_one)).astype(BF)
    gfine = weight_grad(fine_pad, g_one, ROWS, COLS)
    gctx = weight_grad(field, g_one, ROWS, COLS)

    stats = jnp.stack([loss, own_num.astype(F32)])
    stat_rows = jnp.stack([jnp.pad(part, (0, C - 2)) for part in split3(stats)])
    rows_all = jnp.concatenate(
        [
            gctx.reshape(9, 2, HALF, C).transpose(1, 0, 2, 3).reshape(-1, C).astype(BF),
            gfine.reshape(-1, C).astype(BF),
            gconv.reshape(-1, C).astype(BF),
            ghid.reshape(C, 8, C).transpose(1, 0, 2).reshape(-1, C).astype(BF),
            gbin.reshape(HID, 4, C).transpose(1, 0, 2).reshape(-1, C).astype(BF),
            stat_rows,
            jnp.zeros((2 * PEERS * SHARD - BODY - 3, C), BF),
        ],
        axis=0,
    ).reshape(2, PEERS * SHARD, C)
    flip = [(0, 1), (1, 0)]
    keep = lax.dynamic_index_in_dim(rows_all, core, 0, False)
    give = lax.dynamic_index_in_dim(rows_all, 1 - core, 0, False)
    got = lax.ppermute(give, "core", flip)
    pair = keep.astype(F32) + got.astype(F32)
    place = BODY - PEERS * SHARD
    stat = split3(pair[place] + pair[place + 1] + pair[place + 2])
    plain = pair.astype(BF)
    fixed = lax.dynamic_update_slice_in_dim(plain, jnp.stack(stat), place, 0)
    pair = jnp.where(core == 1, fixed, plain)
    pieces = lax.all_to_all(pair.reshape(PEERS, SHARD, C), PLANE, 0, 0, tiled=True)
    mine = jnp.sum(pieces.astype(F32), axis=0)
    plain = mine.astype(BF)
    spot = place % SHARD
    stat = split3(mine[spot] + mine[spot + 1] + mine[spot + 2])
    fixed = lax.dynamic_update_slice_in_dim(plain, jnp.stack(stat), spot, 0)
    owner = (core == 1) & (lax.axis_index(PLANE) == place // SHARD)
    mine = jnp.where(owner, fixed, plain)
    half_sum = lax.all_to_all(
        jnp.broadcast_to(mine[None], (PEERS, SHARD, C)), PLANE, 0, 0, tiled=True
    ).reshape(PEERS * SHARD, C)
    other = lax.ppermute(half_sum, "core", flip)
    low = jnp.where(core == 0, half_sum, other)
    high = jnp.where(core == 0, other, half_sum)
    sums = jnp.concatenate([low, high], axis=0)
    stat = jnp.sum(sums[BODY : BODY + 3].astype(F32), axis=0)
    scale = 1.0 / stat[1]
    gctx = lax.dynamic_slice_in_dim(sums, half * 2304, 2304, 0).astype(F32) * scale
    rest = sums[4608:BODY].astype(F32) * scale
    return (
        stat[0] * scale,
        rest[:1152].reshape(3, 3, C, C),
        gctx.reshape(3, 3, HALF, C),
        rest[1152:2304].reshape(3, 3, C, C),
        rest[2304:3328].reshape(8, C, C).transpose(1, 0, 2).reshape(C, HID),
        rest[3328:].reshape(4, HID, C).transpose(1, 0, 2).reshape(HID, BINS),
    )


def solution(mesh):
    devices = np.asarray(mesh.devices).reshape(4, 2, 4, 2, 2)
    split = Mesh(devices, ("x", "core", "z", "yl", "yh"))
    in_specs = (
        P(TALL, GX, None),
        P(GY, GX, "yh"),
        P(),
        P(),
        P(),
        P(),
        P(),
        P(),
        P(),
        P(TALL, GX, None),
        P(TALL, GX),
        P(TALL, GX, None),
    )
    out_specs = (P(), P(), P(None, None, "yh", None), P(), P(), P())
    return jax.shard_map(local, mesh=split, in_specs=in_specs, out_specs=out_specs, check_vma=False)
```

```python
import functools

import jax
import jax.numpy as jnp
import numpy as np
from jax import lax
from jax.experimental import pallas as pl
from jax.experimental.pallas import tpu as pltpu
from jax.sharding import Mesh
from jax.sharding import PartitionSpec as P

HID = 1024
BINS = 512
CAP = 256
ROWS = 16
COLS = 32
C = 128
K = 512
HALF = 256
SHARD = 96
PEERS = 64
BODY = 12032

GY = ("x", "core")
GX = ("z", "yl")
TALL = ("x", "core", "yh")
PLANE = ("x", "z", "yl", "yh")

BF = jnp.bfloat16
F32 = jnp.float32


def shift(x, axis, count, step):
    pairs = [(i, i + step) for i in range(count) if 0 <= i + step < count]
    return lax.ppermute(x, axis, pairs)


def side_swap(x):
    own = [(2 * t + c, 2 * t + 1 - c) for t in range(8) for c in range(2)]
    return lax.ppermute(x, TALL, own)


def outer_swap(x):
    pairs = []
    for t in range(7):
        pairs += [(2 * t + 1, 2 * t + 2), (2 * t + 2, 2 * t + 1)]
    return lax.ppermute(x, TALL, pairs)


WIDE = 48
EXT = 896
SLOTS = 384
KEEP = PEERS * SHARD
STAT = BODY - KEEP
VMEM = pltpu.CompilerParams(vmem_limit_bytes=56 * 1024 * 1024)


def vmem(n):
    return [pl.BlockSpec(memory_space=pltpu.VMEM)] * n


SMEM = pl.BlockSpec(memory_space=pltpu.SMEM)
ANY = pl.BlockSpec(memory_space=pl.ANY)


def dot(a, b):
    return jnp.dot(a, b, preferred_element_type=F32)


def dot_t(a, b):
    return lax.dot_general(a, b, (((1,), (1,)), ((), ())), preferred_element_type=F32)


def t_dot(a, b):
    return lax.dot_general(a, b, (((0,), (0,)), ((), ())), preferred_element_type=F32)


def iota(shape, dim):
    return lax.broadcasted_iota(jnp.int32, shape, dim)


def split3(v):
    hi = v.astype(BF)
    rest = v - hi.astype(F32)
    mid = rest.astype(BF)
    low = (rest - mid.astype(F32)).astype(BF)
    return [hi.astype(F32), mid.astype(F32), low.astype(F32)]


def stat_rows(v, like):
    hi, mid, low = split3(v)
    row = iota(like, 0)
    out = jnp.where(row == 0, hi, jnp.where(row == 1, mid, jnp.where(row == 2, low, 0.0)))
    return out


def first_conv_kernel(sc, rmat, cmat, block, finep, w_fine, w_ctx, xc, h1, sg, fscr, mid):
    half, row0, col0 = sc[1], sc[2], sc[3]
    r = rmat[pl.ds(pl.multiple_of(half * ROWS, ROWS), 32), :]
    fi = iota((288, 32), 0) // 16
    grow = row0 + fi - 1
    pick = (fi == iota((288, 32), 1)) & (grow >= 0) & (grow < 256)
    left = dot(pick.astype(F32).astype(BF), r).astype(BF)
    spread = (iota((16, 160), 0) == iota((16, 160), 1) // 16).astype(F32).astype(BF)
    full = dot(left, spread)
    same = (iota((288, 160), 0) % 16) == (iota((288, 160), 1) % 16)
    kron = jnp.where(same, full, 0.0).astype(BF)
    mid[...] = dot(kron, block[...]).astype(BF)
    cols = []
    for dx in range(3):
        gcol = col0 + iota((32, 16), 0) + dx - 1
        ok = (gcol >= 0) & (gcol < 256)
        cols.append(jnp.where(ok, cmat[dx : dx + 32, :], 0.0))
    cols = jnp.concatenate(cols, axis=0).astype(BF)
    for i in range(ROWS + 2):
        wide = dot(cols, mid[16 * i : 16 * i + 16, :]).astype(BF)
        for dx in range(3):
            xc[32 * i : 32 * i + 32, 384 + 512 * dx : 896 + 512 * dx] = wide[32 * dx : 32 * dx + 32]
    fscr[...] = finep[...].astype(F32)
    for i in range(ROWS + 2):
        for dx in range(3):
            at = WIDE * i + dx
            xc[32 * i : 32 * i + 32, 128 * dx : 128 * dx + 128] = fscr[at : at + 32, :].astype(BF)
    for part in range(2):
        base = 256 * part
        acc = None
        for dy in range(3):
            rows = slice(base + 32 * dy, base + 32 * dy + 256)
            term = dot(xc[rows, :384], w_fine[384 * dy : 384 * dy + 384, :])
            term += dot(xc[rows, 384:], w_ctx[1536 * dy : 1536 * dy + 1536, :])
            acc = term if acc is None else acc + term
        s = jax.nn.sigmoid(acc)
        h1[base : base + 256, :] = (acc * s).astype(BF)
        sg[base : base + 256, :] = s * (1.0 + acc * (1.0 - s))


def rest_kernel(
    sc, hb, hw, ha, xc, sg1, idx_s, idx_l, lab, cw, hid, binw, keep, give,
    hp, hx, sg2, h2, rows_s, act, sgz, dl, dz, gscr, gx, g2w, g1w, buf, sem,
):
    core = sc[0]
    hp[0:96, :] = hb[...].astype(F32)
    hp[96:864, :] = hw[...].astype(F32)
    hp[864:960, :] = ha[...].astype(F32)
    hp[960:1000, :] = jnp.zeros((40, C), F32)
    for dx in range(3):
        hx[:, 128 * dx : 128 * dx + 128] = hp[dx : dx + 992, :].astype(BF)
    for part in range(7):
        at = 128 * part
        acc = None
        for dy in range(3):
            term = dot(hx[at + WIDE * dy : at + WIDE * dy + 128, :], cw[384 * dy : 384 * dy + 384, :])
            acc = term if acc is None else acc + term
        s = jax.nn.sigmoid(acc)
        h2[at : at + 128, :] = (acc * s).astype(BF)
        sg2[at : at + 128, :] = s * (1.0 + acc * (1.0 - s))
    loss = jnp.zeros((), F32)
    for part in range(3):
        sl = slice(128 * part, 128 * part + 128)
        pick = (idx_s[sl, :] == iota((128, EXT), 1)).astype(F32).astype(BF)
        rows = dot(pick, h2[...]).astype(BF)
        rows_s[sl, :] = rows
        z = dot(rows, hid[...])
        s = jax.nn.sigmoid(z)
        act[sl, :] = (z * s).astype(BF)
        sgz[sl, :] = s * (1.0 + z * (1.0 - s))
        logits = dot(act[sl, :], binw[...])
        peak = jnp.max(logits, axis=1, keepdims=True)
        top = peak + jnp.log(jnp.sum(jnp.exp(logits - peak), axis=1, keepdims=True))
        lb = lab[sl, :]
        onehot = (lb == iota((128, BINS), 1)).astype(F32)
        live = (lb >= 0).astype(F32)
        if part < 2:
            picked = jnp.sum(logits * onehot, axis=1, keepdims=True)
            loss += jnp.sum(live * (top - picked))
        dl[sl, :] = ((jnp.exp(logits - top) - onehot) * live).astype(BF)
        dact = dot_t(dl[sl, :], binw[...])
        dz[sl, :] = (dact * sgz[sl, :]).astype(BF)
        drows = dot_t(dz[sl, :], hid[...])
        hi = drows.astype(BF)
        gscr[sl, 0:128] = hi
        gscr[sl, 128:256] = (drows - hi.astype(F32)).astype(BF)

    def put(row, value):
        buf[(row // KEEP) ^ core, pl.ds(row % KEEP, value.shape[0]), :] = value.astype(BF)

    for n in range(4):
        put(7936 + 1024 * n, t_dot(act[0:CAP, :], dl[0:CAP, 128 * n : 128 * n + 128]))
    ghid = t_dot(rows_s[0:CAP, :], dz[0:CAP, :])
    for n in range(8):
        put(6912 + 128 * n, ghid[:, 128 * n : 128 * n + 128])
    for part in range(7):
        at = 128 * part
        spread = (idx_l[...] == iota((128, SLOTS), 0) + at).astype(F32).astype(BF)
        both = dot(spread, gscr[...])
        gx[at : at + 128, :] = (both[:, :128] + both[:, 128:]) * sg2[at : at + 128, :]
    gx[EXT : EXT + 8, :] = jnp.zeros((8, C), F32)

    g2w[...] = jnp.zeros_like(g2w)
    col = iota((768, C), 0) % WIDE
    own = jnp.where((col >= 1) & (col <= COLS), gx[WIDE : WIDE + 768, :], 0.0).astype(BF)
    for dy in range(3):
        g2w[WIDE * (1 + dy) : WIDE * (1 + dy) + 768, 128 * dy : 128 * dy + 128] = own
    for dx in range(3):
        part = t_dot(hx[0:960, 128 * dx : 128 * dx + 128], g2w[...])
        for dy in range(3):
            put(5760 + 128 * (3 * dy + dx), part[:, 128 * dy : 128 * dy + 128])

    for i in range(ROWS + 2):
        for dx in range(3):
            at = WIDE * i + 2 - dx
            hx[32 * i : 32 * i + 32, 128 * dx : 128 * dx + 128] = gx[at : at + 32, :].astype(BF)
    g1w[...] = jnp.zeros_like(g1w)
    for part in range(2):
        base = 256 * part
        acc = None
        for dy in range(3):
            at = base + 32 * (2 - dy)
            back = jnp.concatenate(
                [cw[384 * dy + 128 * dx : 384 * dy + 128 * dx + 128, :] for dx in range(3)], axis=1
            )
            term = dot_t(hx[at : at + 256, :], back)
            acc = term if acc is None else acc + term
        g1 = (acc * sg1[base : base + 256, :]).astype(BF)
        for dy in range(3):
            at = base + 32 * dy
            g1w[at : at + 256, 128 * dy : 128 * dy + 128] = g1
    for dx in range(3):
        part = t_dot(xc[:, 128 * dx : 128 * dx + 128], g1w[...])
        for dy in range(3):
            put(4608 + 128 * (3 * dy + dx), part[:, 128 * dy : 128 * dy + 128])
        for side in range(2):
            at = 384 + 512 * dx + 256 * side
            part = t_dot(xc[:, at : at + 256], g1w[...])
            for dy in range(3):
                put(2304 * side + 256 * (3 * dy + dx), part[:, 128 * dy : 128 * dy + 128])
    lane = iota((1, C), 1)
    stats = jnp.where(lane == 0, loss, jnp.where(lane == 1, sc[4].astype(F32), 0.0))
    put(BODY, stat_rows(stats, (16, C)))
    put(BODY + 16, jnp.zeros((2 * KEEP - BODY - 16, C), F32))
    one = pltpu.make_async_copy(buf.at[0], keep, sem.at[0])
    two = pltpu.make_async_copy(buf.at[1], give, sem.at[1])
    one.start()
    two.start()
    one.wait()
    two.wait()


def pair_kernel(sc, keep, got, out):
    out[...] = (keep[...].astype(F32) + got[...].astype(F32)).astype(BF)

    @pl.when((pl.program_id(0) == 3) & (sc[0] == 1))
    def _():
        at = STAT - 4608
        rows = keep[at : at + 16, :].astype(F32) + got[at : at + 16, :].astype(F32)
        out[at : at + 16, :] = stat_rows(jnp.sum(rows, axis=0, keepdims=True), (16, C)).astype(BF)


def spread_kernel(sc, pieces, out, mine):
    acc = pieces[0].astype(F32)
    for i in range(1, PEERS):
        acc += pieces[i].astype(F32)
    mine[...] = acc.astype(BF)
    at = STAT % SHARD

    @pl.when(sc[5] == 1)
    def _():
        rows = acc[at : at + 16]
        mine[at : at + 16, :] = stat_rows(jnp.sum(rows, axis=0, keepdims=True), (16, C)).astype(BF)

    for i in range(PEERS):
        out[i] = mine[...]


def finish_kernel(sc, own, other, loss, gfine, gctx, gconv, ghid, gbin, src, vf, vx, vc, vh, vb, sin, sout):
    core, half = sc[0], sc[1]
    a = pltpu.make_async_copy(own, src.at[core], sin.at[0])
    b = pltpu.make_async_copy(other, src.at[1 - core], sin.at[1])
    a.start()
    b.start()
    a.wait()
    b.wait()
    stats = jnp.sum(src[1, STAT : STAT + 16, :].astype(F32), axis=0, keepdims=True)
    lane = iota((1, C), 1)
    total = jnp.sum(jnp.where(lane == 1, stats, 0.0))
    scale = 1.0 / total
    loss[0, 0] = jnp.sum(jnp.where(lane == 0, stats, 0.0)) * scale

    def get(row, n):
        return src[row // KEEP, row % KEEP : row % KEEP + n, :].astype(F32) * scale

    outs = []

    def send(view, dst, n):
        c = pltpu.make_async_copy(view, dst, sout.at[n])
        c.start()
        outs.append(c)

    for n in range(4):
        vb[:, 128 * n : 128 * n + 128] = get(7936 + 1024 * n, 1024)
    send(vb, gbin, 0)
    at = pl.multiple_of(half * 2304, 128)
    for n in range(9):
        part = src[0, pl.ds(at + 256 * n, 256), :].astype(F32) * scale
        vx[256 * n : 256 * n + 256, :] = part
    send(vx, gctx, 1)
    vf[...] = get(4608, 1152)
    send(vf, gfine, 2)
    for n in range(9):
        vc[128 * n : 128 * n + 128, :] = get(5760 + 128 * n, 128)
    send(vc, gconv, 3)
    for n in range(8):
        vh[:, 128 * n : 128 * n + 128] = get(6912 + 128 * n, 128)
    send(vh, ghid, 4)
    for c in outs:
        c.wait()


def sds(shape, dtype):
    return jax.ShapeDtypeStruct(shape, dtype)


def first_conv(sc, rmat, cmat, block, finep, w_fine, w_ctx):
    return pl.pallas_call(
        first_conv_kernel,
        out_shape=(sds((576, 1920), BF), sds((512, C), BF), sds((512, C), F32)),
        in_specs=[SMEM] + vmem(6),
        out_specs=tuple(vmem(3)),
        scratch_shapes=[pltpu.VMEM((18 * WIDE, C), F32), pltpu.VMEM((288, K), BF)],
        compiler_params=VMEM,
        name="first_conv",
    )(sc, rmat, cmat, block, finep, w_fine, w_ctx)


def rest(*args):
    v = pltpu.VMEM
    return pl.pallas_call(
        rest_kernel,
        out_shape=(sds((KEEP, C), BF), sds((KEEP, C), BF)),
        in_specs=[SMEM] + vmem(len(args) - 1),
        out_specs=(ANY, ANY),
        scratch_shapes=[
            v((1000, C), F32),
            v((992, 384), BF),
            v((EXT, C), F32),
            v((EXT, C), BF),
            v((SLOTS, C), BF),
            v((SLOTS, HID), BF),
            v((SLOTS, HID), F32),
            v((SLOTS, BINS), BF),
            v((SLOTS, HID), BF),
            v((SLOTS, 256), BF),
            v((EXT + 8, C), F32),
            v((960, 384), BF),
            v((576, 384), BF),
            v((2, KEEP, C), BF),
            pltpu.SemaphoreType.DMA((2,)),
        ],
        compiler_params=VMEM,
        name="rest",
    )(*args)


def pair_sum(sc, keep, got):
    spec = pl.BlockSpec((KEEP // 4, C), lambda i: (i, 0))
    return pl.pallas_call(
        pair_kernel,
        grid=(4,),
        out_shape=sds((KEEP, C), BF),
        in_specs=[SMEM, spec, spec],
        out_specs=spec,
        name="pair_sum",
    )(sc, keep, got)


def spread(sc, pieces):
    return pl.pallas_call(
        spread_kernel,
        out_shape=sds((PEERS, SHARD, C), BF),
        in_specs=[SMEM] + vmem(1),
        out_specs=vmem(1)[0],
        scratch_shapes=[pltpu.VMEM((SHARD, C), BF)],
        compiler_params=VMEM,
        name="spread",
    )(sc, pieces)


def finish(sc, own, other):
    v = pltpu.VMEM
    shapes = [(1152, C), (2304, C), (1152, C), (C, HID), (HID, BINS)]
    return pl.pallas_call(
        finish_kernel,
        out_shape=(sds((1, 1), F32),) + tuple(sds(s, F32) for s in shapes),
        in_specs=[SMEM, ANY, ANY],
        out_specs=(SMEM,) + (ANY,) * 5,
        scratch_shapes=[v((2, KEEP, C), BF)]
        + [v(s, F32) for s in shapes]
        + [pltpu.SemaphoreType.DMA((2,)), pltpu.SemaphoreType.DMA((5,))],
        compiler_params=VMEM,
        name="finish",
    )(sc, own, other)


def ring_cells():
    cells = [(0, c) for c in range(34)] + [(17, c) for c in range(34)]
    cells += [(r, 0) for r in range(1, 17)] + [(r, 33) for r in range(1, 17)]
    return np.array([WIDE * r + c for r, c in cells] + [-1] * 28, np.int32)


def local(
    fine,
    context,
    interp_rows,
    interp_cols,
    fine_weight,
    ctx_weight,
    conv_weight,
    hidden_weight,
    bin_weight,
    cell_index,
    counts,
    labels,
):
    core = lax.axis_index("core")
    half = lax.axis_index("yh")
    gy = lax.axis_index(GY)
    gx = lax.axis_index(GX)
    lower = half == 1

    own_idx = cell_index[0, 0]
    own_lab = labels[0, 0]
    own_num = counts[0, 0]
    live = jnp.arange(CAP, dtype=jnp.int32) < own_num

    spot = own_idx[:, None] == jnp.arange(ROWS * COLS, dtype=jnp.int32)[None, :]
    code = jnp.sum(
        jnp.where(spot & live[:, None], own_lab[:, None] + 1, 0), axis=0, dtype=jnp.int32
    )
    digits = jnp.stack([code // 32, code % 32], axis=1).astype(BF).reshape(ROWS, COLS, 2)

    fine_dig = jnp.concatenate([fine, jnp.pad(digits, ((0, 0), (0, 0), (0, 126)))], axis=0)

    def pack_cols(col):
        return jnp.concatenate([fine_dig[:, col], context[:, min(col, 7)].reshape(16, C)], axis=0)

    west = shift(pack_cols(COLS - 1), GX, 8, 1)
    east = shift(pack_cols(0), GX, 8, -1)
    wide = jnp.concatenate([west[:32, None], fine_dig, east[:32, None]], axis=1)
    fine_w, dig_w = wide[:ROWS], wide[ROWS:]
    ctx_w = jnp.concatenate(
        [west[32:].reshape(8, 1, HALF), context, east[32:].reshape(8, 1, HALF)], axis=1
    )
    edge = lambda v, last: lax.dynamic_slice_in_dim(v, jnp.where(last, v.shape[0] - 1, 0), 1, 0)
    inner = jnp.concatenate([edge(fine_w, ~lower), edge(dig_w, ~lower)], axis=0).reshape(68, C)
    outer = jnp.concatenate([edge(fine_w, lower), edge(dig_w, lower)], axis=0).reshape(68, C)
    inner = side_swap(jnp.concatenate([inner, ctx_w.reshape(160, C)], axis=0))
    outer = outer_swap(outer)
    inner_edge = inner[:68].reshape(2, 34, C)
    outer_edge = outer.reshape(2, 34, C)
    before = jnp.where(lower, inner_edge, outer_edge)
    after = jnp.where(lower, outer_edge, inner_edge)
    fine_pad = jnp.concatenate([before[:1], fine_w, after[:1]], axis=0)
    dig_pad = jnp.concatenate([before[1:], dig_w, after[1:]], axis=0)[:, :, :2]
    ctx_o = inner[68:].reshape(8, 10, HALF)
    ctx_all = jnp.where(
        lower,
        jnp.concatenate([ctx_o, ctx_w], axis=2),
        jnp.concatenate([ctx_w, ctx_o], axis=2),
    )
    north = shift(ctx_all[7:8], GY, 8, 1)
    south = shift(ctx_all[0:1], GY, 8, -1)
    block = jnp.concatenate([north, ctx_all, south], axis=0)

    row_anchor = gy * 32 + half * ROWS
    col_anchor = gx * COLS
    owner = (core == 1) & (lax.axis_index(PLANE) == STAT // SHARD)
    sc = jnp.stack([core, half, row_anchor, col_anchor, own_num, owner.astype(jnp.int32)])
    sc = jnp.concatenate([sc, jnp.zeros((2,), jnp.int32)])
    rmat = jnp.pad(interp_rows, ((0, 14), (0, 6)))
    cmat = jnp.pad(interp_cols.astype(F32), ((0, 14), (0, 6)))
    block16 = jnp.pad(block, ((0, 0), (0, 6), (0, 0))).reshape(160, K)
    finep = jnp.pad(fine_pad, ((0, 0), (0, WIDE - 34), (0, 0))).reshape(18 * WIDE, C)
    xc, h_flat, sg1 = first_conv(
        sc, rmat, cmat, block16, finep, fine_weight.reshape(1152, C), ctx_weight.reshape(4608, C)
    )
    h_one = h_flat.reshape(ROWS, COLS, C)

    west = shift(h_one[:, COLS - 2 :].reshape(32, C), GX, 8, 1)
    east = shift(h_one[:, :2].reshape(32, C), GX, 8, -1)
    wide = jnp.concatenate(
        [west.reshape(ROWS, 2, C), h_one, east.reshape(ROWS, 2, C), jnp.zeros((ROWS, 12, C), BF)],
        axis=1,
    )
    two = lambda v, last: lax.dynamic_slice_in_dim(v, jnp.where(last, ROWS - 2, 0), 2, 0)
    inner = side_swap(two(wide, ~lower).reshape(96, C))
    outer = outer_swap(two(wide, lower).reshape(96, C))
    hb = jnp.where(lower, inner, outer)
    ha = jnp.where(lower, outer, inner)

    def ring(v):
        parts = [v[0], v[ROWS + 1], v[1 : 1 + ROWS, 0], v[1 : 1 + ROWS, COLS + 1]]
        return jnp.concatenate(parts, axis=0)

    ring_code = jnp.sum(ring(dig_pad).astype(jnp.int32) * jnp.array([32, 1], jnp.int32), axis=1)
    lab = jnp.concatenate(
        [jnp.where(live, own_lab, -1), ring_code - 1, jnp.full((28,), -1, jnp.int32)]
    )
    spots = jnp.concatenate(
        [(own_idx // COLS + 1) * WIDE + own_idx % COLS + 1, jnp.asarray(ring_cells())]
    )
    keep, give = rest(
        sc, hb, wide.reshape(ROWS * WIDE, C), ha, xc, sg1, spots[:, None], spots[None, :],
        lab[:, None], conv_weight.reshape(1152, C), hidden_weight, bin_weight,
    )
    flip = [(0, 1), (1, 0)]
    pair = pair_sum(sc, keep, lax.ppermute(give, "core", flip))
    pieces = lax.all_to_all(pair.reshape(PEERS, SHARD, C), PLANE, 0, 0, tiled=True)
    mine = spread(sc, pieces)
    half_sum = lax.all_to_all(mine, PLANE, 0, 0, tiled=True).reshape(KEEP, C)
    other = lax.ppermute(half_sum, "core", flip)
    loss, gfine, gctx, gconv, ghid, gbin = finish(sc, half_sum, other)
    return (
        loss.reshape(()),
        gfine.reshape(3, 3, C, C),
        gctx.reshape(3, 3, HALF, C),
        gconv.reshape(3, 3, C, C),
        ghid,
        gbin,
    )


def solution(mesh):
    devices = np.asarray(mesh.devices).reshape(4, 2, 4, 2, 2)
    split = Mesh(devices, ("x", "core", "z", "yl", "yh"))
    in_specs = (
        P(TALL, GX, None),
        P(GY, GX, "yh"),
        P(),
        P(),
        P(),
        P(),
        P(),
        P(),
        P(),
        P(TALL, GX, None),
        P(TALL, GX),
        P(TALL, GX, None),
    )
    out_specs = (P(), P(), P(None, None, "yh", None), P(), P(), P())
    return jax.shard_map(local, mesh=split, in_specs=in_specs, out_specs=out_specs, check_vma=False)
```

```python
import functools

import jax
import jax.numpy as jnp
import numpy as np
from jax import lax
from jax.experimental import pallas as pl
from jax.experimental.pallas import tpu as pltpu
from jax.sharding import Mesh
from jax.sharding import PartitionSpec as P

HID = 1024
BINS = 512
CAP = 256
ROWS = 16
COLS = 32
C = 128
K = 512
HALF = 256
SHARD = 96
PEERS = 64
BODY = 12032

GY = ("x", "core")
GX = ("z", "yl")
TALL = ("x", "core", "yh")
PLANE = ("x", "z", "yl", "yh")

BF = jnp.bfloat16
F32 = jnp.float32


def shift(x, axis, count, step):
    pairs = [(i, i + step) for i in range(count) if 0 <= i + step < count]
    return lax.ppermute(x, axis, pairs)


def side_swap(x):
    own = [(2 * t + c, 2 * t + 1 - c) for t in range(8) for c in range(2)]
    return lax.ppermute(x, TALL, own)


def outer_swap(x):
    pairs = []
    for t in range(7):
        pairs += [(2 * t + 1, 2 * t + 2), (2 * t + 2, 2 * t + 1)]
    return lax.ppermute(x, TALL, pairs)


WIDE = 48
EXT = 896
SLOTS = 384
KEEP = PEERS * SHARD
STAT = BODY // 2
MIB = 1024 * 1024
BUSY = pl.CostEstimate(flops=5_000_000_000, bytes_accessed=1_000_000, transcendentals=0)


def limit(mib):
    return pltpu.CompilerParams(vmem_limit_bytes=mib * MIB)


def vmem(n):
    return [pl.BlockSpec(memory_space=pltpu.VMEM)] * n


SMEM = pl.BlockSpec(memory_space=pltpu.SMEM)
ANY = pl.BlockSpec(memory_space=pl.ANY)
HBM = pl.BlockSpec(memory_space=pltpu.HBM)


def dot(a, b):
    return jnp.dot(a, b, preferred_element_type=F32)


def dot_t(a, b):
    return lax.dot_general(a, b, (((1,), (1,)), ((), ())), preferred_element_type=F32)


def t_dot(a, b):
    return lax.dot_general(a, b, (((0,), (0,)), ((), ())), preferred_element_type=F32)


def iota(shape, dim):
    return lax.broadcasted_iota(jnp.int32, shape, dim)


def split3(v):
    hi = v.astype(BF)
    rest = v - hi.astype(F32)
    mid = rest.astype(BF)
    low = (rest - mid.astype(F32)).astype(BF)
    return [hi.astype(F32), mid.astype(F32), low.astype(F32)]


def stat_rows(v, like):
    hi, mid, low = split3(v)
    row = iota(like, 0)
    out = jnp.where(row == 0, hi, jnp.where(row == 1, mid, jnp.where(row == 2, low, 0.0)))
    return out


def fetch(pairs, sem):
    copies = [pltpu.make_async_copy(src, dst, sem.at[n]) for n, (src, dst) in enumerate(pairs)]
    for c in copies:
        c.start()
    return copies


def edge_cols_kernel(fine_in, ctx_in, last, first, fine, ctx, fs, xs):
    fine[...] = fine_in[...]
    ctx[...] = ctx_in[...]
    fs[...] = fine[...].astype(F32)
    for side in range(2):
        xs[side] = ctx[:, 128 * side : 128 * side + 128].astype(F32)
    for out, fc, xc in ((last, COLS - 1, 7), (first, 0, 0)):
        out[0:16, :] = fs[pl.ds(fc, 16, stride=COLS), :].astype(BF)
        sides = [xs.at[side][pl.ds(xc, 8, stride=8), :] for side in range(2)]
        out[16:32, :] = jnp.concatenate(sides, axis=0).astype(BF)


def edge_rows_kernel(sc, fine, ctx, west, east, inner, outer, rows, xs):
    lower = sc[1] == 1
    rows[...] = jnp.zeros_like(rows)
    w, e = west[...].astype(F32), east[...].astype(F32)
    for n, r in ((0, 0), (1, ROWS - 1)):
        at = WIDE * n
        rows[at + 1 : at + 33, :] = fine[COLS * r : COLS * r + COLS, :].astype(F32)
        rows[at : at + 1, :] = w[r : r + 1, :]
        rows[at + 33 : at + 34, :] = e[r : r + 1, :]
    top, bottom = rows[0:WIDE, :].astype(BF), rows[WIDE : 2 * WIDE, :].astype(BF)
    inner[0:WIDE, :] = jnp.where(lower, top, bottom)
    outer[...] = jnp.where(lower, bottom, top)
    xs[...] = jnp.zeros_like(xs)
    for side in range(2):
        base = 128 * side
        for a in range(8):
            at = base + 16 * a
            xs[at + 1 : at + 9, :] = ctx[8 * a : 8 * a + 8, base : base + 128].astype(F32)
        xs[pl.ds(base, 8, stride=16), :] = w[16 + 8 * side : 24 + 8 * side, :]
        xs[pl.ds(base + 9, 8, stride=16), :] = e[16 + 8 * side : 24 + 8 * side, :]
    inner[WIDE:, :] = xs[...].astype(BF)


def column(row):
    n = row.shape[1]
    eye = iota((n, n), 0) == iota((n, n), 1)
    return jnp.sum(jnp.where(eye, row.astype(F32), 0.0), axis=1, keepdims=True)


def first_conv_kernel(
    sc, rows_in, cols_in, fine, west, east, mine, inner, outer, north, south, w_fine, w_ctx, idx_l, lab_l,
    xc_out, h1, sg, last, first, digs,
    fscr, mid, block, hscr, dscr, rmat, cmat, xc, xsem,
):
    half, row0, col0 = sc[1], sc[2], sc[3]
    lower = half == 1
    rmat[...] = jnp.zeros_like(rmat)
    cmat[...] = jnp.zeros_like(cmat)
    rmat[0:10, 0:34] = rows_in[...].astype(F32)
    cmat[0:10, 0:34] = cols_in[...].astype(F32)
    for part, got in ((half, mine), (1 - half, inner)):
        for side in range(2):
            lanes = pl.ds(pl.multiple_of(256 * part + 128 * side, 128), 128)
            block[16:144, lanes] = got[WIDE + 128 * side : WIDE + 128 * side + 128, :]
            which = 0 if got is mine else 32
            block[0:16, lanes] = north[which + 16 * side : which + 16 * side + 16, :]
            block[144:160, lanes] = south[which + 16 * side : which + 16 * side + 16, :]
    fi = iota((288, C), 0) // 16
    grow = row0 + fi - 1
    pick = (fi + 16 * half == iota((288, C), 1)) & (grow >= 0) & (grow < 256)
    left = dot_t(pick.astype(F32).astype(BF), rmat[...].astype(BF)).astype(BF)
    spread = (iota((16, 160), 0) == iota((16, 160), 1) // 16).astype(F32).astype(BF)
    full = dot(left, spread)
    same = (iota((288, 160), 0) % 16) == (iota((288, 160), 1) % 16)
    kron = jnp.where(same, full, 0.0).astype(BF)
    mid[...] = dot(kron, block[...]).astype(BF)
    cell = iota((96, C), 0)
    gcol = col0 + cell % 32 + cell // 32 - 1
    pick = (cell % 32 + cell // 32 == iota((96, C), 1)) & (gcol >= 0) & (gcol < 256)
    cols = dot_t(pick.astype(F32).astype(BF), cmat[...].astype(BF)).astype(BF)
    for i in range(ROWS + 2):
        wide = dot(cols, mid[16 * i : 16 * i + 16, :]).astype(BF)
        for dx in range(3):
            xc[32 * i : 32 * i + 32, 384 + 512 * dx : 896 + 512 * dx] = wide[32 * dx : 32 * dx + 32]
    for i in range(ROWS):
        at = WIDE * (i + 1) + 1
        fscr[at : at + 32, :] = fine[32 * i : 32 * i + 32, :].astype(F32)
    fscr[pl.ds(WIDE, 16, stride=WIDE), :] = west[0:16, :].astype(F32)
    fscr[pl.ds(WIDE + 33, 16, stride=WIDE), :] = east[0:16, :].astype(F32)
    a, b = inner[0:WIDE, :].astype(F32), outer[...].astype(F32)
    fscr[0:WIDE, :] = jnp.where(lower, a, b)
    fscr[17 * WIDE : 18 * WIDE, :] = jnp.where(lower, b, a)
    for i in range(ROWS + 2):
        for dx in range(3):
            at = WIDE * i + dx
            xc[32 * i : 32 * i + 32, 128 * dx : 128 * dx + 128] = fscr[at : at + 32, :].astype(BF)
    save = pltpu.make_async_copy(xc, xc_out, xsem)
    save.start()
    for part in range(2):
        base = 256 * part
        acc = None
        for dy in range(3):
            rows = slice(base + 32 * dy, base + 32 * dy + 256)
            term = dot(xc[rows, :384], w_fine[384 * dy : 384 * dy + 384, :])
            term += dot(xc[rows, 384:], w_ctx[1536 * dy : 1536 * dy + 1536, :])
            acc = term if acc is None else acc + term
        s = jax.nn.sigmoid(acc)
        h = (acc * s).astype(BF)
        h1[base : base + 256, :] = h
        hscr[base : base + 256, :] = h.astype(F32)
        sg[base : base + 256, :] = s * (1.0 + acc * (1.0 - s))
    code = jnp.where(iota((1, CAP), 1) < sc[4], lab_l[...] + 1, 0)
    kind = iota((C, CAP), 0)
    digit = jnp.where(kind == 0, code // 32, jnp.where(kind == 1, code % 32, 0))
    digit = digit.astype(F32).astype(BF)
    for part in range(4):
        at = 128 * part
        named = (idx_l[...] == iota((128, CAP), 0) + at).astype(F32).astype(BF)
        dscr[at : at + 128, :] = dot_t(named, digit)
    digs[0:32, :] = dscr[0:32, :].astype(BF)
    digs[32:64, :] = dscr[480:512, :].astype(BF)
    for out, c0, c1, cd in ((last, COLS - 2, COLS - 1, COLS - 1), (first, 0, 1, 0)):
        out[0:16, :] = hscr[pl.ds(c0, 16, stride=COLS), :].astype(BF)
        out[16:32, :] = hscr[pl.ds(c1, 16, stride=COLS), :].astype(BF)
        out[32:48, :] = dscr[pl.ds(cd, 16, stride=COLS), :].astype(BF)
    save.wait()


def h_rows_kernel(sc, h1, digs, west, east, wide, inner, outer, ws, ds):
    lower = sc[1] == 1
    w, e = west[...].astype(F32), east[...].astype(F32)
    ws[...] = jnp.zeros_like(ws)
    ds[...] = jnp.zeros_like(ds)
    for i in range(ROWS):
        ws[WIDE * i + 2 : WIDE * i + 34, :] = h1[32 * i : 32 * i + 32, :].astype(F32)
    for col, value in ((0, w[0:16]), (1, w[16:32]), (34, e[0:16]), (35, e[16:32])):
        ws[pl.ds(col, 16, stride=WIDE), :] = value
    for n, r in ((0, 0), (1, ROWS - 1)):
        at = WIDE * n
        ds[at + 1 : at + 33, :] = digs[32 * n : 32 * n + 32, :].astype(F32)
        ds[at : at + 1, :] = w[32 + r : 33 + r, :]
        ds[at + 33 : at + 34, :] = e[32 + r : 33 + r, :]
    wide[...] = ws[...].astype(BF)
    top, bottom = ws[0:96, :].astype(BF), ws[14 * WIDE : 16 * WIDE, :].astype(BF)
    inner[0:96, :] = jnp.where(lower, top, bottom)
    outer[0:96, :] = jnp.where(lower, bottom, top)
    top, bottom = ds[0:WIDE, :].astype(BF), ds[WIDE : 2 * WIDE, :].astype(BF)
    inner[96:144, :] = jnp.where(lower, top, bottom)
    outer[96:144, :] = jnp.where(lower, bottom, top)


def rest_kernel(
    sc, hw, inner, outer, west, east, xc_in, sg1, idx_l, ring_l, lab_l, cw, hid, binw,
    keep, give,
    hp, hx, sg2, h2, rows_s, act, sgz, dl, dz, gscr, gx, g2w, g1w, buf, xc, sem,
):
    (load,) = fetch([(xc_in, xc)], sem)
    core, lower = sc[0], sc[1] == 1
    a, b = inner[...].astype(F32), outer[...].astype(F32)
    before, after = jnp.where(lower, a, b), jnp.where(lower, b, a)
    hp[0:96, :] = before[0:96]
    hp[96:864, :] = hw[...].astype(F32)
    hp[864:960, :] = after[0:96]
    hp[960:1000, :] = jnp.zeros((40, C), F32)
    gx[...] = jnp.zeros_like(gx)
    gx[0:WIDE, :] = before[96:144]
    gx[17 * WIDE : 18 * WIDE, :] = after[96:144]
    gx[pl.ds(WIDE, 16, stride=WIDE), :] = west[32:48, :].astype(F32)
    gx[pl.ds(WIDE + 33, 16, stride=WIDE), :] = east[32:48, :].astype(F32)
    slot_l = idx_l[...] + 16 * (idx_l[...] // 32) + WIDE + 1
    slot_s = column(slot_l).astype(jnp.int32)
    ring_s = column(ring_l[...]).astype(jnp.int32)
    ring_pick = (ring_s == iota((128, EXT), 1)).astype(F32).astype(BF)
    code = dot(ring_pick, gx[0:EXT, :].astype(BF))
    lane = iota((128, C), 1)
    code = jnp.sum(jnp.where(lane == 0, 32.0 * code, jnp.where(lane == 1, code, 0.0)), axis=1, keepdims=True)
    own_lab = column(jnp.where(iota((1, CAP), 1) < sc[4], lab_l[...], -1)).astype(jnp.int32)
    for dx in range(3):
        hx[:, 128 * dx : 128 * dx + 128] = hp[dx : dx + 992, :].astype(BF)
    for part in range(7):
        at = 128 * part
        acc = None
        for dy in range(3):
            term = dot(hx[at + WIDE * dy : at + WIDE * dy + 128, :], cw[384 * dy : 384 * dy + 384, :])
            acc = term if acc is None else acc + term
        s = jax.nn.sigmoid(acc)
        h2[at : at + 128, :] = (acc * s).astype(BF)
        sg2[at : at + 128, :] = s * (1.0 + acc * (1.0 - s))
    loss = jnp.zeros((), F32)
    for part in range(3):
        sl = slice(128 * part, 128 * part + 128)
        pick = ring_pick
        if part < 2:
            pick = (slot_s[sl] == iota((128, EXT), 1)).astype(F32).astype(BF)
        rows = dot(pick, h2[...]).astype(BF)
        rows_s[sl, :] = rows
        z = dot(rows, hid[...])
        s = jax.nn.sigmoid(z)
        act[sl, :] = (z * s).astype(BF)
        sgz[sl, :] = s * (1.0 + z * (1.0 - s))
        logits = dot(act[sl, :], binw[...])
        peak = jnp.max(logits, axis=1, keepdims=True)
        top = peak + jnp.log(jnp.sum(jnp.exp(logits - peak), axis=1, keepdims=True))
        lb = own_lab[sl] if part < 2 else code.astype(jnp.int32) - 1
        onehot = (lb == iota((128, BINS), 1)).astype(F32)
        live = (lb >= 0).astype(F32)
        if part < 2:
            picked = jnp.sum(logits * onehot, axis=1, keepdims=True)
            loss += jnp.sum(live * (top - picked))
        dl[sl, :] = ((jnp.exp(logits - top) - onehot) * live).astype(BF)
        dact = dot_t(dl[sl, :], binw[...])
        dz[sl, :] = (dact * sgz[sl, :]).astype(BF)
        drows = dot_t(dz[sl, :], hid[...])
        hi = drows.astype(BF)
        gscr[sl, 0:128] = hi
        gscr[sl, 128:256] = (drows - hi.astype(F32)).astype(BF)

    def put(row, value):
        buf[(row // STAT) ^ core, pl.ds(row % STAT, value.shape[0]), :] = value.astype(BF)

    for n in range(4):
        put(7936 + 1024 * n, t_dot(act[0:CAP, :], dl[0:CAP, 128 * n : 128 * n + 128]))
    ghid = t_dot(rows_s[0:CAP, :], dz[0:CAP, :])
    for n in range(8):
        put(6912 + 128 * n, ghid[:, 128 * n : 128 * n + 128])
    for part in range(7):
        at = 128 * part
        cell = iota((128, CAP), 0) + at
        spread = jnp.concatenate(
            [(slot_l == cell).astype(F32), (ring_l[...] == cell[:, :128]).astype(F32)], axis=1
        ).astype(BF)
        both = dot(spread, gscr[...])
        gx[at : at + 128, :] = (both[:, :128] + both[:, 128:]) * sg2[at : at + 128, :]

    g2w[...] = jnp.zeros_like(g2w)
    col = iota((768, C), 0) % WIDE
    own = jnp.where((col >= 1) & (col <= COLS), gx[WIDE : WIDE + 768, :], 0.0).astype(BF)
    for dy in range(3):
        g2w[WIDE * (1 + dy) : WIDE * (1 + dy) + 768, 128 * dy : 128 * dy + 128] = own
    for dx in range(3):
        part = t_dot(hx[0:960, 128 * dx : 128 * dx + 128], g2w[...])
        for dy in range(3):
            put(5760 + 128 * (3 * dy + dx), part[:, 128 * dy : 128 * dy + 128])

    for i in range(ROWS + 2):
        for dx in range(3):
            at = WIDE * i + 2 - dx
            hx[32 * i : 32 * i + 32, 128 * dx : 128 * dx + 128] = gx[at : at + 32, :].astype(BF)
    g1w[...] = jnp.zeros_like(g1w)
    for part in range(2):
        base = 256 * part
        acc = None
        for dy in range(3):
            at = base + 32 * (2 - dy)
            back = jnp.concatenate(
                [cw[384 * dy + 128 * dx : 384 * dy + 128 * dx + 128, :] for dx in range(3)], axis=1
            )
            term = dot_t(hx[at : at + 256, :], back)
            acc = term if acc is None else acc + term
        g1 = (acc * sg1[base : base + 256, :]).astype(BF)
        for dy in range(3):
            at = base + 32 * dy
            g1w[at : at + 256, 128 * dy : 128 * dy + 128] = g1
    load.wait()
    for dx in range(3):
        part = t_dot(xc[:, 128 * dx : 128 * dx + 128], g1w[...])
        for dy in range(3):
            put(4608 + 128 * (3 * dy + dx), part[:, 128 * dy : 128 * dy + 128])
        for side in range(2):
            at = 384 + 512 * dx + 256 * side
            part = t_dot(xc[:, at : at + 256], g1w[...])
            for dy in range(3):
                put(2304 * side + 256 * (3 * dy + dx), part[:, 128 * dy : 128 * dy + 128])
    lane = iota((1, C), 1)
    stats = jnp.where(lane == 0, loss, jnp.where(lane == 1, sc[4].astype(F32), 0.0))
    for n in range(2):
        buf[n, STAT : STAT + 16, :] = stat_rows(stats, (16, C)).astype(BF)
        buf[n, STAT + 16 : KEEP, :] = jnp.zeros((KEEP - STAT - 16, C), BF)
    one = pltpu.make_async_copy(buf.at[0], keep, sem.at[0])
    two = pltpu.make_async_copy(buf.at[1], give, sem.at[1])
    one.start()
    two.start()
    one.wait()
    two.wait()


def pair_kernel(keep, got, out):
    out[...] = (keep[...].astype(F32) + got[...].astype(F32)).astype(BF)
    sl = slice(STAT, STAT + 16)
    rows = keep[sl, :].astype(F32) + got[sl, :].astype(F32)
    out[sl, :] = stat_rows(jnp.sum(rows, axis=0, keepdims=True), (16, C)).astype(BF)


def spread_kernel(sc, pieces, out, mine):
    acc = pieces[0].astype(F32)
    for i in range(1, PEERS):
        acc += pieces[i].astype(F32)
    mine[...] = acc.astype(BF)
    at = STAT % SHARD

    @pl.when(sc[5] == 1)
    def _():
        rows = acc[at : at + 16]
        mine[at : at + 16, :] = stat_rows(jnp.sum(rows, axis=0, keepdims=True), (16, C)).astype(BF)

    for i in range(PEERS):
        out[i] = mine[...]


def finish_kernel(second, sc, part, *refs):
    refs = refs[5:] if second else refs
    loss, gfine, gctx, gconv, ghid, gbin, vf, vx, vc, vh, vb, sem = refs
    half = sc[1]
    which = 1 - sc[0] if second else sc[0]
    stats = jnp.sum(part[STAT : STAT + 16, :].astype(F32), axis=0, keepdims=True)
    lane = iota((1, C), 1)
    total = jnp.sum(jnp.where(lane == 1, stats, 0.0))
    scale = 1.0 / total
    loss[0, 0] = jnp.sum(jnp.where(lane == 0, stats, 0.0)) * scale

    def get(row, n):
        at = row % STAT
        return part[at : at + n, :].astype(F32) * scale

    def run(copies):
        for c in copies:
            c.start()
        return copies

    @pl.when(which == 0)
    def _():
        at = pl.multiple_of(half * 2304, 128)
        for n in range(9):
            vx[256 * n : 256 * n + 256, :] = part[pl.ds(at + 256 * n, 256), :].astype(F32) * scale
        done = run([pltpu.make_async_copy(vx, gctx, sem.at[0])])
        vf[...] = get(4608, 1152)
        vc[0:256, :] = get(5760, 256)
        done += run(
            [
                pltpu.make_async_copy(vf, gfine, sem.at[1]),
                pltpu.make_async_copy(vc.at[0:256, :], gconv.at[0:256, :], sem.at[2]),
            ]
        )
        for c in done:
            c.wait()

    @pl.when(which == 1)
    def _():
        done = []
        for m in range(4):
            sl = slice(256 * m, 256 * m + 256)
            for n in range(4):
                vb[sl, 128 * n : 128 * n + 128] = get(7936 + 1024 * n + 256 * m, 256)
            done += run([pltpu.make_async_copy(vb.at[sl, :], gbin.at[sl, :], sem.at[m])])
        vc[256:1152, :] = get(6016, 896)
        for n in range(8):
            vh[:, 128 * n : 128 * n + 128] = get(6912 + 128 * n, 128)
        done += run(
            [
                pltpu.make_async_copy(vc.at[256:1152, :], gconv.at[256:1152, :], sem.at[4]),
                pltpu.make_async_copy(vh, ghid, sem.at[5]),
            ]
        )
        for c in done:
            c.wait()


def sds(shape, dtype):
    return jax.ShapeDtypeStruct(shape, dtype)


def edge_cols(fine, ctx):
    return pl.pallas_call(
        edge_cols_kernel,
        out_shape=(sds((32, C), BF),) * 2 + (sds((512, C), BF), sds((64, HALF), BF)),
        in_specs=vmem(2),
        out_specs=tuple(vmem(4)),
        scratch_shapes=[pltpu.VMEM((512, C), F32), pltpu.VMEM((2, 64, C), F32)],
        compiler_params=limit(4),
        cost_estimate=BUSY,
        name="edge_cols",
    )(fine, ctx)


def edge_rows(*args):
    return pl.pallas_call(
        edge_rows_kernel,
        out_shape=(sds((WIDE + 256, C), BF), sds((WIDE, C), BF)),
        in_specs=[SMEM] + vmem(4),
        out_specs=tuple(vmem(2)),
        scratch_shapes=[pltpu.VMEM((2 * WIDE, C), F32), pltpu.VMEM((256, C), F32)],
        compiler_params=limit(4),
        cost_estimate=BUSY,
        name="edge_rows",
    )(*args)


def first_conv(*args):
    v = pltpu.VMEM
    edge = sds((48, C), BF)
    return pl.pallas_call(
        first_conv_kernel,
        out_shape=(sds((576, 1920), BF), sds((512, C), BF), sds((512, C), F32), edge, edge, sds((64, C), BF)),
        in_specs=[SMEM] + vmem(len(args) - 1),
        out_specs=(HBM,) + tuple(vmem(5)),
        scratch_shapes=[
            v((18 * WIDE, C), F32),
            v((288, K), BF),
            v((160, K), BF),
            v((512, C), F32),
            v((512, C), F32),
            v((16, C), F32),
            v((16, C), F32),
            v((576, 1920), BF),
            pltpu.SemaphoreType.DMA,
        ],
        compiler_params=limit(20),
        cost_estimate=pl.CostEstimate(flops=900_000_000, bytes_accessed=5_000_000, transcendentals=0),
        name="first_conv",
    )(*args)


def h_rows(*args):
    edge = sds((144, C), BF)
    return pl.pallas_call(
        h_rows_kernel,
        out_shape=(sds((ROWS * WIDE, C), BF), edge, edge),
        in_specs=[SMEM] + vmem(len(args) - 1),
        out_specs=tuple(vmem(3)),
        scratch_shapes=[pltpu.VMEM((ROWS * WIDE, C), F32), pltpu.VMEM((2 * WIDE, C), F32)],
        compiler_params=limit(6),
        cost_estimate=BUSY,
        name="h_rows",
    )(*args)


def rest(*args):
    v = pltpu.VMEM
    return pl.pallas_call(
        rest_kernel,
        out_shape=(sds((KEEP, C), BF), sds((KEEP, C), BF)),
        in_specs=[SMEM] + vmem(5) + [HBM] + vmem(len(args) - 7),
        out_specs=(ANY, ANY),
        scratch_shapes=[
            v((1000, C), F32),
            v((992, 384), BF),
            v((EXT, C), F32),
            v((EXT, C), BF),
            v((SLOTS, C), BF),
            v((SLOTS, HID), BF),
            v((SLOTS, HID), F32),
            v((SLOTS, BINS), BF),
            v((SLOTS, HID), BF),
            v((SLOTS, 256), BF),
            v((EXT + 8, C), F32),
            v((960, 384), BF),
            v((576, 384), BF),
            v((2, KEEP, C), BF),
            v((576, 1920), BF),
            pltpu.SemaphoreType.DMA((2,)),
        ],
        compiler_params=limit(28),
        cost_estimate=pl.CostEstimate(flops=3_000_000_000, bytes_accessed=8_000_000, transcendentals=0),
        name="rest",
    )(*args)


def pair_sum(keep, got):
    return pl.pallas_call(
        pair_kernel,
        out_shape=sds((KEEP, C), BF),
        in_specs=vmem(2),
        out_specs=vmem(1)[0],
        compiler_params=limit(8),
        name="pair_sum",
    )(keep, got)


def spread(sc, pieces):
    return pl.pallas_call(
        spread_kernel,
        out_shape=sds((PEERS, SHARD, C), BF),
        in_specs=[SMEM] + vmem(1),
        out_specs=vmem(1)[0],
        scratch_shapes=[pltpu.VMEM((SHARD, C), BF)],
        compiler_params=limit(8),
        name="spread",
    )(sc, pieces)


def finish(sc, part, before=None):
    v = pltpu.VMEM
    shapes = [(1152, C), (2304, C), (1152, C), (C, HID), (HID, BINS)]
    more = () if before is None else tuple(before)
    return pl.pallas_call(
        functools.partial(finish_kernel, before is not None),
        out_shape=(sds((1, 1), F32),) + tuple(sds(s, F32) for s in shapes),
        in_specs=[SMEM] + vmem(1) + [ANY] * len(more),
        out_specs=(SMEM,) + (ANY,) * 5,
        input_output_aliases={2 + n: 1 + n for n in range(len(more))},
        scratch_shapes=[v(s, F32) for s in shapes] + [pltpu.SemaphoreType.DMA((6,))],
        compiler_params=limit(16),
        cost_estimate=pl.CostEstimate(flops=800_000, bytes_accessed=5_000_000, transcendentals=0),
        name="finish_other" if more else "finish_own",
    )(sc, part, *more)


def ring_cells():
    cells = [(0, c) for c in range(34)] + [(17, c) for c in range(34)]
    cells += [(r, 0) for r in range(1, 17)] + [(r, 33) for r in range(1, 17)]
    return np.array([WIDE * r + c for r, c in cells] + [-1] * 28, np.int32)


def local(
    fine,
    context,
    interp_rows,
    interp_cols,
    fine_weight,
    ctx_weight,
    conv_weight,
    hidden_weight,
    bin_weight,
    cell_index,
    counts,
    labels,
):
    core = lax.axis_index("core")
    half = lax.axis_index("yh")
    gy = lax.axis_index(GY)
    gx = lax.axis_index(GX)
    owner = lax.axis_index(PLANE) == STAT // SHARD
    zero = jnp.zeros((), jnp.int32)
    sc = jnp.stack(
        [core, half, gy * 32 + half * ROWS, gx * COLS, counts[0, 0], owner.astype(jnp.int32), zero, zero]
    )
    idx = cell_index.reshape(1, CAP)
    lab = labels.reshape(1, CAP)
    ring = jnp.asarray(ring_cells())

    last, first, fine, context = edge_cols(fine.reshape(512, C), context.reshape(64, HALF))
    west = shift(last, GX, 8, 1)
    east = shift(first, GX, 8, -1)
    mine, edge = edge_rows(sc, fine, context, west, east)
    inner = side_swap(mine)
    outer = outer_swap(edge)

    def ctx_row(a):
        picks = [v[WIDE + 128 * s + 16 * a :][:16] for v in (mine, inner) for s in range(2)]
        return jnp.concatenate(picks, axis=0)

    north = shift(ctx_row(7), GY, 8, 1)
    south = shift(ctx_row(0), GY, 8, -1)
    xc, h_one, sg1, last, first, digs = first_conv(
        sc, interp_rows.T, interp_cols.T, fine, west, east, mine, inner, outer, north, south,
        fine_weight.reshape(1152, C), ctx_weight.reshape(4608, C), idx, lab,
    )

    west = shift(last, GX, 8, 1)
    east = shift(first, GX, 8, -1)
    wide, inner, outer = h_rows(sc, h_one, digs, west, east)
    inner = side_swap(inner)
    outer = outer_swap(outer)
    keep, give = rest(
        sc, wide, inner, outer, west, east, xc, sg1, idx, ring[None, :], lab,
        conv_weight.reshape(1152, C), hidden_weight, bin_weight,
    )

    flip = [(0, 1), (1, 0)]
    pair = pair_sum(keep, lax.ppermute(give, "core", flip))
    pieces = lax.all_to_all(pair.reshape(PEERS, SHARD, C), PLANE, 0, 0, tiled=True)
    half_sum = lax.all_to_all(spread(sc, pieces), PLANE, 0, 0, tiled=True).reshape(KEEP, C)
    other = lax.ppermute(half_sum, "core", flip)
    outs = finish(sc, half_sum)
    loss, gfine, gctx, gconv, ghid, gbin = finish(sc, other, outs[1:])
    return (
        loss.reshape(()),
        gfine.reshape(3, 3, C, C),
        gctx.reshape(3, 3, HALF, C),
        gconv.reshape(3, 3, C, C),
        ghid,
        gbin,
    )


def solution(mesh):
    devices = np.asarray(mesh.devices).reshape(4, 2, 4, 2, 2)
    split = Mesh(devices, ("x", "core", "z", "yl", "yh"))
    in_specs = (
        P(TALL, GX, None),
        P(GY, GX, "yh"),
        P(),
        P(),
        P(),
        P(),
        P(),
        P(),
        P(),
        P(TALL, GX, None),
        P(TALL, GX),
        P(TALL, GX, None),
    )
    out_specs = (P(), P(), P(None, None, "yh", None), P(), P(), P())
    return jax.shard_map(local, mesh=split, in_specs=in_specs, out_specs=out_specs, check_vma=False)
```

```python
import functools

import jax
import jax.numpy as jnp
import numpy as np
from jax import lax
from jax.experimental import pallas as pl
from jax.experimental.pallas import tpu as pltpu
from jax.sharding import Mesh
from jax.sharding import PartitionSpec as P

HID = 1024
BINS = 512
CAP = 256
ROWS = 16
COLS = 32
C = 128
K = 512
HALF = 256
SHARD = 96
PEERS = 64
BODY = 12032

GY = ("x", "core")
GX = ("z", "yl")
TALL = ("x", "core", "yh")
PLANE = ("x", "z", "yl", "yh")

BF = jnp.bfloat16
F32 = jnp.float32


def shift(x, axis, count, step):
    pairs = [(i, i + step) for i in range(count) if 0 <= i + step < count]
    return lax.ppermute(x, axis, pairs)


def side_swap(x):
    own = [(2 * t + c, 2 * t + 1 - c) for t in range(8) for c in range(2)]
    return lax.ppermute(x, TALL, own)


def outer_swap(x):
    pairs = []
    for t in range(7):
        pairs += [(2 * t + 1, 2 * t + 2), (2 * t + 2, 2 * t + 1)]
    return lax.ppermute(x, TALL, pairs)


WIDE = 48
EXT = 896
SLOTS = 384
KEEP = PEERS * SHARD
STAT = BODY // 2
MIB = 1024 * 1024
BUSY = pl.CostEstimate(flops=5_000_000_000, bytes_accessed=1_000_000, transcendentals=0)


def limit(mib):
    return pltpu.CompilerParams(vmem_limit_bytes=mib * MIB)


def vmem(n):
    return [pl.BlockSpec(memory_space=pltpu.VMEM)] * n


ANY = pl.BlockSpec(memory_space=pl.ANY)


def dot(a, b):
    return jnp.dot(a, b, preferred_element_type=F32)


def dot_t(a, b):
    return lax.dot_general(a, b, (((1,), (1,)), ((), ())), preferred_element_type=F32)


def t_dot(a, b):
    return lax.dot_general(a, b, (((0,), (0,)), ((), ())), preferred_element_type=F32)


def iota(shape, dim):
    return lax.broadcasted_iota(jnp.int32, shape, dim)


def split3(v):
    hi = v.astype(BF)
    rest = v - hi.astype(F32)
    mid = rest.astype(BF)
    low = (rest - mid.astype(F32)).astype(BF)
    return [hi.astype(F32), mid.astype(F32), low.astype(F32)]


def stat_rows(v, like):
    hi, mid, low = split3(v)
    row = iota(like, 0)
    out = jnp.where(row == 0, hi, jnp.where(row == 1, mid, jnp.where(row == 2, low, 0.0)))
    return out


def edge_cols_kernel(fine_in, ctx_in, last, first, fine, ctx, fs, xs):
    fine[...] = fine_in[...]
    ctx[...] = ctx_in[...]
    fs[...] = fine[...].astype(F32)
    for side in range(2):
        xs[side] = ctx[:, 128 * side : 128 * side + 128].astype(F32)
    for out, fc, xc in ((last, COLS - 1, 7), (first, 0, 0)):
        out[0:16, :] = fs[pl.ds(fc, 16, stride=COLS), :].astype(BF)
        sides = [xs.at[side][pl.ds(xc, 8, stride=8), :] for side in range(2)]
        out[16:32, :] = jnp.concatenate(sides, axis=0).astype(BF)


def edge_rows_kernel(fine, ctx, west, east, inner, outer, rows, xs):
    lower = lax.axis_index("yh") == 1
    rows[...] = jnp.zeros_like(rows)
    w, e = west[...].astype(F32), east[...].astype(F32)
    for n, r in ((0, 0), (1, ROWS - 1)):
        at = WIDE * n
        rows[at + 1 : at + 33, :] = fine[COLS * r : COLS * r + COLS, :].astype(F32)
        rows[at : at + 1, :] = w[r : r + 1, :]
        rows[at + 33 : at + 34, :] = e[r : r + 1, :]
    top, bottom = rows[0:WIDE, :].astype(BF), rows[WIDE : 2 * WIDE, :].astype(BF)
    inner[0:WIDE, :] = jnp.where(lower, top, bottom)
    outer[...] = jnp.where(lower, bottom, top)
    xs[...] = jnp.zeros_like(xs)
    for side in range(2):
        base = 128 * side
        for a in range(8):
            at = base + 16 * a
            xs[at + 1 : at + 9, :] = ctx[8 * a : 8 * a + 8, base : base + 128].astype(F32)
        xs[pl.ds(base, 8, stride=16), :] = w[16 + 8 * side : 24 + 8 * side, :]
        xs[pl.ds(base + 9, 8, stride=16), :] = e[16 + 8 * side : 24 + 8 * side, :]
    inner[WIDE:, :] = xs[...].astype(BF)


def ctx_rows_kernel(mine, inner, outer, down, up, rows):
    for n, got in enumerate((mine, inner)):
        for side in range(2):
            at, to = WIDE + 128 * side, 32 * n + 16 * side
            up[to : to + 16, :] = got[at : at + 16, :]
            down[to : to + 16, :] = got[at + 112 : at + 128, :]
    rows[0:WIDE, :] = inner[0:WIDE, :]
    rows[WIDE : 2 * WIDE, :] = outer[...]


def column(row):
    n = row.shape[1]
    eye = iota((n, n), 0) == iota((n, n), 1)
    return jnp.sum(jnp.where(eye, row.astype(F32), 0.0), axis=1, keepdims=True)


def first_conv_kernel(
    rows_in, cols_in, fine, west, east, mine, inner, rows, north, south, w_fine, w_ctx, idx_l, lab_l,
    xc, h1, sg, last, first, digs,
    fscr, mid, block, hscr, dscr, rmat, cmat, spot,
):
    spot[0] = lax.axis_index("yh")
    spot[1] = (2 * lax.axis_index("x") + lax.axis_index("core")) * 32
    spot[2] = (2 * lax.axis_index("z") + lax.axis_index("yl")) * COLS
    half, row0, col0 = spot[0], spot[1], spot[2]
    lower = half == 1
    for i in range(ROWS):
        at = WIDE * (i + 1) + 1
        fscr[at : at + 32, :] = fine[32 * i : 32 * i + 32, :].astype(F32)
    fscr[pl.ds(WIDE, 16, stride=WIDE), :] = west[0:16, :].astype(F32)
    fscr[pl.ds(WIDE + 33, 16, stride=WIDE), :] = east[0:16, :].astype(F32)
    a, b = rows[0:WIDE, :].astype(F32), rows[WIDE : 2 * WIDE, :].astype(F32)
    fscr[0:WIDE, :] = jnp.where(lower, a, b)
    fscr[17 * WIDE : 18 * WIDE, :] = jnp.where(lower, b, a)
    for i in range(ROWS + 2):
        for dx in range(3):
            at = WIDE * i + dx
            xc[32 * i : 32 * i + 32, 128 * dx : 128 * dx + 128] = fscr[at : at + 32, :].astype(BF)
    rmat[...] = jnp.zeros_like(rmat)
    cmat[...] = jnp.zeros_like(cmat)
    grow = row0 + iota((10, 34), 1) - 1
    gcol = col0 + iota((10, 34), 1) - 1
    rmat[0:10, 0:34] = jnp.where((grow >= 0) & (grow < 256), rows_in[...].astype(F32), 0.0)
    cmat[0:10, 0:34] = jnp.where((gcol >= 0) & (gcol < 256), cols_in[...].astype(F32), 0.0)
    for side in range(2):
        own = pl.ds(pl.multiple_of(256 * half + 128 * side, 128), 128)
        other = pl.ds(pl.multiple_of(256 * (1 - half) + 128 * side, 128), 128)
        for n, lanes, got in ((0, own, mine), (32, other, inner)):
            sl = slice(n + 16 * side, n + 16 * side + 16)
            block[0:16, lanes] = north[sl, :]
            block[16:144, lanes] = got[WIDE + 128 * side : WIDE + 128 * side + 128, :]
            block[144:160, lanes] = south[sl, :]
    pick = (iota((288, C), 0) >> 4) + 16 * half == iota((288, C), 1)
    left = dot_t(pick.astype(F32).astype(BF), rmat[...].astype(BF)).astype(BF)
    spread = (iota((16, 160), 0) == iota((16, 160), 1) >> 4).astype(F32).astype(BF)
    full = dot(left, spread)
    same = (iota((288, 160), 0) & 15) == (iota((288, 160), 1) & 15)
    kron = jnp.where(same, full, 0.0).astype(BF)
    mid[...] = dot(kron, block[...]).astype(BF)
    cell = iota((96, C), 0)
    pick = (cell & 31) + (cell >> 5) == iota((96, C), 1)
    left = dot_t(pick.astype(F32).astype(BF), cmat[...].astype(BF)).astype(BF)
    for i in range(ROWS + 2):
        wide = dot(left, mid[16 * i : 16 * i + 16, :]).astype(BF)
        for dx in range(3):
            xc[32 * i : 32 * i + 32, 384 + 512 * dx : 896 + 512 * dx] = wide[32 * dx : 32 * dx + 32]
    acc = None
    for dy in range(3):
        rows = slice(32 * dy, 32 * dy + 512)
        term = dot(xc[rows, :384], w_fine[384 * dy : 384 * dy + 384, :])
        term += dot(xc[rows, 384:], w_ctx[1536 * dy : 1536 * dy + 1536, :])
        acc = term if acc is None else acc + term
    s = jax.nn.sigmoid(acc)
    h = (acc * s).astype(BF)
    h1[...] = h
    hscr[...] = h.astype(F32)
    sg[...] = s * (1.0 + acc * (1.0 - s))
    code = lab_l[...] + 1
    kind = iota((C, CAP), 0)
    digit = jnp.where(kind == 0, code >> 5, jnp.where(kind == 1, code & 31, 0))
    digit = digit.astype(F32).astype(BF)
    named = (idx_l[...] == iota((512, CAP), 0)).astype(F32).astype(BF)
    dscr[...] = dot_t(named, digit)
    digs[0:32, :] = dscr[0:32, :].astype(BF)
    digs[32:64, :] = dscr[480:512, :].astype(BF)
    for out, c0, c1, cd in ((last, COLS - 2, COLS - 1, COLS - 1), (first, 0, 1, 0)):
        out[0:16, :] = hscr[pl.ds(c0, 16, stride=COLS), :].astype(BF)
        out[16:32, :] = hscr[pl.ds(c1, 16, stride=COLS), :].astype(BF)
        out[32:48, :] = dscr[pl.ds(cd, 16, stride=COLS), :].astype(BF)


def h_rows_kernel(h1, digs, west, east, wide, inner, outer, ws, ds):
    lower = lax.axis_index("yh") == 1
    w, e = west[...].astype(F32), east[...].astype(F32)
    ws[...] = jnp.zeros_like(ws)
    ds[...] = jnp.zeros_like(ds)
    for i in range(ROWS):
        ws[WIDE * i + 2 : WIDE * i + 34, :] = h1[32 * i : 32 * i + 32, :].astype(F32)
    for col, value in ((0, w[0:16]), (1, w[16:32]), (34, e[0:16]), (35, e[16:32])):
        ws[pl.ds(col, 16, stride=WIDE), :] = value
    for n, r in ((0, 0), (1, ROWS - 1)):
        at = WIDE * n
        ds[at + 1 : at + 33, :] = digs[32 * n : 32 * n + 32, :].astype(F32)
        ds[at : at + 1, :] = w[32 + r : 33 + r, :]
        ds[at + 33 : at + 34, :] = e[32 + r : 33 + r, :]
    wide[...] = ws[...].astype(BF)
    top, bottom = ws[0:96, :].astype(BF), ws[14 * WIDE : 16 * WIDE, :].astype(BF)
    inner[0:96, :] = jnp.where(lower, top, bottom)
    outer[0:96, :] = jnp.where(lower, bottom, top)
    top, bottom = ds[0:WIDE, :].astype(BF), ds[WIDE : 2 * WIDE, :].astype(BF)
    inner[96:144, :] = jnp.where(lower, top, bottom)
    outer[96:144, :] = jnp.where(lower, bottom, top)


def rest_kernel(
    hw, inner, outer, west, east, xc, sg1, idx_l, ring_l, lab_l, cw, hid, binw,
    keep, give,
    hp, hx, sg2, h2, rows_s, act, sgz, dl, dz, gscr, gx, g2w, g1w, buf, spot,
):
    spot[0] = lax.axis_index("core")
    spot[1] = lax.axis_index("yh")
    core, lower = spot[0], spot[1] == 1
    a, b = inner[...].astype(F32), outer[...].astype(F32)
    before, after = jnp.where(lower, a, b), jnp.where(lower, b, a)
    hp[0:96, :] = before[0:96]
    hp[96:864, :] = hw[...].astype(F32)
    hp[864:960, :] = after[0:96]
    hp[960:1000, :] = jnp.zeros((40, C), F32)
    gx[...] = jnp.zeros_like(gx)
    gx[0:WIDE, :] = before[96:144]
    gx[17 * WIDE : 18 * WIDE, :] = after[96:144]
    gx[pl.ds(WIDE, 16, stride=WIDE), :] = west[32:48, :].astype(F32)
    gx[pl.ds(WIDE + 33, 16, stride=WIDE), :] = east[32:48, :].astype(F32)
    slot_l = idx_l[...] + 16 * (idx_l[...] >> 5) + WIDE + 1
    slot_s = column(slot_l).astype(jnp.int32)
    ring_s = column(ring_l[...]).astype(jnp.int32)
    ring_pick = (ring_s == iota((128, EXT), 1)).astype(F32).astype(BF)
    code = dot(ring_pick, gx[0:EXT, :].astype(BF))
    lane = iota((128, C), 1)
    code = jnp.sum(jnp.where(lane == 0, 32.0 * code, jnp.where(lane == 1, code, 0.0)), axis=1, keepdims=True)
    own_lab = column(lab_l[...]).astype(jnp.int32)
    for dx in range(3):
        hx[:, 128 * dx : 128 * dx + 128] = hp[dx : dx + 992, :].astype(BF)
    for part in range(2):
        at = 448 * part
        acc = None
        for dy in range(3):
            term = dot(hx[at + WIDE * dy : at + WIDE * dy + 448, :], cw[384 * dy : 384 * dy + 384, :])
            acc = term if acc is None else acc + term
        s = jax.nn.sigmoid(acc)
        h2[at : at + 448, :] = (acc * s).astype(BF)
        sg2[at : at + 448, :] = s * (1.0 + acc * (1.0 - s))
    own_pick = (slot_s == iota((CAP, EXT), 1)).astype(F32).astype(BF)
    rows = dot(jnp.concatenate([own_pick, ring_pick], axis=0), h2[...]).astype(BF)
    rows_s[...] = rows
    z = dot(rows, hid[...])
    s = jax.nn.sigmoid(z)
    act[...] = (z * s).astype(BF)
    sgz[...] = s * (1.0 + z * (1.0 - s))
    logits = dot(act[...], binw[...])
    peak = jnp.max(logits, axis=1, keepdims=True)
    top = peak + jnp.log(jnp.sum(jnp.exp(logits - peak), axis=1, keepdims=True))
    labs = jnp.concatenate([own_lab, code.astype(jnp.int32) - 1], axis=0)
    hit = labs == iota((SLOTS, BINS), 1)
    live = (labs >= 0).astype(F32)
    picked = jnp.sum(jnp.where(hit, logits, 0.0), axis=1, keepdims=True)
    loss = jnp.sum((live * (top - picked))[:CAP])
    dl[...] = ((jnp.exp(logits - top) - hit.astype(F32)) * live).astype(BF)
    dz[...] = (dot_t(dl[...], binw[...]) * sgz[...]).astype(BF)
    drows = dot_t(dz[...], hid[...])
    hi = drows.astype(BF)
    gscr[:, 0:128] = hi
    gscr[:, 128:256] = (drows - hi.astype(F32)).astype(BF)

    def put(row, value):
        buf[row // STAT, pl.ds(row % STAT, value.shape[0]), :] = value.astype(BF)

    for n in range(4):
        put(7936 + 1024 * n, t_dot(act[0:CAP, :], dl[0:CAP, 128 * n : 128 * n + 128]))
    ghid = t_dot(rows_s[0:CAP, :], dz[0:CAP, :])
    for n in range(8):
        put(6912 + 128 * n, ghid[:, 128 * n : 128 * n + 128])
    lane = iota((1, C), 1)
    stats = jnp.where(lane == 0, loss, jnp.where(lane == 1, jnp.sum(live[:CAP]), 0.0))
    for n in range(2):
        buf[n, STAT : STAT + 16, :] = stat_rows(stats, (16, C)).astype(BF)
        buf[n, STAT + 16 : KEEP, :] = jnp.zeros((KEEP - STAT - 16, C), BF)
    cell = iota((EXT, CAP), 0)
    back = jnp.concatenate(
        [(slot_l == cell).astype(F32), (ring_l[...] == cell[:, :128]).astype(F32)], axis=1
    ).astype(BF)
    both = dot(back, gscr[...])
    gx[0:EXT, :] = (both[:, :128] + both[:, 128:]) * sg2[...]

    g2w[...] = jnp.zeros_like(g2w)
    col = iota((768, C), 0) % WIDE
    own = jnp.where((col >= 1) & (col <= COLS), gx[WIDE : WIDE + 768, :], 0.0).astype(BF)
    for dy in range(3):
        g2w[WIDE * (1 + dy) : WIDE * (1 + dy) + 768, 128 * dy : 128 * dy + 128] = own
    for dx in range(3):
        part = t_dot(hx[0:960, 128 * dx : 128 * dx + 128], g2w[...])
        for dy in range(3):
            put(5760 + 128 * (3 * dy + dx), part[:, 128 * dy : 128 * dy + 128])

    for i in range(ROWS + 2):
        for dx in range(3):
            at = WIDE * i + 2 - dx
            hx[32 * i : 32 * i + 32, 128 * dx : 128 * dx + 128] = gx[at : at + 32, :].astype(BF)
    g1w[...] = jnp.zeros_like(g1w)
    acc = None
    for dy in range(3):
        at = 32 * (2 - dy)
        back = jnp.concatenate(
            [cw[384 * dy + 128 * dx : 384 * dy + 128 * dx + 128, :] for dx in range(3)], axis=1
        )
        term = dot_t(hx[at : at + 512, :], back)
        acc = term if acc is None else acc + term
    g1 = (acc * sg1[...]).astype(BF)
    for dy in range(3):
        g1w[32 * dy : 32 * dy + 512, 128 * dy : 128 * dy + 128] = g1
    for dx in range(3):
        part = t_dot(xc[:, 128 * dx : 128 * dx + 128], g1w[...])
        for dy in range(3):
            put(4608 + 128 * (3 * dy + dx), part[:, 128 * dy : 128 * dy + 128])
    for dx in range(3):
        for side in range(2):
            at = 384 + 512 * dx + 256 * side
            part = t_dot(xc[:, at : at + 256], g1w[...])
            for dy in range(3):
                at = 2304 * side + 256 * (3 * dy + dx)
                put(at, part[:, 128 * dy : 128 * dy + 128])
    keep[...] = buf[core]
    give[...] = buf[1 - core]


def pair_kernel(keep, got, out):
    out[...] = (keep[...].astype(F32) + got[...].astype(F32)).astype(BF)
    sl = slice(STAT, STAT + 16)
    rows = keep[sl, :].astype(F32) + got[sl, :].astype(F32)
    out[sl, :] = stat_rows(jnp.sum(rows, axis=0, keepdims=True), (16, C)).astype(BF)


def spread_kernel(pieces, out, mine):
    acc = pieces[0].astype(F32)
    for i in range(1, PEERS):
        acc += pieces[i].astype(F32)
    mine[...] = acc.astype(BF)
    at = STAT % SHARD

    place = [lax.axis_index(a) for a in PLANE]
    owner = 16 * place[0] + 4 * place[1] + 2 * place[2] + place[3]

    @pl.when(owner == STAT // SHARD)
    def _():
        rows = acc[at : at + 16]
        mine[at : at + 16, :] = stat_rows(jnp.sum(rows, axis=0, keepdims=True), (16, C)).astype(BF)

    for i in range(PEERS):
        out[i] = mine[...]


def finish_kernel(second, part, *refs):
    refs = refs[5:] if second else refs
    if second:
        loss, refs = refs[5], refs[:5] + refs[6:]
    gfine, gctx, gconv, ghid, gbin, vf, vx, vc, vh, vb, sem = refs
    half = lax.axis_index("yh")
    which = lax.axis_index("core")
    which = 1 - which if second else which
    stats = jnp.sum(part[STAT : STAT + 16, :].astype(F32), axis=0, keepdims=True)
    lane = iota((1, C), 1)
    total = jnp.sum(jnp.where(lane == 1, stats, 0.0), axis=1, keepdims=True)
    scale = 1.0 / total
    if second:
        loss[...] = jnp.sum(jnp.where(lane == 0, stats, 0.0), axis=1, keepdims=True) * scale

    def get(row, n):
        at = row % STAT
        return part[at : at + n, :].astype(F32) * scale

    def send(done, view, out):
        c = pltpu.make_async_copy(view, out, sem.at[len(done)])
        c.start()
        done.append(c)

    @pl.when(which == 0)
    def _():
        done = []
        at = pl.multiple_of(half * 2304, 128)
        for n in range(9):
            sl = slice(256 * n, 256 * n + 256)
            vx[sl, :] = part[pl.ds(at + 256 * n, 256), :].astype(F32) * scale
            send(done, vx.at[sl, :], gctx.at[sl, :])
        for n in range(3):
            sl = slice(384 * n, 384 * n + 384)
            vf[sl, :] = get(4608 + 384 * n, 384)
            send(done, vf.at[sl, :], gfine.at[sl, :])
        vc[0:256, :] = get(5760, 256)
        send(done, vc.at[0:256, :], gconv.at[0:256, :])
        for c in done:
            c.wait()

    @pl.when(which == 1)
    def _():
        done = []
        for m in range(8):
            sl = slice(128 * m, 128 * m + 128)
            for n in range(4):
                vb[sl, 128 * n : 128 * n + 128] = get(7936 + 1024 * n + 128 * m, 128)
            send(done, vb.at[sl, :], gbin.at[sl, :])
        for n in range(2):
            sl = slice(256 + 448 * n, 704 + 448 * n)
            vc[sl, :] = get(6016 + 448 * n, 448)
            send(done, vc.at[sl, :], gconv.at[sl, :])
        for m in range(4):
            sl = slice(32 * m, 32 * m + 32)
            for n in range(8):
                vh[sl, 128 * n : 128 * n + 128] = get(6912 + 128 * n + 32 * m, 32)
            send(done, vh.at[sl, :], ghid.at[sl, :])
        for c in done:
            c.wait()


def sds(shape, dtype):
    return jax.ShapeDtypeStruct(shape, dtype)


def edge_cols(fine, ctx):
    return pl.pallas_call(
        edge_cols_kernel,
        out_shape=(sds((32, C), BF),) * 2 + (sds((512, C), BF), sds((64, HALF), BF)),
        in_specs=vmem(2),
        out_specs=tuple(vmem(4)),
        scratch_shapes=[pltpu.VMEM((512, C), F32), pltpu.VMEM((2, 64, C), F32)],
        compiler_params=limit(4),
        cost_estimate=BUSY,
        name="edge_cols",
    )(fine, ctx)


def edge_rows(*args):
    return pl.pallas_call(
        edge_rows_kernel,
        out_shape=(sds((WIDE + 256, C), BF), sds((WIDE, C), BF)),
        in_specs=vmem(4),
        out_specs=tuple(vmem(2)),
        scratch_shapes=[pltpu.VMEM((2 * WIDE, C), F32), pltpu.VMEM((256, C), F32)],
        compiler_params=limit(4),
        cost_estimate=BUSY,
        name="edge_rows",
    )(*args)


def ctx_rows(*args):
    return pl.pallas_call(
        ctx_rows_kernel,
        out_shape=(sds((64, C), BF), sds((64, C), BF), sds((2 * WIDE, C), BF)),
        in_specs=vmem(3),
        out_specs=tuple(vmem(3)),
        compiler_params=limit(4),
        cost_estimate=BUSY,
        name="ctx_rows",
    )(*args)


def first_conv(*args):
    v = pltpu.VMEM
    edge = sds((48, C), BF)
    return pl.pallas_call(
        first_conv_kernel,
        out_shape=(sds((576, 1920), BF), sds((512, C), BF), sds((512, C), F32), edge, edge, sds((64, C), BF)),
        in_specs=vmem(len(args)),
        out_specs=tuple(vmem(6)),
        scratch_shapes=[
            v((18 * WIDE, C), F32),
            v((288, K), BF),
            v((160, K), BF),
            v((512, C), F32),
            v((512, C), F32),
            v((16, C), F32),
            v((16, C), F32),
            pltpu.SMEM((4,), jnp.int32),
        ],
        compiler_params=limit(20),
        cost_estimate=pl.CostEstimate(flops=900_000_000, bytes_accessed=5_000_000, transcendentals=0),
        name="first_conv",
    )(*args)


def h_rows(*args):
    edge = sds((144, C), BF)
    return pl.pallas_call(
        h_rows_kernel,
        out_shape=(sds((ROWS * WIDE, C), BF), edge, edge),
        in_specs=vmem(len(args)),
        out_specs=tuple(vmem(3)),
        scratch_shapes=[pltpu.VMEM((ROWS * WIDE, C), F32), pltpu.VMEM((2 * WIDE, C), F32)],
        compiler_params=limit(6),
        cost_estimate=BUSY,
        name="h_rows",
    )(*args)


def rest(*args):
    v = pltpu.VMEM
    return pl.pallas_call(
        rest_kernel,
        out_shape=(sds((KEEP, C), BF), sds((KEEP, C), BF)),
        in_specs=vmem(len(args)),
        out_specs=tuple(vmem(2)),
        scratch_shapes=[
            v((1000, C), F32),
            v((992, 384), BF),
            v((EXT, C), F32),
            v((EXT, C), BF),
            v((SLOTS, C), BF),
            v((SLOTS, HID), BF),
            v((SLOTS, HID), F32),
            v((SLOTS, BINS), BF),
            v((SLOTS, HID), BF),
            v((SLOTS, 256), BF),
            v((EXT + 8, C), F32),
            v((960, 384), BF),
            v((576, 384), BF),
            v((2, KEEP, C), BF),
            pltpu.SMEM((4,), jnp.int32),
        ],
        compiler_params=limit(28),
        cost_estimate=pl.CostEstimate(flops=3_000_000_000, bytes_accessed=8_000_000, transcendentals=0),
        name="rest",
    )(*args)


def pair_sum(keep, got):
    return pl.pallas_call(
        pair_kernel,
        out_shape=sds((KEEP, C), BF),
        in_specs=vmem(2),
        out_specs=vmem(1)[0],
        compiler_params=limit(8),
        name="pair_sum",
    )(keep, got)


def spread(pieces):
    return pl.pallas_call(
        spread_kernel,
        out_shape=sds((PEERS, SHARD, C), BF),
        in_specs=vmem(1),
        out_specs=vmem(1)[0],
        scratch_shapes=[pltpu.VMEM((SHARD, C), BF)],
        compiler_params=limit(8),
        name="spread",
    )(pieces)


def finish(part, before=None):
    v = pltpu.VMEM
    shapes = [(1152, C), (2304, C), (1152, C), (C, HID), (HID, BINS)]
    second = before is not None
    more = tuple(before) if second else ()
    return pl.pallas_call(
        functools.partial(finish_kernel, second),
        out_shape=tuple(sds(s, F32) for s in shapes) + (sds((1, 1), F32),) * second,
        in_specs=vmem(1) + [ANY] * len(more),
        out_specs=(ANY,) * 5 + tuple(vmem(1)) * second,
        input_output_aliases={1 + n: n for n in range(len(more))},
        scratch_shapes=[v(s, F32) for s in shapes] + [pltpu.SemaphoreType.DMA((14,))],
        compiler_params=limit(16),
        cost_estimate=pl.CostEstimate(flops=800_000, bytes_accessed=5_000_000, transcendentals=0),
        name="finish_other" if second else "finish_own",
    )(part, *more)


def ring_cells():
    cells = [(0, c) for c in range(34)] + [(17, c) for c in range(34)]
    cells += [(r, 0) for r in range(1, 17)] + [(r, 33) for r in range(1, 17)]
    return np.array([WIDE * r + c for r, c in cells] + [-1] * 28, np.int32)


def local(
    fine,
    context,
    interp_rows,
    interp_cols,
    fine_weight,
    ctx_weight,
    conv_weight,
    hidden_weight,
    bin_weight,
    cell_index,
    counts,
    labels,
):
    idx = cell_index.reshape(1, CAP)
    live = jnp.arange(CAP, dtype=jnp.int32)[None, :] < counts
    lab = jnp.where(live, labels.reshape(1, CAP), -1)
    ring = jnp.asarray(ring_cells())

    last, first, fine, context = edge_cols(fine.reshape(512, C), context.reshape(64, HALF))
    west = shift(last, GX, 8, 1)
    east = shift(first, GX, 8, -1)
    mine, edge = edge_rows(fine, context, west, east)
    inner = side_swap(mine)
    outer = outer_swap(edge)
    down, up, rows = ctx_rows(mine, inner, outer)
    north = shift(down, GY, 8, 1)
    south = shift(up, GY, 8, -1)
    xc, h_one, sg1, last, first, digs = first_conv(
        interp_rows.T, interp_cols.T, fine, west, east, mine, inner, rows, north, south,
        fine_weight.reshape(1152, C), ctx_weight.reshape(4608, C), idx, lab,
    )

    west = shift(last, GX, 8, 1)
    east = shift(first, GX, 8, -1)
    wide, inner, outer = h_rows(h_one, digs, west, east)
    inner = side_swap(inner)
    outer = outer_swap(outer)
    keep, give = rest(
        wide, inner, outer, west, east, xc, sg1, idx, ring[None, :], lab,
        conv_weight.reshape(1152, C), hidden_weight, bin_weight,
    )

    flip = [(0, 1), (1, 0)]
    pair = pair_sum(keep, lax.ppermute(give, "core", flip))
    pieces = lax.all_to_all(pair.reshape(PEERS, SHARD, C), PLANE, 0, 0, tiled=True)
    half_sum = lax.all_to_all(spread(pieces), PLANE, 0, 0, tiled=True).reshape(KEEP, C)
    other = lax.ppermute(half_sum, "core", flip)
    outs = finish(half_sum)
    gfine, gctx, gconv, ghid, gbin, loss = finish(other, outs)
    return (
        loss.reshape(()),
        gfine.reshape(3, 3, C, C),
        gctx.reshape(3, 3, HALF, C),
        gconv.reshape(3, 3, C, C),
        ghid,
        gbin,
    )


def solution(mesh):
    devices = np.asarray(mesh.devices).reshape(4, 2, 4, 2, 2)
    split = Mesh(devices, ("x", "core", "z", "yl", "yh"))
    in_specs = (
        P(TALL, GX, None),
        P(GY, GX, "yh"),
        P(),
        P(),
        P(),
        P(),
        P(),
        P(),
        P(),
        P(TALL, GX, None),
        P(TALL, GX),
        P(TALL, GX, None),
    )
    out_specs = (P(), P(), P(None, None, "yh", None), P(), P(), P())
    return jax.shard_map(local, mesh=split, in_specs=in_specs, out_specs=out_specs, check_vma=False)
```

```python
import functools

import jax
import jax.numpy as jnp
import numpy as np
from jax import lax
from jax.experimental import pallas as pl
from jax.experimental.pallas import tpu as pltpu
from jax.sharding import Mesh
from jax.sharding import PartitionSpec as P

HID = 1024
BINS = 512
CAP = 256
ROWS = 16
COLS = 32
C = 128
K = 512
HALF = 256
SHARD = 96
PEERS = 64
BODY = 12032

GY = ("x", "core")
GX = ("z", "yl")
TALL = ("x", "core", "yh")
PLANE = ("x", "z", "yl", "yh")

BF = jnp.bfloat16
F32 = jnp.float32


def shift(x, axis, count, step):
    pairs = [(i, i + step) for i in range(count) if 0 <= i + step < count]
    return lax.ppermute(x, axis, pairs)


def side_swap(x):
    own = [(2 * t + c, 2 * t + 1 - c) for t in range(8) for c in range(2)]
    return lax.ppermute(x, TALL, own)


def outer_swap(x):
    pairs = []
    for t in range(7):
        pairs += [(2 * t + 1, 2 * t + 2), (2 * t + 2, 2 * t + 1)]
    return lax.ppermute(x, TALL, pairs)


WIDE = 48
CTX = 2 * WIDE
EXT = 896
SLOTS = 384
KEEP = PEERS * SHARD
STAT = BODY // 2
MIB = 1024 * 1024
BUSY = pl.CostEstimate(flops=5_000_000_000, bytes_accessed=1_000_000, transcendentals=0)


def limit(mib):
    return pltpu.CompilerParams(vmem_limit_bytes=mib * MIB)


def vmem(n):
    return [pl.BlockSpec(memory_space=pltpu.VMEM)] * n


ANY = pl.BlockSpec(memory_space=pl.ANY)


def dot(a, b):
    return jnp.dot(a, b, preferred_element_type=F32)


def dot_t(a, b):
    return lax.dot_general(a, b, (((1,), (1,)), ((), ())), preferred_element_type=F32)


def t_dot(a, b):
    return lax.dot_general(a, b, (((0,), (0,)), ((), ())), preferred_element_type=F32)


def iota(shape, dim):
    return lax.broadcasted_iota(jnp.int32, shape, dim)


def split3(v):
    hi = v.astype(BF)
    rest = v - hi.astype(F32)
    mid = rest.astype(BF)
    low = (rest - mid.astype(F32)).astype(BF)
    return [hi.astype(F32), mid.astype(F32), low.astype(F32)]


def stat_rows(v, like):
    hi, mid, low = split3(v)
    row = iota(like, 0)
    out = jnp.where(row == 0, hi, jnp.where(row == 1, mid, jnp.where(row == 2, low, 0.0)))
    return out


def edge_cols_kernel(fine_in, ctx_in, last, first, fine, ctx, fs, xs):
    fine[...] = fine_in[...]
    ctx[...] = ctx_in[...]
    fs[...] = fine[...].astype(F32)
    for side in range(2):
        xs[side] = ctx[:, 128 * side : 128 * side + 128].astype(F32)
    for out, fc, xc in ((last, COLS - 1, 7), (first, 0, 0)):
        out[0:16, :] = fs[pl.ds(fc, 16, stride=COLS), :].astype(BF)
        sides = [xs.at[side][pl.ds(xc, 8, stride=8), :] for side in range(2)]
        out[16:32, :] = jnp.concatenate(sides, axis=0).astype(BF)


def edge_rows_kernel(fine, ctx, west, east, inner, rows, xs):
    rows[...] = jnp.zeros_like(rows)
    w, e = west[...].astype(F32), east[...].astype(F32)
    for n, r in ((0, 0), (1, ROWS - 1)):
        at = WIDE * n
        rows[at + 1 : at + 33, :] = fine[COLS * r : COLS * r + COLS, :].astype(F32)
        rows[at : at + 1, :] = w[r : r + 1, :]
        rows[at + 33 : at + 34, :] = e[r : r + 1, :]
    inner[0:CTX, :] = rows[...].astype(BF)
    xs[...] = jnp.zeros_like(xs)
    for side in range(2):
        base = 128 * side
        for a in range(8):
            at = base + 16 * a
            xs[at + 1 : at + 9, :] = ctx[8 * a : 8 * a + 8, base : base + 128].astype(F32)
        xs[pl.ds(base, 8, stride=16), :] = w[16 + 8 * side : 24 + 8 * side, :]
        xs[pl.ds(base + 9, 8, stride=16), :] = e[16 + 8 * side : 24 + 8 * side, :]
    inner[CTX:, :] = xs[...].astype(BF)


def ctx_rows_kernel(mine, inner, down, up):
    lower = lax.axis_index("yh") == 1
    for n, got in enumerate((mine, inner)):
        for side in range(2):
            at, to = CTX + 128 * side, 32 * n + 16 * side
            up[to : to + 16, :] = got[at : at + 16, :]
            down[to : to + 16, :] = got[at + 112 : at + 128, :]
    up[64:112, :] = jnp.where(lower, inner[0:WIDE, :], mine[0:WIDE, :])
    down[64:112, :] = jnp.where(lower, mine[WIDE:CTX, :], inner[WIDE:CTX, :])


def column(row):
    n = row.shape[1]
    eye = iota((n, n), 0) == iota((n, n), 1)
    return jnp.sum(jnp.where(eye, row.astype(F32), 0.0), axis=1, keepdims=True)


def first_conv_kernel(
    rows_in, cols_in, fine, west, east, mine, inner, north, south, w_fine, w_ctx, idx_l, lab_l,
    xc, h1, sg, last, first, digs,
    fscr, mid, block, hscr, dscr, rmat, cmat, spot,
):
    spot[0] = lax.axis_index("yh")
    spot[1] = (2 * lax.axis_index("x") + lax.axis_index("core")) * 32
    spot[2] = (2 * lax.axis_index("z") + lax.axis_index("yl")) * COLS
    half, row0, col0 = spot[0], spot[1], spot[2]
    lower = half == 1
    for i in range(ROWS):
        at = WIDE * (i + 1) + 1
        fscr[at : at + 32, :] = fine[32 * i : 32 * i + 32, :].astype(F32)
    fscr[pl.ds(WIDE, 16, stride=WIDE), :] = west[0:16, :].astype(F32)
    fscr[pl.ds(WIDE + 33, 16, stride=WIDE), :] = east[0:16, :].astype(F32)
    above = jnp.where(lower, inner[WIDE:CTX, :], north[64:112, :])
    below = jnp.where(lower, south[64:112, :], inner[0:WIDE, :])
    fscr[0:WIDE, :] = above.astype(F32)
    fscr[17 * WIDE : 18 * WIDE, :] = below.astype(F32)
    for i in range(ROWS + 2):
        for dx in range(3):
            at = WIDE * i + dx
            xc[32 * i : 32 * i + 32, 128 * dx : 128 * dx + 128] = fscr[at : at + 32, :].astype(BF)
    rmat[...] = jnp.zeros_like(rmat)
    cmat[...] = jnp.zeros_like(cmat)
    grow = row0 + iota((10, 34), 1) - 1
    gcol = col0 + iota((10, 34), 1) - 1
    rmat[0:10, 0:34] = jnp.where((grow >= 0) & (grow < 256), rows_in[...].astype(F32), 0.0)
    cmat[0:10, 0:34] = jnp.where((gcol >= 0) & (gcol < 256), cols_in[...].astype(F32), 0.0)
    for side in range(2):
        own = pl.ds(pl.multiple_of(256 * half + 128 * side, 128), 128)
        other = pl.ds(pl.multiple_of(256 * (1 - half) + 128 * side, 128), 128)
        for n, lanes, got in ((0, own, mine), (32, other, inner)):
            sl = slice(n + 16 * side, n + 16 * side + 16)
            block[0:16, lanes] = north[sl, :]
            block[16:144, lanes] = got[CTX + 128 * side : CTX + 128 * side + 128, :]
            block[144:160, lanes] = south[sl, :]
    pick = (iota((288, C), 0) >> 4) + 16 * half == iota((288, C), 1)
    left = dot_t(pick.astype(F32).astype(BF), rmat[...].astype(BF)).astype(BF)
    spread = (iota((16, 160), 0) == iota((16, 160), 1) >> 4).astype(F32).astype(BF)
    full = dot(left, spread)
    same = (iota((288, 160), 0) & 15) == (iota((288, 160), 1) & 15)
    kron = jnp.where(same, full, 0.0).astype(BF)
    mid[...] = dot(kron, block[...]).astype(BF)
    cell = iota((96, C), 0)
    pick = (cell & 31) + (cell >> 5) == iota((96, C), 1)
    left = dot_t(pick.astype(F32).astype(BF), cmat[...].astype(BF)).astype(BF)
    for i in range(ROWS + 2):
        wide = dot(left, mid[16 * i : 16 * i + 16, :]).astype(BF)
        for dx in range(3):
            xc[32 * i : 32 * i + 32, 384 + 512 * dx : 896 + 512 * dx] = wide[32 * dx : 32 * dx + 32]
    acc = None
    for dy in range(3):
        rows = slice(32 * dy, 32 * dy + 512)
        term = dot(xc[rows, :384], w_fine[384 * dy : 384 * dy + 384, :])
        term += dot(xc[rows, 384:], w_ctx[1536 * dy : 1536 * dy + 1536, :])
        acc = term if acc is None else acc + term
    s = jax.nn.sigmoid(acc)
    h = (acc * s).astype(BF)
    h1[...] = h
    hscr[...] = h.astype(F32)
    sg[...] = s * (1.0 + acc * (1.0 - s))
    code = lab_l[...] + 1
    kind = iota((C, CAP), 0)
    digit = jnp.where(kind == 0, code >> 5, jnp.where(kind == 1, code & 31, 0))
    digit = digit.astype(F32).astype(BF)
    named = (idx_l[...] == iota((512, CAP), 0)).astype(F32).astype(BF)
    dscr[...] = dot_t(named, digit)
    digs[0:32, :] = dscr[0:32, :].astype(BF)
    digs[32:64, :] = dscr[480:512, :].astype(BF)
    for out, c0, c1, cd in ((last, COLS - 2, COLS - 1, COLS - 1), (first, 0, 1, 0)):
        out[0:16, :] = hscr[pl.ds(c0, 16, stride=COLS), :].astype(BF)
        out[16:32, :] = hscr[pl.ds(c1, 16, stride=COLS), :].astype(BF)
        out[32:48, :] = dscr[pl.ds(cd, 16, stride=COLS), :].astype(BF)


def h_rows_kernel(h1, digs, west, east, wide, inner, outer, ws, ds):
    lower = lax.axis_index("yh") == 1
    w, e = west[...].astype(F32), east[...].astype(F32)
    ws[...] = jnp.zeros_like(ws)
    ds[...] = jnp.zeros_like(ds)
    for i in range(ROWS):
        ws[WIDE * i + 2 : WIDE * i + 34, :] = h1[32 * i : 32 * i + 32, :].astype(F32)
    for col, value in ((0, w[0:16]), (1, w[16:32]), (34, e[0:16]), (35, e[16:32])):
        ws[pl.ds(col, 16, stride=WIDE), :] = value
    for n, r in ((0, 0), (1, ROWS - 1)):
        at = WIDE * n
        ds[at + 1 : at + 33, :] = digs[32 * n : 32 * n + 32, :].astype(F32)
        ds[at : at + 1, :] = w[32 + r : 33 + r, :]
        ds[at + 33 : at + 34, :] = e[32 + r : 33 + r, :]
    wide[...] = ws[...].astype(BF)
    top, bottom = ws[0:96, :].astype(BF), ws[14 * WIDE : 16 * WIDE, :].astype(BF)
    inner[0:96, :] = jnp.where(lower, top, bottom)
    outer[0:96, :] = jnp.where(lower, bottom, top)
    top, bottom = ds[0:WIDE, :].astype(BF), ds[WIDE : 2 * WIDE, :].astype(BF)
    inner[96:144, :] = jnp.where(lower, top, bottom)
    outer[96:144, :] = jnp.where(lower, bottom, top)


def rest_kernel(
    hw, inner, outer, west, east, xc, sg1, idx_l, ring_l, lab_l, cw, hid, binw,
    keep, give,
    hp, hx, sg2, h2, rows_s, act, sgz, dl, dz, gscr, gx, g2w, g1w, buf, spot,
):
    spot[0] = lax.axis_index("core")
    spot[1] = lax.axis_index("yh")
    core, lower = spot[0], spot[1] == 1
    a, b = inner[...].astype(F32), outer[...].astype(F32)
    before, after = jnp.where(lower, a, b), jnp.where(lower, b, a)
    hp[0:96, :] = before[0:96]
    hp[96:864, :] = hw[...].astype(F32)
    hp[864:960, :] = after[0:96]
    hp[960:1000, :] = jnp.zeros((40, C), F32)
    gx[...] = jnp.zeros_like(gx)
    gx[0:WIDE, :] = before[96:144]
    gx[17 * WIDE : 18 * WIDE, :] = after[96:144]
    gx[pl.ds(WIDE, 16, stride=WIDE), :] = west[32:48, :].astype(F32)
    gx[pl.ds(WIDE + 33, 16, stride=WIDE), :] = east[32:48, :].astype(F32)
    slot_l = idx_l[...] + 16 * (idx_l[...] >> 5) + WIDE + 1
    slot_s = column(slot_l).astype(jnp.int32)
    ring_s = column(ring_l[...]).astype(jnp.int32)
    ring_pick = (ring_s == iota((128, EXT), 1)).astype(F32).astype(BF)
    code = dot(ring_pick, gx[0:EXT, :].astype(BF))
    lane = iota((128, C), 1)
    code = jnp.sum(jnp.where(lane == 0, 32.0 * code, jnp.where(lane == 1, code, 0.0)), axis=1, keepdims=True)
    own_lab = column(lab_l[...]).astype(jnp.int32)
    for dx in range(3):
        hx[:, 128 * dx : 128 * dx + 128] = hp[dx : dx + 992, :].astype(BF)
    for part in range(2):
        at = 448 * part
        acc = None
        for dy in range(3):
            term = dot(hx[at + WIDE * dy : at + WIDE * dy + 448, :], cw[384 * dy : 384 * dy + 384, :])
            acc = term if acc is None else acc + term
        s = jax.nn.sigmoid(acc)
        h2[at : at + 448, :] = (acc * s).astype(BF)
        sg2[at : at + 448, :] = s * (1.0 + acc * (1.0 - s))
    own_pick = (slot_s == iota((CAP, EXT), 1)).astype(F32).astype(BF)
    rows = dot(jnp.concatenate([own_pick, ring_pick], axis=0), h2[...]).astype(BF)
    rows_s[...] = rows
    z = dot(rows, hid[...])
    s = jax.nn.sigmoid(z)
    act[...] = (z * s).astype(BF)
    sgz[...] = s * (1.0 + z * (1.0 - s))
    logits = dot(act[...], binw[...])
    peak = jnp.max(logits, axis=1, keepdims=True)
    top = peak + jnp.log(jnp.sum(jnp.exp(logits - peak), axis=1, keepdims=True))
    labs = jnp.concatenate([own_lab, code.astype(jnp.int32) - 1], axis=0)
    hit = labs == iota((SLOTS, BINS), 1)
    live = (labs >= 0).astype(F32)
    picked = jnp.sum(jnp.where(hit, logits, 0.0), axis=1, keepdims=True)
    loss = jnp.sum((live * (top - picked))[:CAP])
    dl[...] = ((jnp.exp(logits - top) - hit.astype(F32)) * live).astype(BF)
    dz[...] = (dot_t(dl[...], binw[...]) * sgz[...]).astype(BF)
    drows = dot_t(dz[...], hid[...])
    hi = drows.astype(BF)
    gscr[:, 0:128] = hi
    gscr[:, 128:256] = (drows - hi.astype(F32)).astype(BF)

    def put(row, value):
        buf[row // STAT, pl.ds(row % STAT, value.shape[0]), :] = value.astype(BF)

    for n in range(4):
        put(7936 + 1024 * n, t_dot(act[0:CAP, :], dl[0:CAP, 128 * n : 128 * n + 128]))
    ghid = t_dot(rows_s[0:CAP, :], dz[0:CAP, :])
    for n in range(8):
        put(6912 + 128 * n, ghid[:, 128 * n : 128 * n + 128])
    lane = iota((1, C), 1)
    stats = jnp.where(lane == 0, loss, jnp.where(lane == 1, jnp.sum(live[:CAP]), 0.0))
    for n in range(2):
        buf[n, STAT : STAT + 16, :] = stat_rows(stats, (16, C)).astype(BF)
        buf[n, STAT + 16 : KEEP, :] = jnp.zeros((KEEP - STAT - 16, C), BF)
    cell = iota((EXT, CAP), 0)
    back = jnp.concatenate(
        [(slot_l == cell).astype(F32), (ring_l[...] == cell[:, :128]).astype(F32)], axis=1
    ).astype(BF)
    both = dot(back, gscr[...])
    gx[0:EXT, :] = (both[:, :128] + both[:, 128:]) * sg2[...]

    g2w[...] = jnp.zeros_like(g2w)
    col = iota((768, C), 0) % WIDE
    own = jnp.where((col >= 1) & (col <= COLS), gx[WIDE : WIDE + 768, :], 0.0).astype(BF)
    for dy in range(3):
        g2w[WIDE * (1 + dy) : WIDE * (1 + dy) + 768, 128 * dy : 128 * dy + 128] = own
    for dx in range(3):
        part = t_dot(hx[0:960, 128 * dx : 128 * dx + 128], g2w[...])
        for dy in range(3):
            put(5760 + 128 * (3 * dy + dx), part[:, 128 * dy : 128 * dy + 128])

    for i in range(ROWS + 2):
        for dx in range(3):
            at = WIDE * i + 2 - dx
            hx[32 * i : 32 * i + 32, 128 * dx : 128 * dx + 128] = gx[at : at + 32, :].astype(BF)
    g1w[...] = jnp.zeros_like(g1w)
    acc = None
    for dy in range(3):
        at = 32 * (2 - dy)
        back = jnp.concatenate(
            [cw[384 * dy + 128 * dx : 384 * dy + 128 * dx + 128, :] for dx in range(3)], axis=1
        )
        term = dot_t(hx[at : at + 512, :], back)
        acc = term if acc is None else acc + term
    g1 = (acc * sg1[...]).astype(BF)
    for dy in range(3):
        g1w[32 * dy : 32 * dy + 512, 128 * dy : 128 * dy + 128] = g1
    for dx in range(3):
        part = t_dot(xc[:, 128 * dx : 128 * dx + 128], g1w[...])
        for dy in range(3):
            put(4608 + 128 * (3 * dy + dx), part[:, 128 * dy : 128 * dy + 128])
    for dx in range(3):
        for side in range(2):
            at = 384 + 512 * dx + 256 * side
            part = t_dot(xc[:, at : at + 256], g1w[...])
            for dy in range(3):
                at = 2304 * side + 256 * (3 * dy + dx)
                put(at, part[:, 128 * dy : 128 * dy + 128])
    keep[...] = buf[core]
    give[...] = buf[1 - core]


def pair_kernel(keep, got, out):
    out[...] = (keep[...].astype(F32) + got[...].astype(F32)).astype(BF)
    sl = slice(STAT, STAT + 16)
    rows = keep[sl, :].astype(F32) + got[sl, :].astype(F32)
    out[sl, :] = stat_rows(jnp.sum(rows, axis=0, keepdims=True), (16, C)).astype(BF)


def spread_kernel(pieces, out, mine):
    acc = pieces[0].astype(F32)
    for i in range(1, PEERS):
        acc += pieces[i].astype(F32)
    mine[...] = acc.astype(BF)
    at = STAT % SHARD

    place = [lax.axis_index(a) for a in PLANE]
    owner = 16 * place[0] + 4 * place[1] + 2 * place[2] + place[3]

    @pl.when(owner == STAT // SHARD)
    def _():
        rows = acc[at : at + 16]
        mine[at : at + 16, :] = stat_rows(jnp.sum(rows, axis=0, keepdims=True), (16, C)).astype(BF)

    for i in range(PEERS):
        out[i] = mine[...]


def finish_kernel(second, part, *refs):
    refs = refs[5:] if second else refs
    if second:
        loss, refs = refs[5], refs[:5] + refs[6:]
    gfine, gctx, gconv, ghid, gbin, vf, vx, vc, vh, vb, sem = refs
    half = lax.axis_index("yh")
    which = lax.axis_index("core")
    which = 1 - which if second else which
    stats = jnp.sum(part[STAT : STAT + 16, :].astype(F32), axis=0, keepdims=True)
    lane = iota((1, C), 1)
    total = jnp.sum(jnp.where(lane == 1, stats, 0.0), axis=1, keepdims=True)
    scale = 1.0 / total
    if second:
        loss[...] = jnp.sum(jnp.where(lane == 0, stats, 0.0), axis=1, keepdims=True) * scale

    def get(row, n):
        at = row % STAT
        return part[at : at + n, :].astype(F32) * scale

    def send(done, view, out):
        c = pltpu.make_async_copy(view, out, sem.at[len(done)])
        c.start()
        done.append(c)

    @pl.when(which == 0)
    def _():
        done = []
        at = pl.multiple_of(half * 2304, 128)
        for n in range(9):
            sl = slice(256 * n, 256 * n + 256)
            vx[sl, :] = part[pl.ds(at + 256 * n, 256), :].astype(F32) * scale
            send(done, vx.at[sl, :], gctx.at[sl, :])
        for n in range(3):
            sl = slice(384 * n, 384 * n + 384)
            vf[sl, :] = get(4608 + 384 * n, 384)
            send(done, vf.at[sl, :], gfine.at[sl, :])
        vc[0:256, :] = get(5760, 256)
        send(done, vc.at[0:256, :], gconv.at[0:256, :])
        for c in done:
            c.wait()

    @pl.when(which == 1)
    def _():
        done = []
        for m in range(8):
            sl = slice(128 * m, 128 * m + 128)
            for n in range(4):
                vb[sl, 128 * n : 128 * n + 128] = get(7936 + 1024 * n + 128 * m, 128)
            send(done, vb.at[sl, :], gbin.at[sl, :])
        for n in range(2):
            sl = slice(256 + 448 * n, 704 + 448 * n)
            vc[sl, :] = get(6016 + 448 * n, 448)
            send(done, vc.at[sl, :], gconv.at[sl, :])
        for m in range(4):
            sl = slice(32 * m, 32 * m + 32)
            for n in range(8):
                vh[sl, 128 * n : 128 * n + 128] = get(6912 + 128 * n + 32 * m, 32)
            send(done, vh.at[sl, :], ghid.at[sl, :])
        for c in done:
            c.wait()


def sds(shape, dtype):
    return jax.ShapeDtypeStruct(shape, dtype)


def edge_cols(fine, ctx):
    return pl.pallas_call(
        edge_cols_kernel,
        out_shape=(sds((32, C), BF),) * 2 + (sds((512, C), BF), sds((64, HALF), BF)),
        in_specs=vmem(2),
        out_specs=tuple(vmem(4)),
        scratch_shapes=[pltpu.VMEM((512, C), F32), pltpu.VMEM((2, 64, C), F32)],
        compiler_params=limit(4),
        cost_estimate=BUSY,
        name="edge_cols",
    )(fine, ctx)


def edge_rows(*args):
    return pl.pallas_call(
        edge_rows_kernel,
        out_shape=sds((CTX + 256, C), BF),
        in_specs=vmem(4),
        out_specs=vmem(1)[0],
        scratch_shapes=[pltpu.VMEM((2 * WIDE, C), F32), pltpu.VMEM((256, C), F32)],
        compiler_params=limit(4),
        cost_estimate=BUSY,
        name="edge_rows",
    )(*args)


def ctx_rows(*args):
    return pl.pallas_call(
        ctx_rows_kernel,
        out_shape=(sds((112, C), BF), sds((112, C), BF)),
        in_specs=vmem(2),
        out_specs=tuple(vmem(2)),
        compiler_params=limit(4),
        cost_estimate=BUSY,
        name="ctx_rows",
    )(*args)


def first_conv(*args):
    v = pltpu.VMEM
    edge = sds((48, C), BF)
    return pl.pallas_call(
        first_conv_kernel,
        out_shape=(sds((576, 1920), BF), sds((512, C), BF), sds((512, C), F32), edge, edge, sds((64, C), BF)),
        in_specs=vmem(len(args)),
        out_specs=tuple(vmem(6)),
        scratch_shapes=[
            v((18 * WIDE, C), F32),
            v((288, K), BF),
            v((160, K), BF),
            v((512, C), F32),
            v((512, C), F32),
            v((16, C), F32),
            v((16, C), F32),
            pltpu.SMEM((4,), jnp.int32),
        ],
        compiler_params=limit(20),
        cost_estimate=pl.CostEstimate(flops=900_000_000, bytes_accessed=5_000_000, transcendentals=0),
        name="first_conv",
    )(*args)


def h_rows(*args):
    edge = sds((144, C), BF)
    return pl.pallas_call(
        h_rows_kernel,
        out_shape=(sds((ROWS * WIDE, C), BF), edge, edge),
        in_specs=vmem(len(args)),
        out_specs=tuple(vmem(3)),
        scratch_shapes=[pltpu.VMEM((ROWS * WIDE, C), F32), pltpu.VMEM((2 * WIDE, C), F32)],
        compiler_params=limit(6),
        cost_estimate=BUSY,
        name="h_rows",
    )(*args)


def rest(*args):
    v = pltpu.VMEM
    return pl.pallas_call(
        rest_kernel,
        out_shape=(sds((KEEP, C), BF), sds((KEEP, C), BF)),
        in_specs=vmem(len(args)),
        out_specs=tuple(vmem(2)),
        scratch_shapes=[
            v((1000, C), F32),
            v((992, 384), BF),
            v((EXT, C), F32),
            v((EXT, C), BF),
            v((SLOTS, C), BF),
            v((SLOTS, HID), BF),
            v((SLOTS, HID), F32),
            v((SLOTS, BINS), BF),
            v((SLOTS, HID), BF),
            v((SLOTS, 256), BF),
            v((EXT + 8, C), F32),
            v((960, 384), BF),
            v((576, 384), BF),
            v((2, KEEP, C), BF),
            pltpu.SMEM((4,), jnp.int32),
        ],
        compiler_params=limit(28),
        cost_estimate=pl.CostEstimate(flops=3_000_000_000, bytes_accessed=8_000_000, transcendentals=0),
        name="rest",
    )(*args)


def pair_sum(keep, got):
    return pl.pallas_call(
        pair_kernel,
        out_shape=sds((KEEP, C), BF),
        in_specs=vmem(2),
        out_specs=vmem(1)[0],
        compiler_params=limit(8),
        name="pair_sum",
    )(keep, got)


def spread(pieces):
    return pl.pallas_call(
        spread_kernel,
        out_shape=sds((PEERS, SHARD, C), BF),
        in_specs=vmem(1),
        out_specs=vmem(1)[0],
        scratch_shapes=[pltpu.VMEM((SHARD, C), BF)],
        compiler_params=limit(8),
        name="spread",
    )(pieces)


def finish(part, before=None):
    v = pltpu.VMEM
    shapes = [(1152, C), (2304, C), (1152, C), (C, HID), (HID, BINS)]
    second = before is not None
    more = tuple(before) if second else ()
    return pl.pallas_call(
        functools.partial(finish_kernel, second),
        out_shape=tuple(sds(s, F32) for s in shapes) + (sds((1, 1), F32),) * second,
        in_specs=vmem(1) + [ANY] * len(more),
        out_specs=(ANY,) * 5 + tuple(vmem(1)) * second,
        input_output_aliases={1 + n: n for n in range(len(more))},
        scratch_shapes=[v(s, F32) for s in shapes] + [pltpu.SemaphoreType.DMA((14,))],
        compiler_params=limit(16),
        cost_estimate=pl.CostEstimate(flops=800_000, bytes_accessed=5_000_000, transcendentals=0),
        name="finish_other" if second else "finish_own",
    )(part, *more)


def ring_cells():
    cells = [(0, c) for c in range(34)] + [(17, c) for c in range(34)]
    cells += [(r, 0) for r in range(1, 17)] + [(r, 33) for r in range(1, 17)]
    return np.array([WIDE * r + c for r, c in cells] + [-1] * 28, np.int32)


def local(
    fine,
    context,
    interp_rows,
    interp_cols,
    fine_weight,
    ctx_weight,
    conv_weight,
    hidden_weight,
    bin_weight,
    cell_index,
    counts,
    labels,
):
    idx = cell_index.reshape(1, CAP)
    live = jnp.arange(CAP, dtype=jnp.int32)[None, :] < counts
    lab = jnp.where(live, labels.reshape(1, CAP), -1)
    ring = jnp.asarray(ring_cells())

    last, first, fine, context = edge_cols(fine.reshape(512, C), context.reshape(64, HALF))
    west = shift(last, GX, 8, 1)
    east = shift(first, GX, 8, -1)
    mine = edge_rows(fine, context, west, east)
    inner = side_swap(mine)
    down, up = ctx_rows(mine, inner)
    north = shift(down, GY, 8, 1)
    south = shift(up, GY, 8, -1)
    xc, h_one, sg1, last, first, digs = first_conv(
        interp_rows.T, interp_cols.T, fine, west, east, mine, inner, north, south,
        fine_weight.reshape(1152, C), ctx_weight.reshape(4608, C), idx, lab,
    )

    west = shift(last, GX, 8, 1)
    east = shift(first, GX, 8, -1)
    wide, inner, outer = h_rows(h_one, digs, west, east)
    inner = side_swap(inner)
    outer = outer_swap(outer)
    keep, give = rest(
        wide, inner, outer, west, east, xc, sg1, idx, ring[None, :], lab,
        conv_weight.reshape(1152, C), hidden_weight, bin_weight,
    )

    flip = [(0, 1), (1, 0)]
    pair = pair_sum(keep, lax.ppermute(give, "core", flip))
    pieces = lax.all_to_all(pair.reshape(PEERS, SHARD, C), PLANE, 0, 0, tiled=True)
    half_sum = lax.all_to_all(spread(pieces), PLANE, 0, 0, tiled=True).reshape(KEEP, C)
    other = lax.ppermute(half_sum, "core", flip)
    outs = finish(half_sum)
    gfine, gctx, gconv, ghid, gbin, loss = finish(other, outs)
    return (
        loss.reshape(()),
        gfine.reshape(3, 3, C, C),
        gctx.reshape(3, 3, HALF, C),
        gconv.reshape(3, 3, C, C),
        ghid,
        gbin,
    )


def solution(mesh):
    devices = np.asarray(mesh.devices).reshape(4, 2, 4, 2, 2)
    split = Mesh(devices, ("x", "core", "z", "yl", "yh"))
    in_specs = (
        P(TALL, GX, None),
        P(GY, GX, "yh"),
        P(),
        P(),
        P(),
        P(),
        P(),
        P(),
        P(),
        P(TALL, GX, None),
        P(TALL, GX),
        P(TALL, GX, None),
    )
    out_specs = (P(), P(), P(None, None, "yh", None), P(), P(), P())
    return jax.shard_map(local, mesh=split, in_specs=in_specs, out_specs=out_specs, check_vma=False)
```

```python
import functools

import jax
import jax.numpy as jnp
import numpy as np
from jax import lax
from jax.experimental import pallas as pl
from jax.experimental.pallas import tpu as pltpu
from jax.sharding import Mesh
from jax.sharding import PartitionSpec as P

HID = 1024
BINS = 512
CAP = 256
ROWS = 16
COLS = 32
C = 128
K = 512
HALF = 256
SHARD = 96
PEERS = 64
BODY = 12032

GY = ("x", "core")
GX = ("z", "yl")
TALL = ("x", "core", "yh")
PLANE = ("x", "z", "yl", "yh")

BF = jnp.bfloat16
F32 = jnp.float32


def shift(x, axis, count, step):
    pairs = [(i, i + step) for i in range(count) if 0 <= i + step < count]
    return lax.ppermute(x, axis, pairs)


def side_swap(x):
    own = [(2 * t + c, 2 * t + 1 - c) for t in range(8) for c in range(2)]
    return lax.ppermute(x, TALL, own)


def outer_swap(x):
    pairs = []
    for t in range(7):
        pairs += [(2 * t + 1, 2 * t + 2), (2 * t + 2, 2 * t + 1)]
    return lax.ppermute(x, TALL, pairs)


WIDE = 48
CTX = 2 * WIDE
EXT = 896
SLOTS = 384
KEEP = PEERS * SHARD
STAT = BODY // 2
MIB = 1024 * 1024
BUSY = pl.CostEstimate(flops=5_000_000_000, bytes_accessed=1_000_000, transcendentals=0)


def limit(mib):
    return pltpu.CompilerParams(vmem_limit_bytes=mib * MIB)


def vmem(n):
    return [pl.BlockSpec(memory_space=pltpu.VMEM)] * n


ANY = pl.BlockSpec(memory_space=pl.ANY)


def dot(a, b):
    return jnp.dot(a, b, preferred_element_type=F32)


def dot_t(a, b):
    return lax.dot_general(a, b, (((1,), (1,)), ((), ())), preferred_element_type=F32)


def t_dot(a, b):
    return lax.dot_general(a, b, (((0,), (0,)), ((), ())), preferred_element_type=F32)


def iota(shape, dim):
    return lax.broadcasted_iota(jnp.int32, shape, dim)


def split3(v):
    hi = v.astype(BF)
    rest = v - hi.astype(F32)
    mid = rest.astype(BF)
    low = (rest - mid.astype(F32)).astype(BF)
    return [hi.astype(F32), mid.astype(F32), low.astype(F32)]


def stat_rows(v, like):
    hi, mid, low = split3(v)
    row = iota(like, 0)
    out = jnp.where(row == 0, hi, jnp.where(row == 1, mid, jnp.where(row == 2, low, 0.0)))
    return out


def edge_cols_kernel(fine_in, ctx_in, last, first, fine, ctx, fs, xs):
    fine[...] = fine_in[...]
    ctx[...] = ctx_in[...]
    fs[...] = fine[...].astype(F32)
    for side in range(2):
        xs[side] = ctx[:, 128 * side : 128 * side + 128].astype(F32)
    for out, fc, xc in ((last, COLS - 1, 7), (first, 0, 0)):
        out[0:16, :] = fs[pl.ds(fc, 16, stride=COLS), :].astype(BF)
        sides = [xs.at[side][pl.ds(xc, 8, stride=8), :] for side in range(2)]
        out[16:32, :] = jnp.concatenate(sides, axis=0).astype(BF)


def edge_rows_kernel(fine, ctx, west, east, inner, rows, xs):
    rows[...] = jnp.zeros_like(rows)
    w, e = west[...].astype(F32), east[...].astype(F32)
    for n, r in ((0, 0), (1, ROWS - 1)):
        at = WIDE * n
        rows[at + 1 : at + 33, :] = fine[COLS * r : COLS * r + COLS, :].astype(F32)
        rows[at : at + 1, :] = w[r : r + 1, :]
        rows[at + 33 : at + 34, :] = e[r : r + 1, :]
    inner[0:CTX, :] = rows[...].astype(BF)
    for side in range(2):
        base = 80 * side
        lanes = slice(128 * side, 128 * side + 128)
        for a in range(8):
            at = base + 10 * a
            xs[at + 1 : at + 9, :] = ctx[8 * a : 8 * a + 8, lanes].astype(F32)
        xs[pl.ds(base, 8, stride=10), :] = w[16 + 8 * side : 24 + 8 * side, :]
        xs[pl.ds(base + 9, 8, stride=10), :] = e[16 + 8 * side : 24 + 8 * side, :]
    inner[CTX:, :] = xs[...].astype(BF)


def ctx_rows_kernel(mine, inner, down, up, xs):
    lower = lax.axis_index("yh") == 1
    xs[160:, :] = jnp.zeros((16, C), F32)
    for n, got in enumerate((mine, inner)):
        xs[0:160, :] = got[CTX:, :].astype(F32)
        for side in range(2):
            at, to = 80 * side, 32 * n + 16 * side
            up[to : to + 16, :] = xs[at : at + 16, :].astype(BF)
            down[to : to + 16, :] = xs[at + 70 : at + 86, :].astype(BF)
    up[64:112, :] = jnp.where(lower, inner[0:WIDE, :], mine[0:WIDE, :])
    down[64:112, :] = jnp.where(lower, mine[WIDE:CTX, :], inner[WIDE:CTX, :])


def column(row):
    n = row.shape[1]
    eye = iota((n, n), 0) == iota((n, n), 1)
    return jnp.sum(jnp.where(eye, row.astype(F32), 0.0), axis=1, keepdims=True)


def first_conv_kernel(
    rows_in, cols_in, fine, west, east, mine, inner, north, south, w_fine, w_ctx, idx_l, lab_l,
    xc, h1, sg, last, first, digs,
    fscr, mid, block, hscr, dscr, rmat, cmat, xs, pre, spot,
):
    spot[0] = lax.axis_index("yh")
    spot[1] = (2 * lax.axis_index("x") + lax.axis_index("core")) * 32
    spot[2] = (2 * lax.axis_index("z") + lax.axis_index("yl")) * COLS
    half, row0, col0 = spot[0], spot[1], spot[2]
    lower = half == 1
    for i in range(ROWS):
        at = WIDE * (i + 1) + 1
        fscr[at : at + 32, :] = fine[32 * i : 32 * i + 32, :].astype(F32)
    fscr[pl.ds(WIDE, 16, stride=WIDE), :] = west[0:16, :].astype(F32)
    fscr[pl.ds(WIDE + 33, 16, stride=WIDE), :] = east[0:16, :].astype(F32)
    above = jnp.where(lower, inner[WIDE:CTX, :], north[64:112, :])
    below = jnp.where(lower, south[64:112, :], inner[0:WIDE, :])
    fscr[0:WIDE, :] = above.astype(F32)
    fscr[17 * WIDE : 18 * WIDE, :] = below.astype(F32)
    for i in range(ROWS + 2):
        for dx in range(3):
            at = WIDE * i + dx
            xc[32 * i : 32 * i + 32, 128 * dx : 128 * dx + 128] = fscr[at : at + 32, :].astype(BF)
    rmat[...] = jnp.zeros_like(rmat)
    cmat[...] = jnp.zeros_like(cmat)
    grow = row0 + iota((10, 34), 1) - 1
    gcol = col0 + iota((10, 34), 1) - 1
    rmat[0:10, 0:34] = jnp.where((grow >= 0) & (grow < 256), rows_in[...].astype(F32), 0.0)
    cmat[0:10, 0:34] = jnp.where((gcol >= 0) & (gcol < 256), cols_in[...].astype(F32), 0.0)
    xs[160:, :] = jnp.zeros((16, C), F32)
    for n, part, got in ((0, half, mine), (32, 1 - half, inner)):
        xs[0:160, :] = got[CTX:, :].astype(F32)
        for side in range(2):
            lanes = pl.ds(pl.multiple_of(256 * part + 128 * side, 128), 128)
            sl = slice(n + 16 * side, n + 16 * side + 16)
            block[0:16, lanes] = north[sl, :]
            for a in range(8):
                at = 80 * side + 10 * a
                block[16 + 16 * a : 32 + 16 * a, lanes] = xs[at : at + 16, :].astype(BF)
            block[144:160, lanes] = south[sl, :]
    pick = (iota((288, C), 0) >> 4) + 16 * half == iota((288, C), 1)
    left = dot_t(pick.astype(F32).astype(BF), rmat[...].astype(BF)).astype(BF)
    spread = (iota((16, 160), 0) == iota((16, 160), 1) >> 4).astype(F32).astype(BF)
    full = dot(left, spread)
    same = (iota((288, 160), 0) & 15) == (iota((288, 160), 1) & 15)
    kron = jnp.where(same, full, 0.0).astype(BF)
    mid[...] = dot(kron, block[...]).astype(BF)
    cell = iota((96, C), 0)
    pick = (cell & 31) + (cell >> 5) == iota((96, C), 1)
    left = dot_t(pick.astype(F32).astype(BF), cmat[...].astype(BF)).astype(BF)
    for i in range(ROWS + 2):
        wide = dot(left, mid[16 * i : 16 * i + 16, :]).astype(BF)
        for dx in range(3):
            xc[32 * i : 32 * i + 32, 384 + 512 * dx : 896 + 512 * dx] = wide[32 * dx : 32 * dx + 32]
    wf = jnp.concatenate([w_fine[384 * dy : 384 * dy + 384, :] for dy in range(3)], axis=1)
    wc = jnp.concatenate([w_ctx[1536 * dy : 1536 * dy + 1536, :] for dy in range(3)], axis=1)
    pre[...] = dot(xc[:, :384], wf) + dot(xc[:, 384:], wc)
    acc = sum(pre[32 * dy : 32 * dy + 512, 128 * dy : 128 * dy + 128] for dy in range(3))
    s = jax.nn.sigmoid(acc)
    h = (acc * s).astype(BF)
    h1[...] = h
    hscr[...] = h.astype(F32)
    sg[...] = s * (1.0 + acc * (1.0 - s))
    code = lab_l[...] + 1
    kind = iota((C, CAP), 0)
    digit = jnp.where(kind == 0, code >> 5, jnp.where(kind == 1, code & 31, 0))
    digit = digit.astype(F32).astype(BF)
    named = (idx_l[...] == iota((512, CAP), 0)).astype(F32).astype(BF)
    dscr[...] = dot_t(named, digit)
    digs[0:32, :] = dscr[0:32, :].astype(BF)
    digs[32:64, :] = dscr[480:512, :].astype(BF)
    for out, c0, c1, cd in ((last, COLS - 2, COLS - 1, COLS - 1), (first, 0, 1, 0)):
        out[0:16, :] = hscr[pl.ds(c0, 16, stride=COLS), :].astype(BF)
        out[16:32, :] = hscr[pl.ds(c1, 16, stride=COLS), :].astype(BF)
        out[32:48, :] = dscr[pl.ds(cd, 16, stride=COLS), :].astype(BF)


def h_rows_kernel(h1, digs, west, east, wide, inner, outer, ws, ds):
    lower = lax.axis_index("yh") == 1
    w, e = west[...].astype(F32), east[...].astype(F32)
    ws[...] = jnp.zeros_like(ws)
    ds[...] = jnp.zeros_like(ds)
    for i in range(ROWS):
        ws[WIDE * i + 2 : WIDE * i + 34, :] = h1[32 * i : 32 * i + 32, :].astype(F32)
    for col, value in ((0, w[0:16]), (1, w[16:32]), (34, e[0:16]), (35, e[16:32])):
        ws[pl.ds(col, 16, stride=WIDE), :] = value
    for n, r in ((0, 0), (1, ROWS - 1)):
        at = WIDE * n
        ds[at + 1 : at + 33, :] = digs[32 * n : 32 * n + 32, :].astype(F32)
        ds[at : at + 1, :] = w[32 + r : 33 + r, :]
        ds[at + 33 : at + 34, :] = e[32 + r : 33 + r, :]
    wide[...] = ws[...].astype(BF)
    top, bottom = ws[0:96, :].astype(BF), ws[14 * WIDE : 16 * WIDE, :].astype(BF)
    inner[0:96, :] = jnp.where(lower, top, bottom)
    outer[0:96, :] = jnp.where(lower, bottom, top)
    top, bottom = ds[0:WIDE, :].astype(BF), ds[WIDE : 2 * WIDE, :].astype(BF)
    inner[96:144, :] = jnp.where(lower, top, bottom)
    outer[96:144, :] = jnp.where(lower, bottom, top)


def rest_kernel(
    hw, inner, outer, west, east, xc, sg1, idx_l, ring_l, lab_l, cw, hid, binw,
    out,
    hp, hx, sg2, h2, rows_s, act, sgz, dl, dz, gscr, gx, g2w, g1w, pre, spot,
):
    spot[0] = lax.axis_index("core")
    spot[1] = lax.axis_index("yh")
    core, lower = spot[0], spot[1] == 1
    a, b = inner[...].astype(F32), outer[...].astype(F32)
    before, after = jnp.where(lower, a, b), jnp.where(lower, b, a)
    hp[0:96, :] = before[0:96]
    hp[96:864, :] = hw[...].astype(F32)
    hp[864:960, :] = after[0:96]
    hp[960:1000, :] = jnp.zeros((40, C), F32)
    gx[...] = jnp.zeros_like(gx)
    gx[0:WIDE, :] = before[96:144]
    gx[17 * WIDE : 18 * WIDE, :] = after[96:144]
    gx[pl.ds(WIDE, 16, stride=WIDE), :] = west[32:48, :].astype(F32)
    gx[pl.ds(WIDE + 33, 16, stride=WIDE), :] = east[32:48, :].astype(F32)
    slot_l = idx_l[...] + 16 * (idx_l[...] >> 5) + WIDE + 1
    slot_s = column(slot_l).astype(jnp.int32)
    ring_s = column(ring_l[...]).astype(jnp.int32)
    ring_pick = (ring_s == iota((128, EXT), 1)).astype(F32).astype(BF)
    code = dot(ring_pick, gx[0:EXT, :].astype(BF))
    lane = iota((128, C), 1)
    code = jnp.sum(jnp.where(lane == 0, 32.0 * code, jnp.where(lane == 1, code, 0.0)), axis=1, keepdims=True)
    own_lab = column(lab_l[...]).astype(jnp.int32)
    for dx in range(3):
        hx[:, 128 * dx : 128 * dx + 128] = hp[dx : dx + 992, :].astype(BF)
    forth = jnp.concatenate([cw[384 * dy : 384 * dy + 384, :] for dy in range(3)], axis=1)
    pre[...] = dot(hx[...], forth)
    acc = sum(pre[WIDE * dy : WIDE * dy + EXT, 128 * dy : 128 * dy + 128] for dy in range(3))
    s = jax.nn.sigmoid(acc)
    h2[...] = (acc * s).astype(BF)
    sg2[...] = s * (1.0 + acc * (1.0 - s))
    own_pick = (slot_s == iota((CAP, EXT), 1)).astype(F32).astype(BF)
    rows = dot(jnp.concatenate([own_pick, ring_pick], axis=0), h2[...]).astype(BF)
    rows_s[...] = rows
    z = dot(rows, hid[...])
    s = jax.nn.sigmoid(z)
    act[...] = (z * s).astype(BF)
    sgz[...] = s * (1.0 + z * (1.0 - s))
    logits = dot(act[...], binw[...])
    peak = jnp.max(logits, axis=1, keepdims=True)
    top = peak + jnp.log(jnp.sum(jnp.exp(logits - peak), axis=1, keepdims=True))
    labs = jnp.concatenate([own_lab, code.astype(jnp.int32) - 1], axis=0)
    hit = labs == iota((SLOTS, BINS), 1)
    live = (labs >= 0).astype(F32)
    picked = jnp.sum(jnp.where(hit, logits, 0.0), axis=1, keepdims=True)
    loss = jnp.sum((live * (top - picked))[:CAP])
    dl[...] = ((jnp.exp(logits - top) - hit.astype(F32)) * live).astype(BF)
    dz[...] = (dot_t(dl[...], binw[...]) * sgz[...]).astype(BF)
    drows = dot_t(dz[...], hid[...])
    hi = drows.astype(BF)
    gscr[:, 0:128] = hi
    gscr[:, 128:256] = (drows - hi.astype(F32)).astype(BF)

    def put(row, value):
        out[(row // STAT) ^ core, pl.ds(row % STAT, value.shape[0]), :] = value.astype(BF)

    for n in range(4):
        put(7936 + 1024 * n, t_dot(act[0:CAP, :], dl[0:CAP, 128 * n : 128 * n + 128]))
    ghid = t_dot(rows_s[0:CAP, :], dz[0:CAP, :])
    for n in range(8):
        put(6912 + 128 * n, ghid[:, 128 * n : 128 * n + 128])
    lane = iota((1, C), 1)
    stats = jnp.where(lane == 0, loss, jnp.where(lane == 1, jnp.sum(live[:CAP]), 0.0))
    for n in range(2):
        out[n, STAT : STAT + 16, :] = stat_rows(stats, (16, C)).astype(BF)
        out[n, STAT + 16 : KEEP, :] = jnp.zeros((KEEP - STAT - 16, C), BF)
    cell = iota((EXT, CAP), 0)
    back = jnp.concatenate(
        [(slot_l == cell).astype(F32), (ring_l[...] == cell[:, :128]).astype(F32)], axis=1
    ).astype(BF)
    both = dot(back, gscr[...])
    gx[0:EXT, :] = (both[:, :128] + both[:, 128:]) * sg2[...]

    g2w[...] = jnp.zeros_like(g2w)
    col = iota((WIDE, C), 0)
    inside = jnp.where((col >= 1) & (col <= COLS), 1.0, 0.0)
    own = (gx[WIDE : WIDE + 768, :] * jnp.concatenate([inside] * ROWS, axis=0)).astype(BF)
    for dy in range(3):
        g2w[WIDE * (1 + dy) : WIDE * (1 + dy) + 768, 128 * dy : 128 * dy + 128] = own
    for dx in range(3):
        part = t_dot(hx[0:960, 128 * dx : 128 * dx + 128], g2w[...])
        for dy in range(3):
            put(5760 + 128 * (3 * dy + dx), part[:, 128 * dy : 128 * dy + 128])

    for i in range(ROWS + 2):
        for dx in range(3):
            at = WIDE * i + 2 - dx
            hx[32 * i : 32 * i + 32, 128 * dx : 128 * dx + 128] = gx[at : at + 32, :].astype(BF)
    g1w[...] = jnp.zeros_like(g1w)
    back = [
        jnp.concatenate([cw[384 * dy + 128 * dx : 384 * dy + 128 * dx + 128, :] for dx in range(3)], axis=1)
        for dy in range(3)
    ]
    pre[0:576, :] = dot_t(hx[0:576, :], jnp.concatenate(back, axis=0))
    acc = sum(pre[64 - 32 * dy : 576 - 32 * dy, 128 * dy : 128 * dy + 128] for dy in range(3))
    g1 = (acc * sg1[...]).astype(BF)
    for dy in range(3):
        g1w[32 * dy : 32 * dy + 512, 128 * dy : 128 * dy + 128] = g1
    for dx in range(3):
        part = t_dot(xc[:, 128 * dx : 128 * dx + 128], g1w[...])
        for dy in range(3):
            put(4608 + 128 * (3 * dy + dx), part[:, 128 * dy : 128 * dy + 128])
    for dx in range(3):
        for side in range(2):
            at = 384 + 512 * dx + 256 * side
            part = t_dot(g1w[...], xc[:, at : at + 256]).astype(BF)
            for dy in range(3):
                at = 2304 * side + 256 * (3 * dy + dx)
                put(at, part[128 * dy : 128 * dy + 128, :].T)


def pair_kernel(both, got, out):
    keep = both.at[0]
    out[...] = (keep[...].astype(F32) + got[...].astype(F32)).astype(BF)
    sl = slice(STAT, STAT + 16)
    rows = keep[sl, :].astype(F32) + got[sl, :].astype(F32)
    out[sl, :] = stat_rows(jnp.sum(rows, axis=0, keepdims=True), (16, C)).astype(BF)


def spread_kernel(pieces, out, mine):
    acc = pieces[0].astype(F32)
    for i in range(1, PEERS):
        acc += pieces[i].astype(F32)
    mine[...] = acc.astype(BF)
    at = STAT % SHARD

    place = [lax.axis_index(a) for a in PLANE]
    owner = 16 * place[0] + 4 * place[1] + 2 * place[2] + place[3]

    @pl.when(owner == STAT // SHARD)
    def _():
        rows = acc[at : at + 16]
        mine[at : at + 16, :] = stat_rows(jnp.sum(rows, axis=0, keepdims=True), (16, C)).astype(BF)

    for i in range(PEERS):
        out[i] = mine[...]


def finish_kernel(second, part, *refs):
    refs = refs[5:] if second else refs
    if second:
        loss, refs = refs[5], refs[:5] + refs[6:]
    gfine, gctx, gconv, ghid, gbin, vf, vx, vc, vh, vb, sem = refs
    half = lax.axis_index("yh")
    which = lax.axis_index("core")
    which = 1 - which if second else which
    stats = jnp.sum(part[STAT : STAT + 16, :].astype(F32), axis=0, keepdims=True)
    lane = iota((1, C), 1)
    total = jnp.sum(jnp.where(lane == 1, stats, 0.0), axis=1, keepdims=True)
    scale = 1.0 / total
    if second:
        loss[...] = jnp.sum(jnp.where(lane == 0, stats, 0.0), axis=1, keepdims=True) * scale

    def get(row, n):
        at = row % STAT
        return part[at : at + n, :].astype(F32) * scale

    def send(done, view, out):
        c = pltpu.make_async_copy(view, out, sem.at[len(done)])
        c.start()
        done.append(c)

    @pl.when(which == 0)
    def _():
        done = []
        at = pl.multiple_of(half * 2304, 128)
        for n in range(9):
            sl = slice(256 * n, 256 * n + 256)
            vx[sl, :] = part[pl.ds(at + 256 * n, 256), :].astype(F32) * scale
            send(done, vx.at[sl, :], gctx.at[sl, :])
        for n in range(3):
            sl = slice(384 * n, 384 * n + 384)
            vf[sl, :] = get(4608 + 384 * n, 384)
            send(done, vf.at[sl, :], gfine.at[sl, :])
        vc[0:256, :] = get(5760, 256)
        send(done, vc.at[0:256, :], gconv.at[0:256, :])
        for c in done:
            c.wait()

    @pl.when(which == 1)
    def _():
        done = []
        for m in range(8):
            sl = slice(128 * m, 128 * m + 128)
            for n in range(4):
                vb[sl, 128 * n : 128 * n + 128] = get(7936 + 1024 * n + 128 * m, 128)
            send(done, vb.at[sl, :], gbin.at[sl, :])
        for n in range(2):
            sl = slice(256 + 448 * n, 704 + 448 * n)
            vc[sl, :] = get(6016 + 448 * n, 448)
            send(done, vc.at[sl, :], gconv.at[sl, :])
        for m in range(4):
            sl = slice(32 * m, 32 * m + 32)
            for n in range(8):
                vh[sl, 128 * n : 128 * n + 128] = get(6912 + 128 * n + 32 * m, 32)
            send(done, vh.at[sl, :], ghid.at[sl, :])
        for c in done:
            c.wait()


def sds(shape, dtype):
    return jax.ShapeDtypeStruct(shape, dtype)


def edge_cols(fine, ctx):
    return pl.pallas_call(
        edge_cols_kernel,
        out_shape=(sds((32, C), BF),) * 2 + (sds((512, C), BF), sds((64, HALF), BF)),
        in_specs=vmem(2),
        out_specs=tuple(vmem(4)),
        scratch_shapes=[pltpu.VMEM((512, C), F32), pltpu.VMEM((2, 64, C), F32)],
        compiler_params=limit(4),
        cost_estimate=BUSY,
        name="edge_cols",
    )(fine, ctx)


def edge_rows(*args):
    return pl.pallas_call(
        edge_rows_kernel,
        out_shape=sds((CTX + 160, C), BF),
        in_specs=vmem(4),
        out_specs=vmem(1)[0],
        scratch_shapes=[pltpu.VMEM((2 * WIDE, C), F32), pltpu.VMEM((160, C), F32)],
        compiler_params=limit(4),
        cost_estimate=BUSY,
        name="edge_rows",
    )(*args)


def ctx_rows(*args):
    return pl.pallas_call(
        ctx_rows_kernel,
        out_shape=(sds((112, C), BF), sds((112, C), BF)),
        in_specs=vmem(2),
        out_specs=tuple(vmem(2)),
        scratch_shapes=[pltpu.VMEM((176, C), F32)],
        compiler_params=limit(4),
        cost_estimate=BUSY,
        name="ctx_rows",
    )(*args)


def first_conv(*args):
    v = pltpu.VMEM
    edge = sds((48, C), BF)
    return pl.pallas_call(
        first_conv_kernel,
        out_shape=(sds((576, 1920), BF), sds((512, C), BF), sds((512, C), F32), edge, edge, sds((64, C), BF)),
        in_specs=vmem(len(args)),
        out_specs=tuple(vmem(6)),
        scratch_shapes=[
            v((18 * WIDE, C), F32),
            v((288, K), BF),
            v((160, K), BF),
            v((512, C), F32),
            v((512, C), F32),
            v((16, C), F32),
            v((16, C), F32),
            v((176, C), F32),
            v((576, 384), F32),
            pltpu.SMEM((4,), jnp.int32),
        ],
        compiler_params=limit(20),
        cost_estimate=pl.CostEstimate(flops=900_000_000, bytes_accessed=5_000_000, transcendentals=0),
        name="first_conv",
    )(*args)


def h_rows(*args):
    edge = sds((144, C), BF)
    return pl.pallas_call(
        h_rows_kernel,
        out_shape=(sds((ROWS * WIDE, C), BF), edge, edge),
        in_specs=vmem(len(args)),
        out_specs=tuple(vmem(3)),
        scratch_shapes=[pltpu.VMEM((ROWS * WIDE, C), F32), pltpu.VMEM((2 * WIDE, C), F32)],
        compiler_params=limit(6),
        cost_estimate=BUSY,
        name="h_rows",
    )(*args)


def rest(*args):
    v = pltpu.VMEM
    return pl.pallas_call(
        rest_kernel,
        out_shape=sds((2, KEEP, C), BF),
        in_specs=vmem(len(args)),
        out_specs=vmem(1)[0],
        scratch_shapes=[
            v((1000, C), F32),
            v((992, 384), BF),
            v((EXT, C), F32),
            v((EXT, C), BF),
            v((SLOTS, C), BF),
            v((SLOTS, HID), BF),
            v((SLOTS, HID), F32),
            v((SLOTS, BINS), BF),
            v((SLOTS, HID), BF),
            v((SLOTS, 256), BF),
            v((EXT + 8, C), F32),
            v((960, 384), BF),
            v((576, 384), BF),
            v((992, 384), F32),
            pltpu.SMEM((4,), jnp.int32),
        ],
        compiler_params=limit(28),
        cost_estimate=pl.CostEstimate(flops=3_000_000_000, bytes_accessed=8_000_000, transcendentals=0),
        name="rest",
    )(*args)


def pair_sum(keep, got):
    return pl.pallas_call(
        pair_kernel,
        out_shape=sds((KEEP, C), BF),
        in_specs=vmem(2),
        out_specs=vmem(1)[0],
        compiler_params=limit(8),
        name="pair_sum",
    )(keep, got)


def spread(pieces):
    return pl.pallas_call(
        spread_kernel,
        out_shape=sds((PEERS, SHARD, C), BF),
        in_specs=vmem(1),
        out_specs=vmem(1)[0],
        scratch_shapes=[pltpu.VMEM((SHARD, C), BF)],
        compiler_params=limit(8),
        name="spread",
    )(pieces)


def finish(part, before=None):
    v = pltpu.VMEM
    shapes = [(1152, C), (2304, C), (1152, C), (C, HID), (HID, BINS)]
    second = before is not None
    more = tuple(before) if second else ()
    return pl.pallas_call(
        functools.partial(finish_kernel, second),
        out_shape=tuple(sds(s, F32) for s in shapes) + (sds((1, 1), F32),) * second,
        in_specs=vmem(1) + [ANY] * len(more),
        out_specs=(ANY,) * 5 + tuple(vmem(1)) * second,
        input_output_aliases={1 + n: n for n in range(len(more))},
        scratch_shapes=[v(s, F32) for s in shapes] + [pltpu.SemaphoreType.DMA((14,))],
        compiler_params=limit(16),
        cost_estimate=pl.CostEstimate(flops=800_000, bytes_accessed=5_000_000, transcendentals=0),
        name="finish_other" if second else "finish_own",
    )(part, *more)


def ring_cells():
    cells = [(0, c) for c in range(34)] + [(17, c) for c in range(34)]
    cells += [(r, 0) for r in range(1, 17)] + [(r, 33) for r in range(1, 17)]
    return np.array([WIDE * r + c for r, c in cells] + [-1] * 28, np.int32)


def local(
    fine,
    context,
    interp_rows,
    interp_cols,
    fine_weight,
    ctx_weight,
    conv_weight,
    hidden_weight,
    bin_weight,
    cell_index,
    counts,
    labels,
):
    idx = cell_index.reshape(1, CAP)
    live = jnp.arange(CAP, dtype=jnp.int32)[None, :] < counts
    lab = jnp.where(live, labels.reshape(1, CAP), -1)
    ring = jnp.asarray(ring_cells())

    last, first, fine, context = edge_cols(fine.reshape(512, C), context.reshape(64, HALF))
    west = shift(last, GX, 8, 1)
    east = shift(first, GX, 8, -1)
    mine = edge_rows(fine, context, west, east)
    inner = side_swap(mine)
    down, up = ctx_rows(mine, inner)
    north = shift(down, GY, 8, 1)
    south = shift(up, GY, 8, -1)
    xc, h_one, sg1, last, first, digs = first_conv(
        interp_rows.T, interp_cols.T, fine, west, east, mine, inner, north, south,
        fine_weight.reshape(1152, C), ctx_weight.reshape(4608, C), idx, lab,
    )

    west = shift(last, GX, 8, 1)
    east = shift(first, GX, 8, -1)
    wide, inner, outer = h_rows(h_one, digs, west, east)
    outer = outer_swap(outer)
    inner = side_swap(inner)
    both = rest(
        wide, inner, outer, west, east, xc, sg1, idx, ring[None, :], lab,
        conv_weight.reshape(1152, C), hidden_weight, bin_weight,
    )

    flip = [(0, 1), (1, 0)]
    pair = pair_sum(both, lax.ppermute(both[1], "core", flip))
    pieces = lax.all_to_all(pair.reshape(PEERS, SHARD, C), PLANE, 0, 0, tiled=True)
    half_sum = lax.all_to_all(spread(pieces), PLANE, 0, 0, tiled=True).reshape(KEEP, C)
    other = lax.ppermute(half_sum, "core", flip)
    outs = finish(half_sum)
    gfine, gctx, gconv, ghid, gbin, loss = finish(other, outs)
    return (
        loss.reshape(()),
        gfine.reshape(3, 3, C, C),
        gctx.reshape(3, 3, HALF, C),
        gconv.reshape(3, 3, C, C),
        ghid,
        gbin,
    )


def solution(mesh):
    devices = np.asarray(mesh.devices).reshape(4, 2, 4, 2, 2)
    split = Mesh(devices, ("x", "core", "z", "yl", "yh"))
    in_specs = (
        P(TALL, GX, None),
        P(GY, GX, "yh"),
        P(),
        P(),
        P(),
        P(),
        P(),
        P(),
        P(),
        P(TALL, GX, None),
        P(TALL, GX),
        P(TALL, GX, None),
    )
    out_specs = (P(), P(), P(None, None, "yh", None), P(), P(), P())
    return jax.shard_map(local, mesh=split, in_specs=in_specs, out_specs=out_specs, check_vma=False)
```

```python
import functools

import jax
import jax.numpy as jnp
import numpy as np
from jax import lax
from jax.experimental import pallas as pl
from jax.experimental.pallas import tpu as pltpu
from jax.sharding import Mesh
from jax.sharding import PartitionSpec as P

HID = 1024
BINS = 512
CAP = 256
ROWS = 16
COLS = 32
C = 128
K = 512
HALF = 256
SHARD = 96
PEERS = 64
BODY = 12032

GY = ("x", "core")
GX = ("z", "yl")
TALL = ("x", "core", "yh")
PLANE = ("x", "z", "yl", "yh")

BF = jnp.bfloat16
F32 = jnp.float32


def shift(x, axis, count, step):
    pairs = [(i, i + step) for i in range(count) if 0 <= i + step < count]
    return lax.ppermute(x, axis, pairs)


def side_swap(x):
    own = [(2 * t + c, 2 * t + 1 - c) for t in range(8) for c in range(2)]
    return lax.ppermute(x, TALL, own)


def outer_swap(x):
    pairs = []
    for t in range(7):
        pairs += [(2 * t + 1, 2 * t + 2), (2 * t + 2, 2 * t + 1)]
    return lax.ppermute(x, TALL, pairs)


WIDE = 48
CTX = 2 * WIDE
EXT = 896
SLOTS = 384
KEEP = PEERS * SHARD
STAT = BODY // 2
MIB = 1024 * 1024
BUSY = pl.CostEstimate(flops=5_000_000_000, bytes_accessed=1_000_000, transcendentals=0)


def limit(mib):
    return pltpu.CompilerParams(vmem_limit_bytes=mib * MIB)


def vmem(n):
    return [pl.BlockSpec(memory_space=pltpu.VMEM)] * n


ANY = pl.BlockSpec(memory_space=pl.ANY)


def dot(a, b):
    return jnp.dot(a, b, preferred_element_type=F32)


def dot_t(a, b):
    return lax.dot_general(a, b, (((1,), (1,)), ((), ())), preferred_element_type=F32)


def t_dot(a, b):
    return lax.dot_general(a, b, (((0,), (0,)), ((), ())), preferred_element_type=F32)


def iota(shape, dim):
    return lax.broadcasted_iota(jnp.int32, shape, dim)


def split3(v):
    hi = v.astype(BF)
    rest = v - hi.astype(F32)
    mid = rest.astype(BF)
    low = (rest - mid.astype(F32)).astype(BF)
    return [hi.astype(F32), mid.astype(F32), low.astype(F32)]


def stat_rows(v, like):
    hi, mid, low = split3(v)
    row = iota(like, 0)
    out = jnp.where(row == 0, hi, jnp.where(row == 1, mid, jnp.where(row == 2, low, 0.0)))
    return out


def edge_cols_kernel(fine_in, ctx_in, last, first, fine, ctx, fs, xs):
    fine[...] = fine_in[...]
    ctx[...] = ctx_in[...]
    fs[...] = fine[...].astype(F32)
    for side in range(2):
        xs[side] = ctx[:, 128 * side : 128 * side + 128].astype(F32)
    for out, fc, xc in ((last, COLS - 1, 7), (first, 0, 0)):
        out[0:16, :] = fs[pl.ds(fc, 16, stride=COLS), :].astype(BF)
        sides = [xs.at[side][pl.ds(xc, 8, stride=8), :] for side in range(2)]
        out[16:32, :] = jnp.concatenate(sides, axis=0).astype(BF)


def edge_rows_kernel(fine, ctx, west, east, inner, rows, xs):
    rows[...] = jnp.zeros_like(rows)
    w, e = west[...].astype(F32), east[...].astype(F32)
    for n, r in ((0, 0), (1, ROWS - 1)):
        at = WIDE * n
        rows[at + 1 : at + 33, :] = fine[COLS * r : COLS * r + COLS, :].astype(F32)
        rows[at : at + 1, :] = w[r : r + 1, :]
        rows[at + 33 : at + 34, :] = e[r : r + 1, :]
    inner[0:CTX, :] = rows[...].astype(BF)
    for side in range(2):
        base = 80 * side
        lanes = slice(128 * side, 128 * side + 128)
        for a in range(8):
            at = base + 10 * a
            xs[at + 1 : at + 9, :] = ctx[8 * a : 8 * a + 8, lanes].astype(F32)
        xs[pl.ds(base, 8, stride=10), :] = w[16 + 8 * side : 24 + 8 * side, :]
        xs[pl.ds(base + 9, 8, stride=10), :] = e[16 + 8 * side : 24 + 8 * side, :]
    inner[CTX:, :] = xs[...].astype(BF)


def ctx_rows_kernel(mine, inner, down, up, xs):
    lower = lax.axis_index("yh") == 1
    xs[160:, :] = jnp.zeros((16, C), F32)
    for n, got in enumerate((mine, inner)):
        xs[0:160, :] = got[CTX:, :].astype(F32)
        for side in range(2):
            at, to = 80 * side, 32 * n + 16 * side
            up[to : to + 16, :] = xs[at : at + 16, :].astype(BF)
            down[to : to + 16, :] = xs[at + 70 : at + 86, :].astype(BF)
    up[64:112, :] = jnp.where(lower, inner[0:WIDE, :], mine[0:WIDE, :])
    down[64:112, :] = jnp.where(lower, mine[WIDE:CTX, :], inner[WIDE:CTX, :])


def column(row):
    n = row.shape[1]
    eye = iota((n, n), 0) == iota((n, n), 1)
    return jnp.sum(jnp.where(eye, row.astype(F32), 0.0), axis=1, keepdims=True)


def plan_kernel(rows_in, cols_in, idx_l, ring_l, lab_l, after, kron, left, digs, pick, back, labs, rmat, cmat):
    half = lax.axis_index("yh")
    row0 = (2 * lax.axis_index("x") + lax.axis_index("core")) * 32
    col0 = (2 * lax.axis_index("z") + lax.axis_index("yl")) * COLS
    rmat[...] = jnp.zeros_like(rmat)
    cmat[...] = jnp.zeros_like(cmat)
    grow = row0 + iota((10, 34), 1) - 1
    gcol = col0 + iota((10, 34), 1) - 1
    rmat[0:10, 0:34] = jnp.where((grow >= 0) & (grow < 256), rows_in[...].astype(F32), 0.0)
    cmat[0:10, 0:34] = jnp.where((gcol >= 0) & (gcol < 256), cols_in[...].astype(F32), 0.0)
    chosen = (iota((288, C), 0) >> 4) + 16 * half == iota((288, C), 1)
    side = dot_t(chosen.astype(F32).astype(BF), rmat[...].astype(BF)).astype(BF)
    spread = (iota((16, 160), 0) == iota((16, 160), 1) >> 4).astype(F32).astype(BF)
    full = dot(side, spread)
    same = (iota((288, 160), 0) & 15) == (iota((288, 160), 1) & 15)
    kron[...] = jnp.where(same, full, 0.0).astype(BF)
    cell = iota((96, C), 0)
    chosen = (cell & 31) + (cell >> 5) == iota((96, C), 1)
    left[...] = dot_t(chosen.astype(F32).astype(BF), cmat[...].astype(BF)).astype(BF)
    code = lab_l[...] + 1
    kind = iota((C, CAP), 0)
    digit = jnp.where(kind == 0, code >> 5, jnp.where(kind == 1, code & 31, 0))
    named = (idx_l[...] == iota((512, CAP), 0)).astype(F32).astype(BF)
    digs[...] = dot_t(named, digit.astype(F32).astype(BF)).astype(BF)
    slot_l = idx_l[...] + 16 * (idx_l[...] >> 5) + WIDE + 1
    slot_s = column(slot_l).astype(jnp.int32)
    ring_s = column(ring_l[...]).astype(jnp.int32)
    pick[0:CAP, :] = (slot_s == iota((CAP, EXT), 1)).astype(F32).astype(BF)
    pick[CAP:, :] = (ring_s == iota((SLOTS - CAP, EXT), 1)).astype(F32).astype(BF)
    cell = iota((EXT, CAP), 0)
    back[:, 0:CAP] = (slot_l == cell).astype(F32).astype(BF)
    back[:, CAP:] = (ring_l[...] == cell[:, :128]).astype(F32).astype(BF)
    labs[...] = column(lab_l[...]).astype(jnp.int32)


def first_conv_kernel(
    kron, left, dig, fine, west, east, mine, inner, north, south, w_fine, w_ctx,
    xc, h1, sg, last, first, digs,
    fscr, mid, block, hscr, dscr, xs, pre, spot,
):
    spot[0] = lax.axis_index("yh")
    half = spot[0]
    lower = half == 1
    for i in range(ROWS):
        at = WIDE * (i + 1) + 1
        fscr[at : at + 32, :] = fine[32 * i : 32 * i + 32, :].astype(F32)
    fscr[pl.ds(WIDE, 16, stride=WIDE), :] = west[0:16, :].astype(F32)
    fscr[pl.ds(WIDE + 33, 16, stride=WIDE), :] = east[0:16, :].astype(F32)
    above = jnp.where(lower, inner[WIDE:CTX, :], north[64:112, :])
    below = jnp.where(lower, south[64:112, :], inner[0:WIDE, :])
    fscr[0:WIDE, :] = above.astype(F32)
    fscr[17 * WIDE : 18 * WIDE, :] = below.astype(F32)
    for i in range(ROWS + 2):
        for dx in range(3):
            at = WIDE * i + dx
            xc[32 * i : 32 * i + 32, 128 * dx : 128 * dx + 128] = fscr[at : at + 32, :].astype(BF)
    xs[160:, :] = jnp.zeros((16, C), F32)
    for n, part, got in ((0, half, mine), (32, 1 - half, inner)):
        xs[0:160, :] = got[CTX:, :].astype(F32)
        for side in range(2):
            lanes = pl.ds(pl.multiple_of(256 * part + 128 * side, 128), 128)
            sl = slice(n + 16 * side, n + 16 * side + 16)
            block[0:16, lanes] = north[sl, :]
            for a in range(8):
                at = 80 * side + 10 * a
                block[16 + 16 * a : 32 + 16 * a, lanes] = xs[at : at + 16, :].astype(BF)
            block[144:160, lanes] = south[sl, :]
    mid[...] = dot(kron[...], block[...]).astype(BF)
    for i in range(ROWS + 2):
        wide = dot(left[...], mid[16 * i : 16 * i + 16, :]).astype(BF)
        for dx in range(3):
            xc[32 * i : 32 * i + 32, 384 + 512 * dx : 896 + 512 * dx] = wide[32 * dx : 32 * dx + 32]
    wf = jnp.concatenate([w_fine[384 * dy : 384 * dy + 384, :] for dy in range(3)], axis=1)
    wc = jnp.concatenate([w_ctx[1536 * dy : 1536 * dy + 1536, :] for dy in range(3)], axis=1)
    pre[...] = dot(xc[:, :384], wf) + dot(xc[:, 384:], wc)
    acc = sum(pre[32 * dy : 32 * dy + 512, 128 * dy : 128 * dy + 128] for dy in range(3))
    s = jax.nn.sigmoid(acc)
    h = (acc * s).astype(BF)
    h1[...] = h
    hscr[...] = h.astype(F32)
    sg[...] = s * (1.0 + acc * (1.0 - s))
    dscr[...] = dig[...].astype(F32)
    digs[0:32, :] = dscr[0:32, :].astype(BF)
    digs[32:64, :] = dscr[480:512, :].astype(BF)
    for out, c0, c1, cd in ((last, COLS - 2, COLS - 1, COLS - 1), (first, 0, 1, 0)):
        out[0:16, :] = hscr[pl.ds(c0, 16, stride=COLS), :].astype(BF)
        out[16:32, :] = hscr[pl.ds(c1, 16, stride=COLS), :].astype(BF)
        out[32:48, :] = dscr[pl.ds(cd, 16, stride=COLS), :].astype(BF)


def h_rows_kernel(h1, digs, west, east, wide, inner, outer, ws, ds):
    lower = lax.axis_index("yh") == 1
    w, e = west[...].astype(F32), east[...].astype(F32)
    ws[...] = jnp.zeros_like(ws)
    ds[...] = jnp.zeros_like(ds)
    for i in range(ROWS):
        ws[WIDE * i + 2 : WIDE * i + 34, :] = h1[32 * i : 32 * i + 32, :].astype(F32)
    for col, value in ((0, w[0:16]), (1, w[16:32]), (34, e[0:16]), (35, e[16:32])):
        ws[pl.ds(col, 16, stride=WIDE), :] = value
    for n, r in ((0, 0), (1, ROWS - 1)):
        at = WIDE * n
        ds[at + 1 : at + 33, :] = digs[32 * n : 32 * n + 32, :].astype(F32)
        ds[at : at + 1, :] = w[32 + r : 33 + r, :]
        ds[at + 33 : at + 34, :] = e[32 + r : 33 + r, :]
    wide[...] = ws[...].astype(BF)
    top, bottom = ws[0:96, :].astype(BF), ws[14 * WIDE : 16 * WIDE, :].astype(BF)
    inner[0:96, :] = jnp.where(lower, top, bottom)
    outer[0:96, :] = jnp.where(lower, bottom, top)
    top, bottom = ds[0:WIDE, :].astype(BF), ds[WIDE : 2 * WIDE, :].astype(BF)
    inner[96:144, :] = jnp.where(lower, top, bottom)
    outer[96:144, :] = jnp.where(lower, bottom, top)


def rest_kernel(
    hw, inner, outer, west, east, xc, sg1, pick, back, labs_s, cw, hid, binw,
    out,
    hp, hx, sg2, h2, rows_s, act, sgz, dl, dz, gscr, gx, g2w, g1w, pre, spot,
):
    spot[0] = lax.axis_index("core")
    spot[1] = lax.axis_index("yh")
    core, lower = spot[0], spot[1] == 1
    a, b = inner[...].astype(F32), outer[...].astype(F32)
    before, after = jnp.where(lower, a, b), jnp.where(lower, b, a)
    hp[0:96, :] = before[0:96]
    hp[96:864, :] = hw[...].astype(F32)
    hp[864:960, :] = after[0:96]
    hp[960:1000, :] = jnp.zeros((40, C), F32)
    gx[...] = jnp.zeros_like(gx)
    gx[0:WIDE, :] = before[96:144]
    gx[17 * WIDE : 18 * WIDE, :] = after[96:144]
    gx[pl.ds(WIDE, 16, stride=WIDE), :] = west[32:48, :].astype(F32)
    gx[pl.ds(WIDE + 33, 16, stride=WIDE), :] = east[32:48, :].astype(F32)
    code = dot(pick[CAP:, :], gx[0:EXT, :].astype(BF))
    lane = iota((128, C), 1)
    code = jnp.sum(jnp.where(lane == 0, 32.0 * code, jnp.where(lane == 1, code, 0.0)), axis=1, keepdims=True)
    for dx in range(3):
        hx[:, 128 * dx : 128 * dx + 128] = hp[dx : dx + 992, :].astype(BF)
    forth = jnp.concatenate([cw[384 * dy : 384 * dy + 384, :] for dy in range(3)], axis=1)
    pre[...] = dot(hx[...], forth)
    acc = sum(pre[WIDE * dy : WIDE * dy + EXT, 128 * dy : 128 * dy + 128] for dy in range(3))
    s = jax.nn.sigmoid(acc)
    h2[...] = (acc * s).astype(BF)
    sg2[...] = s * (1.0 + acc * (1.0 - s))
    rows = dot(pick[...], h2[...]).astype(BF)
    rows_s[...] = rows
    z = dot(rows, hid[...])
    s = jax.nn.sigmoid(z)
    act[...] = (z * s).astype(BF)
    sgz[...] = s * (1.0 + z * (1.0 - s))
    logits = dot(act[...], binw[...])
    peak = jnp.max(logits, axis=1, keepdims=True)
    top = peak + jnp.log(jnp.sum(jnp.exp(logits - peak), axis=1, keepdims=True))
    labs = jnp.concatenate([labs_s[...], code.astype(jnp.int32) - 1], axis=0)
    hit = labs == iota((SLOTS, BINS), 1)
    live = (labs >= 0).astype(F32)
    picked = jnp.sum(jnp.where(hit, logits, 0.0), axis=1, keepdims=True)
    loss = jnp.sum((live * (top - picked))[:CAP])
    dl[...] = ((jnp.exp(logits - top) - hit.astype(F32)) * live).astype(BF)
    dz[...] = (dot_t(dl[...], binw[...]) * sgz[...]).astype(BF)
    drows = dot_t(dz[...], hid[...])
    hi = drows.astype(BF)
    gscr[:, 0:128] = hi
    gscr[:, 128:256] = (drows - hi.astype(F32)).astype(BF)

    def put(row, value):
        out[(row // STAT) ^ core, pl.ds(row % STAT, value.shape[0]), :] = value.astype(BF)

    for n in range(4):
        put(7936 + 1024 * n, t_dot(act[0:CAP, :], dl[0:CAP, 128 * n : 128 * n + 128]))
    ghid = t_dot(rows_s[0:CAP, :], dz[0:CAP, :])
    for n in range(8):
        put(6912 + 128 * n, ghid[:, 128 * n : 128 * n + 128])
    lane = iota((1, C), 1)
    stats = jnp.where(lane == 0, loss, jnp.where(lane == 1, jnp.sum(live[:CAP]), 0.0))
    for n in range(2):
        out[n, STAT : STAT + 16, :] = stat_rows(stats, (16, C)).astype(BF)
        out[n, STAT + 16 : KEEP, :] = jnp.zeros((KEEP - STAT - 16, C), BF)
    both = dot(back[...], gscr[...])
    gx[0:EXT, :] = (both[:, :128] + both[:, 128:]) * sg2[...]

    g2w[...] = jnp.zeros_like(g2w)
    col = iota((WIDE, C), 0)
    inside = jnp.where((col >= 1) & (col <= COLS), 1.0, 0.0)
    own = (gx[WIDE : WIDE + 768, :] * jnp.concatenate([inside] * ROWS, axis=0)).astype(BF)
    for dy in range(3):
        g2w[WIDE * (1 + dy) : WIDE * (1 + dy) + 768, 128 * dy : 128 * dy + 128] = own
    for dx in range(3):
        part = t_dot(hx[0:960, 128 * dx : 128 * dx + 128], g2w[...])
        for dy in range(3):
            put(5760 + 128 * (3 * dy + dx), part[:, 128 * dy : 128 * dy + 128])

    for i in range(ROWS + 2):
        for dx in range(3):
            at = WIDE * i + 2 - dx
            hx[32 * i : 32 * i + 32, 128 * dx : 128 * dx + 128] = gx[at : at + 32, :].astype(BF)
    g1w[...] = jnp.zeros_like(g1w)
    flipped = [
        jnp.concatenate([cw[384 * dy + 128 * dx : 384 * dy + 128 * dx + 128, :] for dx in range(3)], axis=1)
        for dy in range(3)
    ]
    pre[0:576, :] = dot_t(hx[0:576, :], jnp.concatenate(flipped, axis=0))
    acc = sum(pre[64 - 32 * dy : 576 - 32 * dy, 128 * dy : 128 * dy + 128] for dy in range(3))
    g1 = (acc * sg1[...]).astype(BF)
    for dy in range(3):
        g1w[32 * dy : 32 * dy + 512, 128 * dy : 128 * dy + 128] = g1
    for dx in range(3):
        part = t_dot(xc[:, 128 * dx : 128 * dx + 128], g1w[...])
        for dy in range(3):
            put(4608 + 128 * (3 * dy + dx), part[:, 128 * dy : 128 * dy + 128])
    for dx in range(3):
        for side in range(2):
            at = 384 + 512 * dx + 256 * side
            part = t_dot(g1w[...], xc[:, at : at + 256]).astype(BF)
            for dy in range(3):
                at = 2304 * side + 256 * (3 * dy + dx)
                put(at, part[128 * dy : 128 * dy + 128, :].T)


def pair_kernel(both, got, out):
    keep = both.at[0]
    out[...] = (keep[...].astype(F32) + got[...].astype(F32)).astype(BF)
    sl = slice(STAT, STAT + 16)
    rows = keep[sl, :].astype(F32) + got[sl, :].astype(F32)
    out[sl, :] = stat_rows(jnp.sum(rows, axis=0, keepdims=True), (16, C)).astype(BF)


def spread_kernel(pieces, out, mine):
    acc = pieces[0].astype(F32)
    for i in range(1, PEERS):
        acc += pieces[i].astype(F32)
    mine[...] = acc.astype(BF)
    at = STAT % SHARD

    place = [lax.axis_index(a) for a in PLANE]
    owner = 16 * place[0] + 4 * place[1] + 2 * place[2] + place[3]

    @pl.when(owner == STAT // SHARD)
    def _():
        rows = acc[at : at + 16]
        mine[at : at + 16, :] = stat_rows(jnp.sum(rows, axis=0, keepdims=True), (16, C)).astype(BF)

    for i in range(PEERS):
        out[i] = mine[...]


def finish_kernel(second, part, *refs):
    refs = refs[5:] if second else refs
    if second:
        loss, refs = refs[5], refs[:5] + refs[6:]
    gfine, gctx, gconv, ghid, gbin, vf, vx, vc, vh, vb, sem = refs
    half = lax.axis_index("yh")
    which = lax.axis_index("core")
    which = 1 - which if second else which
    stats = jnp.sum(part[STAT : STAT + 16, :].astype(F32), axis=0, keepdims=True)
    lane = iota((1, C), 1)
    total = jnp.sum(jnp.where(lane == 1, stats, 0.0), axis=1, keepdims=True)
    scale = 1.0 / total
    if second:
        loss[...] = jnp.sum(jnp.where(lane == 0, stats, 0.0), axis=1, keepdims=True) * scale

    def get(row, n):
        at = row % STAT
        return part[at : at + n, :].astype(F32) * scale

    def send(done, view, out):
        c = pltpu.make_async_copy(view, out, sem.at[len(done)])
        c.start()
        done.append(c)

    @pl.when(which == 0)
    def _():
        done = []
        at = pl.multiple_of(half * 2304, 128)
        for n in range(9):
            sl = slice(256 * n, 256 * n + 256)
            vx[sl, :] = part[pl.ds(at + 256 * n, 256), :].astype(F32) * scale
            send(done, vx.at[sl, :], gctx.at[sl, :])
        for n in range(3):
            sl = slice(384 * n, 384 * n + 384)
            vf[sl, :] = get(4608 + 384 * n, 384)
            send(done, vf.at[sl, :], gfine.at[sl, :])
        vc[0:256, :] = get(5760, 256)
        send(done, vc.at[0:256, :], gconv.at[0:256, :])
        for c in done:
            c.wait()

    @pl.when(which == 1)
    def _():
        done = []
        for m in range(8):
            sl = slice(128 * m, 128 * m + 128)
            for n in range(4):
                vb[sl, 128 * n : 128 * n + 128] = get(7936 + 1024 * n + 128 * m, 128)
            send(done, vb.at[sl, :], gbin.at[sl, :])
        for n in range(2):
            sl = slice(256 + 448 * n, 704 + 448 * n)
            vc[sl, :] = get(6016 + 448 * n, 448)
            send(done, vc.at[sl, :], gconv.at[sl, :])
        for m in range(4):
            sl = slice(32 * m, 32 * m + 32)
            for n in range(8):
                vh[sl, 128 * n : 128 * n + 128] = get(6912 + 128 * n + 32 * m, 32)
            send(done, vh.at[sl, :], ghid.at[sl, :])
        for c in done:
            c.wait()


def sds(shape, dtype):
    return jax.ShapeDtypeStruct(shape, dtype)


def edge_cols(fine, ctx):
    return pl.pallas_call(
        edge_cols_kernel,
        out_shape=(sds((32, C), BF),) * 2 + (sds((512, C), BF), sds((64, HALF), BF)),
        in_specs=vmem(2),
        out_specs=tuple(vmem(4)),
        scratch_shapes=[pltpu.VMEM((512, C), F32), pltpu.VMEM((2, 64, C), F32)],
        compiler_params=limit(4),
        cost_estimate=BUSY,
        name="edge_cols",
    )(fine, ctx)


def edge_rows(*args):
    return pl.pallas_call(
        edge_rows_kernel,
        out_shape=sds((CTX + 160, C), BF),
        in_specs=vmem(4),
        out_specs=vmem(1)[0],
        scratch_shapes=[pltpu.VMEM((2 * WIDE, C), F32), pltpu.VMEM((160, C), F32)],
        compiler_params=limit(4),
        cost_estimate=BUSY,
        name="edge_rows",
    )(*args)


def ctx_rows(*args):
    return pl.pallas_call(
        ctx_rows_kernel,
        out_shape=(sds((112, C), BF), sds((112, C), BF)),
        in_specs=vmem(2),
        out_specs=tuple(vmem(2)),
        scratch_shapes=[pltpu.VMEM((176, C), F32)],
        compiler_params=limit(4),
        cost_estimate=BUSY,
        name="ctx_rows",
    )(*args)


def plan(*args):
    shapes = [((288, 160), BF), ((96, 16), BF), ((512, C), BF), ((SLOTS, EXT), BF), ((EXT, SLOTS), BF)]
    return pl.pallas_call(
        plan_kernel,
        out_shape=tuple(sds(*s) for s in shapes) + (sds((CAP, 1), jnp.int32),),
        in_specs=vmem(len(args)),
        out_specs=tuple(vmem(6)),
        scratch_shapes=[pltpu.VMEM((16, C), F32), pltpu.VMEM((16, C), F32)],
        compiler_params=limit(8),
        cost_estimate=BUSY,
        name="plan",
    )(*args)


def first_conv(*args):
    v = pltpu.VMEM
    edge = sds((48, C), BF)
    return pl.pallas_call(
        first_conv_kernel,
        out_shape=(sds((576, 1920), BF), sds((512, C), BF), sds((512, C), F32), edge, edge, sds((64, C), BF)),
        in_specs=vmem(len(args)),
        out_specs=tuple(vmem(6)),
        scratch_shapes=[
            v((18 * WIDE, C), F32),
            v((288, K), BF),
            v((160, K), BF),
            v((512, C), F32),
            v((512, C), F32),
            v((176, C), F32),
            v((576, 384), F32),
            pltpu.SMEM((4,), jnp.int32),
        ],
        compiler_params=limit(20),
        cost_estimate=pl.CostEstimate(flops=900_000_000, bytes_accessed=5_000_000, transcendentals=0),
        name="first_conv",
    )(*args)


def h_rows(*args):
    edge = sds((144, C), BF)
    return pl.pallas_call(
        h_rows_kernel,
        out_shape=(sds((ROWS * WIDE, C), BF), edge, edge),
        in_specs=vmem(len(args)),
        out_specs=tuple(vmem(3)),
        scratch_shapes=[pltpu.VMEM((ROWS * WIDE, C), F32), pltpu.VMEM((2 * WIDE, C), F32)],
        compiler_params=limit(6),
        cost_estimate=BUSY,
        name="h_rows",
    )(*args)


def rest(*args):
    v = pltpu.VMEM
    return pl.pallas_call(
        rest_kernel,
        out_shape=sds((2, KEEP, C), BF),
        in_specs=vmem(len(args)),
        out_specs=vmem(1)[0],
        scratch_shapes=[
            v((1000, C), F32),
            v((992, 384), BF),
            v((EXT, C), F32),
            v((EXT, C), BF),
            v((SLOTS, C), BF),
            v((SLOTS, HID), BF),
            v((SLOTS, HID), F32),
            v((SLOTS, BINS), BF),
            v((SLOTS, HID), BF),
            v((SLOTS, 256), BF),
            v((EXT + 8, C), F32),
            v((960, 384), BF),
            v((576, 384), BF),
            v((992, 384), F32),
            pltpu.SMEM((4,), jnp.int32),
        ],
        compiler_params=limit(28),
        cost_estimate=pl.CostEstimate(flops=3_000_000_000, bytes_accessed=8_000_000, transcendentals=0),
        name="rest",
    )(*args)


def pair_sum(keep, got):
    return pl.pallas_call(
        pair_kernel,
        out_shape=sds((KEEP, C), BF),
        in_specs=vmem(2),
        out_specs=vmem(1)[0],
        compiler_params=limit(8),
        name="pair_sum",
    )(keep, got)


def spread(pieces):
    return pl.pallas_call(
        spread_kernel,
        out_shape=sds((PEERS, SHARD, C), BF),
        in_specs=vmem(1),
        out_specs=vmem(1)[0],
        scratch_shapes=[pltpu.VMEM((SHARD, C), BF)],
        compiler_params=limit(8),
        name="spread",
    )(pieces)


def finish(part, before=None):
    v = pltpu.VMEM
    shapes = [(1152, C), (2304, C), (1152, C), (C, HID), (HID, BINS)]
    second = before is not None
    more = tuple(before) if second else ()
    return pl.pallas_call(
        functools.partial(finish_kernel, second),
        out_shape=tuple(sds(s, F32) for s in shapes) + (sds((1, 1), F32),) * second,
        in_specs=vmem(1) + [ANY] * len(more),
        out_specs=(ANY,) * 5 + tuple(vmem(1)) * second,
        input_output_aliases={1 + n: n for n in range(len(more))},
        scratch_shapes=[v(s, F32) for s in shapes] + [pltpu.SemaphoreType.DMA((14,))],
        compiler_params=limit(16),
        cost_estimate=pl.CostEstimate(flops=800_000, bytes_accessed=5_000_000, transcendentals=0),
        name="finish_other" if second else "finish_own",
    )(part, *more)


def ring_cells():
    cells = [(0, c) for c in range(34)] + [(17, c) for c in range(34)]
    cells += [(r, 0) for r in range(1, 17)] + [(r, 33) for r in range(1, 17)]
    return np.array([WIDE * r + c for r, c in cells] + [-1] * 28, np.int32)


def local(
    fine,
    context,
    interp_rows,
    interp_cols,
    fine_weight,
    ctx_weight,
    conv_weight,
    hidden_weight,
    bin_weight,
    cell_index,
    counts,
    labels,
):
    idx = cell_index.reshape(1, CAP)
    live = jnp.arange(CAP, dtype=jnp.int32)[None, :] < counts
    lab = jnp.where(live, labels.reshape(1, CAP), -1)
    ring = jnp.asarray(ring_cells())

    last, first, fine, context = edge_cols(fine.reshape(512, C), context.reshape(64, HALF))
    west = shift(last, GX, 8, 1)
    east = shift(first, GX, 8, -1)
    kron, left, dig, pick, back, labs = plan(interp_rows.T, interp_cols.T, idx, ring[None, :], lab, last)
    mine = edge_rows(fine, context, west, east)
    inner = side_swap(mine)
    down, up = ctx_rows(mine, inner)
    north = shift(down, GY, 8, 1)
    south = shift(up, GY, 8, -1)
    xc, h_one, sg1, last, first, digs = first_conv(
        kron, left, dig, fine, west, east, mine, inner, north, south,
        fine_weight.reshape(1152, C), ctx_weight.reshape(4608, C),
    )

    west = shift(last, GX, 8, 1)
    east = shift(first, GX, 8, -1)
    wide, inner, outer = h_rows(h_one, digs, west, east)
    outer = outer_swap(outer)
    inner = side_swap(inner)
    both = rest(
        wide, inner, outer, west, east, xc, sg1, pick, back, labs,
        conv_weight.reshape(1152, C), hidden_weight, bin_weight,
    )

    flip = [(0, 1), (1, 0)]
    pair = pair_sum(both, lax.ppermute(both[1], "core", flip))
    pieces = lax.all_to_all(pair.reshape(PEERS, SHARD, C), PLANE, 0, 0, tiled=True)
    half_sum = lax.all_to_all(spread(pieces), PLANE, 0, 0, tiled=True).reshape(KEEP, C)
    other = lax.ppermute(half_sum, "core", flip)
    outs = finish(half_sum)
    gfine, gctx, gconv, ghid, gbin, loss = finish(other, outs)
    return (
        loss.reshape(()),
        gfine.reshape(3, 3, C, C),
        gctx.reshape(3, 3, HALF, C),
        gconv.reshape(3, 3, C, C),
        ghid,
        gbin,
    )


def solution(mesh):
    devices = np.asarray(mesh.devices).reshape(4, 2, 4, 2, 2)
    split = Mesh(devices, ("x", "core", "z", "yl", "yh"))
    in_specs = (
        P(TALL, GX, None),
        P(GY, GX, "yh"),
        P(),
        P(),
        P(),
        P(),
        P(),
        P(),
        P(),
        P(TALL, GX, None),
        P(TALL, GX),
        P(TALL, GX, None),
    )
    out_specs = (P(), P(), P(None, None, "yh", None), P(), P(), P())
    return jax.shard_map(local, mesh=split, in_specs=in_specs, out_specs=out_specs, check_vma=False)
```

```python
import functools

import jax
import jax.numpy as jnp
import numpy as np
from jax import lax
from jax.experimental import pallas as pl
from jax.experimental.pallas import tpu as pltpu
from jax.sharding import Mesh
from jax.sharding import PartitionSpec as P

HID = 1024
BINS = 512
CAP = 256
ROWS = 16
COLS = 32
C = 128
K = 512
HALF = 256
SHARD = 96
PEERS = 64
BODY = 12032

GY = ("x", "core")
GX = ("z", "yl")
TALL = ("x", "core", "yh")
PLANE = ("x", "z", "yl", "yh")

BF = jnp.bfloat16
F32 = jnp.float32


def shift(x, axis, count, step):
    pairs = [(i, i + step) for i in range(count) if 0 <= i + step < count]
    return lax.ppermute(x, axis, pairs)


def side_swap(x):
    own = [(2 * t + c, 2 * t + 1 - c) for t in range(8) for c in range(2)]
    return lax.ppermute(x, TALL, own)


def outer_swap(x):
    pairs = []
    for t in range(7):
        pairs += [(2 * t + 1, 2 * t + 2), (2 * t + 2, 2 * t + 1)]
    return lax.ppermute(x, TALL, pairs)


WIDE = 48
CTX = 2 * WIDE
EXT = 896
SLOTS = 384
KEEP = PEERS * SHARD
STAT = BODY // 2
MIB = 1024 * 1024
BUSY = pl.CostEstimate(flops=5_000_000_000, bytes_accessed=1_000_000, transcendentals=0)


def limit(mib):
    return pltpu.CompilerParams(vmem_limit_bytes=mib * MIB)


def vmem(n):
    return [pl.BlockSpec(memory_space=pltpu.VMEM)] * n


ANY = pl.BlockSpec(memory_space=pl.ANY)


def dot(a, b):
    return jnp.dot(a, b, preferred_element_type=F32)


def dot_t(a, b):
    return lax.dot_general(a, b, (((1,), (1,)), ((), ())), preferred_element_type=F32)


def t_dot(a, b):
    return lax.dot_general(a, b, (((0,), (0,)), ((), ())), preferred_element_type=F32)


def iota(shape, dim):
    return lax.broadcasted_iota(jnp.int32, shape, dim)


def split3(v):
    hi = v.astype(BF)
    rest = v - hi.astype(F32)
    mid = rest.astype(BF)
    low = (rest - mid.astype(F32)).astype(BF)
    return [hi.astype(F32), mid.astype(F32), low.astype(F32)]


def stat_rows(v, like):
    hi, mid, low = split3(v)
    row = iota(like, 0)
    out = jnp.where(row == 0, hi, jnp.where(row == 1, mid, jnp.where(row == 2, low, 0.0)))
    return out


def edge_cols_kernel(fine_in, ctx_in, last, first, fine, ctx, fs, xs):
    fine[...] = fine_in[...]
    ctx[...] = ctx_in[...]
    fs[0:512, :] = fine[...].astype(F32)
    for side in range(2):
        xs[side, 0:64, :] = ctx[:, 128 * side : 128 * side + 128].astype(F32)
    for out, fc, xc in ((last, COLS - 1, 7), (first, 0, 0)):
        out[0:16, :] = fs[pl.ds(fc, 16, stride=COLS), :].astype(BF)
        sides = [xs.at[side][pl.ds(xc, 8, stride=8), :] for side in range(2)]
        out[16:32, :] = jnp.concatenate(sides, axis=0).astype(BF)


def edge_rows_kernel(fine, ctx, west, east, inner, rows, xs):
    rows[...] = jnp.zeros_like(rows)
    w, e = west[...].astype(F32), east[...].astype(F32)
    for n, r in ((0, 0), (1, ROWS - 1)):
        at = WIDE * n
        rows[at + 1 : at + 33, :] = fine[COLS * r : COLS * r + COLS, :].astype(F32)
        rows[at : at + 1, :] = w[r : r + 1, :]
        rows[at + 33 : at + 34, :] = e[r : r + 1, :]
    inner[0:CTX, :] = rows[...].astype(BF)
    for side in range(2):
        base = 80 * side
        lanes = slice(128 * side, 128 * side + 128)
        for a in range(8):
            at = base + 10 * a
            xs[at + 1 : at + 9, :] = ctx[8 * a : 8 * a + 8, lanes].astype(F32)
        xs[pl.ds(base, 8, stride=10), :] = w[16 + 8 * side : 24 + 8 * side, :]
        xs[pl.ds(base + 9, 8, stride=10), :] = e[16 + 8 * side : 24 + 8 * side, :]
    inner[CTX:, :] = xs[0:160, :].astype(BF)


def ctx_rows_kernel(mine, inner, down, up, xs):
    lower = lax.axis_index("yh") == 1
    xs[160:, :] = jnp.zeros((16, C), F32)
    for n, got in enumerate((mine, inner)):
        xs[0:160, :] = got[CTX:, :].astype(F32)
        for side in range(2):
            at, to = 80 * side, 32 * n + 16 * side
            up[to : to + 16, :] = xs[at : at + 16, :].astype(BF)
            down[to : to + 16, :] = xs[at + 70 : at + 86, :].astype(BF)
    up[64:112, :] = jnp.where(lower, inner[0:WIDE, :], mine[0:WIDE, :])
    down[64:112, :] = jnp.where(lower, mine[WIDE:CTX, :], inner[WIDE:CTX, :])


def column(row):
    n = row.shape[1]
    eye = iota((n, n), 0) == iota((n, n), 1)
    return jnp.sum(jnp.where(eye, row.astype(F32), 0.0), axis=1, keepdims=True)


def plan_kernel(rows_in, cols_in, idx_l, ring_l, lab_l, after, kron, left, digs, pick, back, labs, rmat, cmat):
    half = lax.axis_index("yh")
    row0 = (2 * lax.axis_index("x") + lax.axis_index("core")) * 32
    col0 = (2 * lax.axis_index("z") + lax.axis_index("yl")) * COLS
    rmat[...] = jnp.zeros_like(rmat)
    cmat[...] = jnp.zeros_like(cmat)
    grow = row0 + iota((10, 34), 1) - 1
    gcol = col0 + iota((10, 34), 1) - 1
    rmat[0:10, 0:34] = jnp.where((grow >= 0) & (grow < 256), rows_in[...].astype(F32), 0.0)
    cmat[0:10, 0:34] = jnp.where((gcol >= 0) & (gcol < 256), cols_in[...].astype(F32), 0.0)
    chosen = (iota((288, C), 0) >> 4) + 16 * half == iota((288, C), 1)
    side = dot_t(chosen.astype(F32).astype(BF), rmat[...].astype(BF)).astype(BF)
    spread = (iota((16, 160), 0) == iota((16, 160), 1) >> 4).astype(F32).astype(BF)
    full = dot(side, spread)
    same = (iota((288, 160), 0) & 15) == (iota((288, 160), 1) & 15)
    kron[...] = jnp.where(same, full, 0.0).astype(BF)
    cell = iota((96, C), 0)
    chosen = (cell & 31) + (cell >> 5) == iota((96, C), 1)
    left[...] = dot_t(chosen.astype(F32).astype(BF), cmat[...].astype(BF)).astype(BF)
    code = lab_l[...] + 1
    kind = iota((C, CAP), 0)
    digit = jnp.where(kind == 0, code >> 5, jnp.where(kind == 1, code & 31, 0))
    named = (idx_l[...] == iota((512, CAP), 0)).astype(F32).astype(BF)
    digs[...] = dot_t(named, digit.astype(F32).astype(BF)).astype(BF)
    slot_l = idx_l[...] + 16 * (idx_l[...] >> 5) + WIDE + 1
    slot_s = column(slot_l).astype(jnp.int32)
    ring_s = column(ring_l[...]).astype(jnp.int32)
    pick[0:CAP, :] = (slot_s == iota((CAP, EXT), 1)).astype(F32).astype(BF)
    pick[CAP:, :] = (ring_s == iota((SLOTS - CAP, EXT), 1)).astype(F32).astype(BF)
    cell = iota((EXT, CAP), 0)
    back[:, 0:CAP] = (slot_l == cell).astype(F32).astype(BF)
    back[:, CAP:] = (ring_l[...] == cell[:, :128]).astype(F32).astype(BF)
    labs[...] = column(lab_l[...]).astype(jnp.int32)


def first_conv_kernel(
    kron, left, dig, fine, west, east, mine, inner, north, south, w_fine, w_ctx,
    xc, h1, sg, last, first, digs,
    fscr, mid, block, hscr, dscr, xs, pre, spot,
):
    spot[0] = lax.axis_index("yh")
    half = spot[0]
    lower = half == 1
    for i in range(ROWS):
        at = WIDE * (i + 1) + 1
        fscr[at : at + 32, :] = fine[32 * i : 32 * i + 32, :].astype(F32)
    fscr[pl.ds(WIDE, 16, stride=WIDE), :] = west[0:16, :].astype(F32)
    fscr[pl.ds(WIDE + 33, 16, stride=WIDE), :] = east[0:16, :].astype(F32)
    above = jnp.where(lower, inner[WIDE:CTX, :], north[64:112, :])
    below = jnp.where(lower, south[64:112, :], inner[0:WIDE, :])
    fscr[0:WIDE, :] = above.astype(F32)
    fscr[17 * WIDE : 18 * WIDE, :] = below.astype(F32)
    for i in range(ROWS + 2):
        for dx in range(3):
            at = WIDE * i + dx
            xc[32 * i : 32 * i + 32, 128 * dx : 128 * dx + 128] = fscr[at : at + 32, :].astype(BF)
    xs[160:, :] = jnp.zeros((16, C), F32)
    for n, part, got in ((0, half, mine), (32, 1 - half, inner)):
        xs[0:160, :] = got[CTX:, :].astype(F32)
        for side in range(2):
            lanes = pl.ds(pl.multiple_of(256 * part + 128 * side, 128), 128)
            sl = slice(n + 16 * side, n + 16 * side + 16)
            block[0:16, lanes] = north[sl, :]
            for a in range(8):
                at = 80 * side + 10 * a
                block[16 + 16 * a : 32 + 16 * a, lanes] = xs[at : at + 16, :].astype(BF)
            block[144:160, lanes] = south[sl, :]
    mid[...] = dot(kron[...], block[...]).astype(BF)
    for i in range(ROWS + 2):
        wide = dot(left[...], mid[16 * i : 16 * i + 16, :]).astype(BF)
        for dx in range(3):
            xc[32 * i : 32 * i + 32, 384 + 512 * dx : 896 + 512 * dx] = wide[32 * dx : 32 * dx + 32]
    wf = jnp.concatenate([w_fine[384 * dy : 384 * dy + 384, :] for dy in range(3)], axis=1)
    wc = jnp.concatenate([w_ctx[1536 * dy : 1536 * dy + 1536, :] for dy in range(3)], axis=1)
    pre[...] = dot(xc[:, :384], wf) + dot(xc[:, 384:], wc)
    acc = sum(pre[32 * dy : 32 * dy + 512, 128 * dy : 128 * dy + 128] for dy in range(3))
    s = jax.nn.sigmoid(acc)
    h = (acc * s).astype(BF)
    h1[...] = h
    hscr[0:512, :] = h.astype(F32)
    sg[...] = s * (1.0 + acc * (1.0 - s))
    dscr[0:512, :] = dig[...].astype(F32)
    digs[0:32, :] = dscr[0:32, :].astype(BF)
    digs[32:64, :] = dscr[480:512, :].astype(BF)
    for out, c0, c1, cd in ((last, COLS - 2, COLS - 1, COLS - 1), (first, 0, 1, 0)):
        out[0:16, :] = hscr[pl.ds(c0, 16, stride=COLS), :].astype(BF)
        out[16:32, :] = hscr[pl.ds(c1, 16, stride=COLS), :].astype(BF)
        out[32:48, :] = dscr[pl.ds(cd, 16, stride=COLS), :].astype(BF)


def h_rows_kernel(h1, digs, west, east, wide, inner, outer, ws, ds):
    lower = lax.axis_index("yh") == 1
    w, e = west[...].astype(F32), east[...].astype(F32)
    ws[...] = jnp.zeros_like(ws)
    ds[...] = jnp.zeros_like(ds)
    for i in range(ROWS):
        ws[WIDE * i + 2 : WIDE * i + 34, :] = h1[32 * i : 32 * i + 32, :].astype(F32)
    for col, value in ((0, w[0:16]), (1, w[16:32]), (34, e[0:16]), (35, e[16:32])):
        ws[pl.ds(col, 16, stride=WIDE), :] = value
    for n, r in ((0, 0), (1, ROWS - 1)):
        at = WIDE * n
        ds[at + 1 : at + 33, :] = digs[32 * n : 32 * n + 32, :].astype(F32)
        ds[at : at + 1, :] = w[32 + r : 33 + r, :]
        ds[at + 33 : at + 34, :] = e[32 + r : 33 + r, :]
    wide[...] = ws[0 : ROWS * WIDE, :].astype(BF)
    top, bottom = ws[0:96, :].astype(BF), ws[14 * WIDE : 16 * WIDE, :].astype(BF)
    inner[0:96, :] = jnp.where(lower, top, bottom)
    outer[0:96, :] = jnp.where(lower, bottom, top)
    top, bottom = ds[0:WIDE, :].astype(BF), ds[WIDE : 2 * WIDE, :].astype(BF)
    inner[96:144, :] = jnp.where(lower, top, bottom)
    outer[96:144, :] = jnp.where(lower, bottom, top)


def rest_kernel(
    hw, inner, outer, west, east, xc, sg1, pick, back, labs_s, cw, hid, binw,
    out,
    hp, hx, sg2, h2, rows_s, act, sgz, dl, dz, gscr, gx, g2w, g1w, pre, spot,
):
    spot[0] = lax.axis_index("core")
    spot[1] = lax.axis_index("yh")
    core, lower = spot[0], spot[1] == 1
    a, b = inner[...].astype(F32), outer[...].astype(F32)
    before, after = jnp.where(lower, a, b), jnp.where(lower, b, a)
    hp[0:96, :] = before[0:96]
    hp[96:864, :] = hw[...].astype(F32)
    hp[864:960, :] = after[0:96]
    hp[960:1000, :] = jnp.zeros((40, C), F32)
    gx[...] = jnp.zeros_like(gx)
    gx[0:WIDE, :] = before[96:144]
    gx[17 * WIDE : 18 * WIDE, :] = after[96:144]
    gx[pl.ds(WIDE, 16, stride=WIDE), :] = west[32:48, :].astype(F32)
    gx[pl.ds(WIDE + 33, 16, stride=WIDE), :] = east[32:48, :].astype(F32)
    code = dot(pick[CAP:, :], gx[0:EXT, :].astype(BF))
    lane = iota((128, C), 1)
    code = jnp.sum(jnp.where(lane == 0, 32.0 * code, jnp.where(lane == 1, code, 0.0)), axis=1, keepdims=True)
    for dx in range(3):
        hx[:, 128 * dx : 128 * dx + 128] = hp[dx : dx + 992, :].astype(BF)
    forth = jnp.concatenate([cw[384 * dy : 384 * dy + 384, :] for dy in range(3)], axis=1)
    pre[...] = dot(hx[...], forth)
    acc = sum(pre[WIDE * dy : WIDE * dy + EXT, 128 * dy : 128 * dy + 128] for dy in range(3))
    s = jax.nn.sigmoid(acc)
    h2[...] = (acc * s).astype(BF)
    sg2[...] = s * (1.0 + acc * (1.0 - s))
    rows = dot(pick[...], h2[...]).astype(BF)
    rows_s[...] = rows
    z = dot(rows, hid[...])
    s = jax.nn.sigmoid(z)
    act[...] = (z * s).astype(BF)
    sgz[...] = s * (1.0 + z * (1.0 - s))
    logits = dot(act[...], binw[...])
    peak = jnp.max(logits, axis=1, keepdims=True)
    top = peak + jnp.log(jnp.sum(jnp.exp(logits - peak), axis=1, keepdims=True))
    labs = jnp.concatenate([labs_s[...], code.astype(jnp.int32) - 1], axis=0)
    hit = labs == iota((SLOTS, BINS), 1)
    live = (labs >= 0).astype(F32)
    picked = jnp.sum(jnp.where(hit, logits, 0.0), axis=1, keepdims=True)
    loss = jnp.sum((live * (top - picked))[:CAP])
    dl[...] = ((jnp.exp(logits - top) - hit.astype(F32)) * live).astype(BF)
    dz[...] = (dot_t(dl[...], binw[...]) * sgz[...]).astype(BF)
    drows = dot_t(dz[...], hid[...])
    hi = drows.astype(BF)
    gscr[:, 0:128] = hi
    gscr[:, 128:256] = (drows - hi.astype(F32)).astype(BF)

    def put(row, value):
        out[(row // STAT) ^ core, pl.ds(row % STAT, value.shape[0]), :] = value.astype(BF)

    for n in range(4):
        put(7936 + 1024 * n, t_dot(act[0:CAP, :], dl[0:CAP, 128 * n : 128 * n + 128]))
    ghid = t_dot(rows_s[0:CAP, :], dz[0:CAP, :])
    for n in range(8):
        put(6912 + 128 * n, ghid[:, 128 * n : 128 * n + 128])
    lane = iota((1, C), 1)
    stats = jnp.where(lane == 0, loss, jnp.where(lane == 1, jnp.sum(live[:CAP]), 0.0))
    for n in range(2):
        out[n, STAT : STAT + 16, :] = stat_rows(stats, (16, C)).astype(BF)
        out[n, STAT + 16 : KEEP, :] = jnp.zeros((KEEP - STAT - 16, C), BF)
    both = dot(back[...], gscr[...])
    gx[0:EXT, :] = (both[:, :128] + both[:, 128:]) * sg2[...]

    g2w[...] = jnp.zeros_like(g2w)
    col = iota((WIDE, C), 0)
    inside = jnp.where((col >= 1) & (col <= COLS), 1.0, 0.0)
    own = (gx[WIDE : WIDE + 768, :] * jnp.concatenate([inside] * ROWS, axis=0)).astype(BF)
    for dy in range(3):
        g2w[WIDE * (1 + dy) : WIDE * (1 + dy) + 768, 128 * dy : 128 * dy + 128] = own
    for dx in range(3):
        part = t_dot(hx[0:960, 128 * dx : 128 * dx + 128], g2w[...])
        for dy in range(3):
            put(5760 + 128 * (3 * dy + dx), part[:, 128 * dy : 128 * dy + 128])

    for i in range(ROWS + 2):
        for dx in range(3):
            at = WIDE * i + 2 - dx
            hx[32 * i : 32 * i + 32, 128 * dx : 128 * dx + 128] = gx[at : at + 32, :].astype(BF)
    g1w[...] = jnp.zeros_like(g1w)
    flipped = [
        jnp.concatenate([cw[384 * dy + 128 * dx : 384 * dy + 128 * dx + 128, :] for dx in range(3)], axis=1)
        for dy in range(3)
    ]
    pre[0:576, :] = dot_t(hx[0:576, :], jnp.concatenate(flipped, axis=0))
    acc = sum(pre[64 - 32 * dy : 576 - 32 * dy, 128 * dy : 128 * dy + 128] for dy in range(3))
    g1 = (acc * sg1[...]).astype(BF)
    for dy in range(3):
        g1w[32 * dy : 32 * dy + 512, 128 * dy : 128 * dy + 128] = g1
    for dx in range(3):
        part = t_dot(xc[:, 128 * dx : 128 * dx + 128], g1w[...])
        for dy in range(3):
            put(4608 + 128 * (3 * dy + dx), part[:, 128 * dy : 128 * dy + 128])
    for dx in range(3):
        for side in range(2):
            at = 384 + 512 * dx + 256 * side
            part = t_dot(g1w[...], xc[:, at : at + 256]).astype(BF)
            for dy in range(3):
                at = 2304 * side + 256 * (3 * dy + dx)
                put(at, part[128 * dy : 128 * dy + 128, :].T)


def pair_kernel(both, got, out):
    keep = both.at[0]
    out[...] = (keep[...].astype(F32) + got[...].astype(F32)).astype(BF)
    sl = slice(STAT, STAT + 16)
    rows = keep[sl, :].astype(F32) + got[sl, :].astype(F32)
    out[sl, :] = stat_rows(jnp.sum(rows, axis=0, keepdims=True), (16, C)).astype(BF)


def spread_kernel(pieces, out, mine):
    acc = pieces[0].astype(F32)
    for i in range(1, PEERS):
        acc += pieces[i].astype(F32)
    mine[...] = acc.astype(BF)
    at = STAT % SHARD

    place = [lax.axis_index(a) for a in PLANE]
    owner = 16 * place[0] + 4 * place[1] + 2 * place[2] + place[3]

    @pl.when(owner == STAT // SHARD)
    def _():
        rows = acc[at : at + 16]
        mine[at : at + 16, :] = stat_rows(jnp.sum(rows, axis=0, keepdims=True), (16, C)).astype(BF)

    for i in range(PEERS):
        out[i] = mine[...]


def finish_kernel(second, part, *refs):
    refs = refs[5:] if second else refs
    if second:
        loss, refs = refs[5], refs[:5] + refs[6:]
    gfine, gctx, gconv, ghid, gbin, vf, vx, vc, vh, vb, sem = refs
    half = lax.axis_index("yh")
    which = lax.axis_index("core")
    which = 1 - which if second else which
    stats = jnp.sum(part[STAT : STAT + 16, :].astype(F32), axis=0, keepdims=True)
    lane = iota((1, C), 1)
    total = jnp.sum(jnp.where(lane == 1, stats, 0.0), axis=1, keepdims=True)
    scale = 1.0 / total
    if second:
        loss[...] = jnp.sum(jnp.where(lane == 0, stats, 0.0), axis=1, keepdims=True) * scale

    def get(row, n):
        at = row % STAT
        return part[at : at + n, :].astype(F32) * scale

    def send(done, view, out):
        c = pltpu.make_async_copy(view, out, sem.at[len(done)])
        c.start()
        done.append(c)

    @pl.when(which == 0)
    def _():
        done = []
        at = pl.multiple_of(half * 2304, 128)
        for n in range(9):
            sl = slice(256 * n, 256 * n + 256)
            vx[sl, :] = part[pl.ds(at + 256 * n, 256), :].astype(F32) * scale
            send(done, vx.at[sl, :], gctx.at[sl, :])
        for n in range(3):
            sl = slice(384 * n, 384 * n + 384)
            vf[sl, :] = get(4608 + 384 * n, 384)
            send(done, vf.at[sl, :], gfine.at[sl, :])
        vc[0:256, :] = get(5760, 256)
        send(done, vc.at[0:256, :], gconv.at[0:256, :])
        for c in done:
            c.wait()

    @pl.when(which == 1)
    def _():
        done = []
        for m in range(8):
            sl = slice(128 * m, 128 * m + 128)
            for n in range(4):
                vb[sl, 128 * n : 128 * n + 128] = get(7936 + 1024 * n + 128 * m, 128)
            send(done, vb.at[sl, :], gbin.at[sl, :])
        for n in range(2):
            sl = slice(256 + 448 * n, 704 + 448 * n)
            vc[sl, :] = get(6016 + 448 * n, 448)
            send(done, vc.at[sl, :], gconv.at[sl, :])
        for m in range(4):
            sl = slice(32 * m, 32 * m + 32)
            for n in range(8):
                vh[sl, 128 * n : 128 * n + 128] = get(6912 + 128 * n + 32 * m, 32)
            send(done, vh.at[sl, :], ghid.at[sl, :])
        for c in done:
            c.wait()


def sds(shape, dtype):
    return jax.ShapeDtypeStruct(shape, dtype)


def edge_cols(fine, ctx):
    return pl.pallas_call(
        edge_cols_kernel,
        out_shape=(sds((32, C), BF),) * 2 + (sds((512, C), BF), sds((64, HALF), BF)),
        in_specs=vmem(2),
        out_specs=tuple(vmem(4)),
        scratch_shapes=[pltpu.VMEM((544, C), F32), pltpu.VMEM((2, 72, C), F32)],
        compiler_params=limit(4),
        cost_estimate=BUSY,
        name="edge_cols",
    )(fine, ctx)


def edge_rows(*args):
    return pl.pallas_call(
        edge_rows_kernel,
        out_shape=sds((CTX + 160, C), BF),
        in_specs=vmem(4),
        out_specs=vmem(1)[0],
        scratch_shapes=[pltpu.VMEM((2 * WIDE, C), F32), pltpu.VMEM((176, C), F32)],
        compiler_params=limit(4),
        cost_estimate=BUSY,
        name="edge_rows",
    )(*args)


def ctx_rows(*args):
    return pl.pallas_call(
        ctx_rows_kernel,
        out_shape=(sds((112, C), BF), sds((112, C), BF)),
        in_specs=vmem(2),
        out_specs=tuple(vmem(2)),
        scratch_shapes=[pltpu.VMEM((176, C), F32)],
        compiler_params=limit(4),
        cost_estimate=BUSY,
        name="ctx_rows",
    )(*args)


def plan(*args):
    shapes = [((288, 160), BF), ((96, 16), BF), ((512, C), BF), ((SLOTS, EXT), BF), ((EXT, SLOTS), BF)]
    return pl.pallas_call(
        plan_kernel,
        out_shape=tuple(sds(*s) for s in shapes) + (sds((CAP, 1), jnp.int32),),
        in_specs=vmem(len(args)),
        out_specs=tuple(vmem(6)),
        scratch_shapes=[pltpu.VMEM((16, C), F32), pltpu.VMEM((16, C), F32)],
        compiler_params=limit(8),
        cost_estimate=BUSY,
        name="plan",
    )(*args)


def first_conv(*args):
    v = pltpu.VMEM
    edge = sds((48, C), BF)
    return pl.pallas_call(
        first_conv_kernel,
        out_shape=(sds((576, 1920), BF), sds((512, C), BF), sds((512, C), F32), edge, edge, sds((64, C), BF)),
        in_specs=vmem(len(args)),
        out_specs=tuple(vmem(6)),
        scratch_shapes=[
            v((18 * WIDE, C), F32),
            v((288, K), BF),
            v((160, K), BF),
            v((544, C), F32),
            v((544, C), F32),
            v((176, C), F32),
            v((576, 384), F32),
            pltpu.SMEM((4,), jnp.int32),
        ],
        compiler_params=limit(20),
        cost_estimate=pl.CostEstimate(flops=900_000_000, bytes_accessed=5_000_000, transcendentals=0),
        name="first_conv",
    )(*args)


def h_rows(*args):
    edge = sds((144, C), BF)
    return pl.pallas_call(
        h_rows_kernel,
        out_shape=(sds((ROWS * WIDE, C), BF), edge, edge),
        in_specs=vmem(len(args)),
        out_specs=tuple(vmem(3)),
        scratch_shapes=[pltpu.VMEM((ROWS * WIDE + WIDE, C), F32), pltpu.VMEM((2 * WIDE, C), F32)],
        compiler_params=limit(6),
        cost_estimate=BUSY,
        name="h_rows",
    )(*args)


def rest(*args):
    v = pltpu.VMEM
    return pl.pallas_call(
        rest_kernel,
        out_shape=sds((2, KEEP, C), BF),
        in_specs=vmem(len(args)),
        out_specs=vmem(1)[0],
        scratch_shapes=[
            v((1000, C), F32),
            v((992, 384), BF),
            v((EXT, C), F32),
            v((EXT, C), BF),
            v((SLOTS, C), BF),
            v((SLOTS, HID), BF),
            v((SLOTS, HID), F32),
            v((SLOTS, BINS), BF),
            v((SLOTS, HID), BF),
            v((SLOTS, 256), BF),
            v((EXT + 8, C), F32),
            v((960, 384), BF),
            v((576, 384), BF),
            v((992, 384), F32),
            pltpu.SMEM((4,), jnp.int32),
        ],
        compiler_params=limit(28),
        cost_estimate=pl.CostEstimate(flops=3_000_000_000, bytes_accessed=8_000_000, transcendentals=0),
        name="rest",
    )(*args)


def pair_sum(keep, got):
    return pl.pallas_call(
        pair_kernel,
        out_shape=sds((KEEP, C), BF),
        in_specs=vmem(2),
        out_specs=vmem(1)[0],
        compiler_params=limit(8),
        name="pair_sum",
    )(keep, got)


def spread(pieces):
    return pl.pallas_call(
        spread_kernel,
        out_shape=sds((PEERS, SHARD, C), BF),
        in_specs=vmem(1),
        out_specs=vmem(1)[0],
        scratch_shapes=[pltpu.VMEM((SHARD, C), BF)],
        compiler_params=limit(8),
        name="spread",
    )(pieces)


def finish(part, before=None):
    v = pltpu.VMEM
    shapes = [(1152, C), (2304, C), (1152, C), (C, HID), (HID, BINS)]
    second = before is not None
    more = tuple(before) if second else ()
    return pl.pallas_call(
        functools.partial(finish_kernel, second),
        out_shape=tuple(sds(s, F32) for s in shapes) + (sds((1, 1), F32),) * second,
        in_specs=vmem(1) + [ANY] * len(more),
        out_specs=(ANY,) * 5 + tuple(vmem(1)) * second,
        input_output_aliases={1 + n: n for n in range(len(more))},
        scratch_shapes=[v(s, F32) for s in shapes] + [pltpu.SemaphoreType.DMA((14,))],
        compiler_params=limit(16),
        cost_estimate=pl.CostEstimate(flops=800_000, bytes_accessed=5_000_000, transcendentals=0),
        name="finish_other" if second else "finish_own",
    )(part, *more)


def ring_cells():
    cells = [(0, c) for c in range(34)] + [(17, c) for c in range(34)]
    cells += [(r, 0) for r in range(1, 17)] + [(r, 33) for r in range(1, 17)]
    return np.array([WIDE * r + c for r, c in cells] + [-1] * 28, np.int32)


def local(
    fine,
    context,
    interp_rows,
    interp_cols,
    fine_weight,
    ctx_weight,
    conv_weight,
    hidden_weight,
    bin_weight,
    cell_index,
    counts,
    labels,
):
    idx = cell_index.reshape(1, CAP)
    live = jnp.arange(CAP, dtype=jnp.int32)[None, :] < counts
    lab = jnp.where(live, labels.reshape(1, CAP), -1)
    ring = jnp.asarray(ring_cells())

    last, first, fine, context = edge_cols(fine.reshape(512, C), context.reshape(64, HALF))
    east = shift(first, GX, 8, -1)
    west = shift(last, GX, 8, 1)
    kron, left, dig, pick, back, labs = plan(interp_rows.T, interp_cols.T, idx, ring[None, :], lab, last)
    mine = edge_rows(fine, context, west, east)
    inner = side_swap(mine)
    down, up = ctx_rows(mine, inner)
    north = shift(down, GY, 8, 1)
    south = shift(up, GY, 8, -1)
    xc, h_one, sg1, last, first, digs = first_conv(
        kron, left, dig, fine, west, east, mine, inner, north, south,
        fine_weight.reshape(1152, C), ctx_weight.reshape(4608, C),
    )

    east = shift(first, GX, 8, -1)
    west = shift(last, GX, 8, 1)
    wide, inner, outer = h_rows(h_one, digs, west, east)
    outer = outer_swap(outer)
    inner = side_swap(inner)
    both = rest(
        wide, inner, outer, west, east, xc, sg1, pick, back, labs,
        conv_weight.reshape(1152, C), hidden_weight, bin_weight,
    )

    flip = [(0, 1), (1, 0)]
    pair = pair_sum(both, lax.ppermute(both[1], "core", flip))
    pieces = lax.all_to_all(pair.reshape(PEERS, SHARD, C), PLANE, 0, 0, tiled=True)
    half_sum = lax.all_to_all(spread(pieces), PLANE, 0, 0, tiled=True).reshape(KEEP, C)
    other = lax.ppermute(half_sum, "core", flip)
    outs = finish(half_sum)
    gfine, gctx, gconv, ghid, gbin, loss = finish(other, outs)
    return (
        loss.reshape(()),
        gfine.reshape(3, 3, C, C),
        gctx.reshape(3, 3, HALF, C),
        gconv.reshape(3, 3, C, C),
        ghid,
        gbin,
    )


def solution(mesh):
    devices = np.asarray(mesh.devices).reshape(4, 2, 4, 2, 2)
    split = Mesh(devices, ("x", "core", "z", "yl", "yh"))
    in_specs = (
        P(TALL, GX, None),
        P(GY, GX, "yh"),
        P(),
        P(),
        P(),
        P(),
        P(),
        P(),
        P(),
        P(TALL, GX, None),
        P(TALL, GX),
        P(TALL, GX, None),
    )
    out_specs = (P(), P(), P(None, None, "yh", None), P(), P(), P())
    return jax.shard_map(local, mesh=split, in_specs=in_specs, out_specs=out_specs, check_vma=False)
```

```python
import functools

import jax
import jax.numpy as jnp
import numpy as np
from jax import lax
from jax.experimental import pallas as pl
from jax.experimental.pallas import tpu as pltpu
from jax.sharding import Mesh
from jax.sharding import PartitionSpec as P

HID = 1024
BINS = 512
CAP = 256
ROWS = 16
COLS = 32
C = 128
K = 512
HALF = 256
SHARD = 96
PEERS = 64
BODY = 12032

GY = ("x", "core")
GX = ("z", "yl")
TALL = ("x", "core", "yh")
PLANE = ("x", "z", "yl", "yh")

BF = jnp.bfloat16
F32 = jnp.float32


def shift(x, axis, count, step):
    pairs = [(i, i + step) for i in range(count) if 0 <= i + step < count]
    return lax.ppermute(x, axis, pairs)


def side_swap(x):
    own = [(2 * t + c, 2 * t + 1 - c) for t in range(8) for c in range(2)]
    return lax.ppermute(x, TALL, own)


def outer_swap(x):
    pairs = []
    for t in range(7):
        pairs += [(2 * t + 1, 2 * t + 2), (2 * t + 2, 2 * t + 1)]
    return lax.ppermute(x, TALL, pairs)


WIDE = 48
CTX = 2 * WIDE
EXT = 896
SLOTS = 384
KEEP = PEERS * SHARD
STAT = BODY // 2
MIB = 1024 * 1024
BUSY = pl.CostEstimate(flops=5_000_000_000, bytes_accessed=1_000_000, transcendentals=0)


def limit(mib):
    return pltpu.CompilerParams(vmem_limit_bytes=mib * MIB)


def vmem(n):
    return [pl.BlockSpec(memory_space=pltpu.VMEM)] * n


ANY = pl.BlockSpec(memory_space=pl.ANY)


def dot(a, b):
    return jnp.dot(a, b, preferred_element_type=F32)


def dot_t(a, b):
    return lax.dot_general(a, b, (((1,), (1,)), ((), ())), preferred_element_type=F32)


def t_dot(a, b):
    return lax.dot_general(a, b, (((0,), (0,)), ((), ())), preferred_element_type=F32)


def iota(shape, dim):
    return lax.broadcasted_iota(jnp.int32, shape, dim)


def split3(v):
    hi = v.astype(BF)
    rest = v - hi.astype(F32)
    mid = rest.astype(BF)
    low = (rest - mid.astype(F32)).astype(BF)
    return [hi.astype(F32), mid.astype(F32), low.astype(F32)]


def stat_rows(v, like):
    hi, mid, low = split3(v)
    row = iota(like, 0)
    out = jnp.where(row == 0, hi, jnp.where(row == 1, mid, jnp.where(row == 2, low, 0.0)))
    return out


def edge_cols_kernel(fine_in, ctx_in, last, first, fine, ctx, fs, xs):
    fine[...] = fine_in[...]
    ctx[...] = ctx_in[...]
    fs[0:512, :] = fine[...].astype(F32)
    for side in range(2):
        xs[side, 0:64, :] = ctx[:, 128 * side : 128 * side + 128].astype(F32)
    for out, fc, xc in ((last, COLS - 1, 7), (first, 0, 0)):
        out[0:16, :] = fs[pl.ds(fc, 16, stride=COLS), :].astype(BF)
        sides = [xs.at[side][pl.ds(xc, 8, stride=8), :] for side in range(2)]
        out[16:32, :] = jnp.concatenate(sides, axis=0).astype(BF)


def edge_rows_kernel(fine, ctx, west, east, inner, rows, xs):
    rows[...] = jnp.zeros_like(rows)
    w, e = west[...].astype(F32), east[...].astype(F32)
    for n, r in ((0, 0), (1, ROWS - 1)):
        at = WIDE * n
        rows[at + 1 : at + 33, :] = fine[COLS * r : COLS * r + COLS, :].astype(F32)
        rows[at : at + 1, :] = w[r : r + 1, :]
        rows[at + 33 : at + 34, :] = e[r : r + 1, :]
    inner[0:CTX, :] = rows[...].astype(BF)
    for side in range(2):
        base = 80 * side
        lanes = slice(128 * side, 128 * side + 128)
        for a in range(8):
            at = base + 10 * a
            xs[at + 1 : at + 9, :] = ctx[8 * a : 8 * a + 8, lanes].astype(F32)
        xs[pl.ds(base, 8, stride=10), :] = w[16 + 8 * side : 24 + 8 * side, :]
        xs[pl.ds(base + 9, 8, stride=10), :] = e[16 + 8 * side : 24 + 8 * side, :]
    inner[CTX:, :] = xs[0:160, :].astype(BF)


def ctx_rows_kernel(mine, inner, down, up, xs):
    lower = lax.axis_index("yh") == 1
    xs[160:, :] = jnp.zeros((16, C), F32)
    for n, got in enumerate((mine, inner)):
        xs[0:160, :] = got[CTX:, :].astype(F32)
        for side in range(2):
            at, to = 80 * side, 32 * n + 16 * side
            up[to : to + 16, :] = xs[at : at + 16, :].astype(BF)
            down[to : to + 16, :] = xs[at + 70 : at + 86, :].astype(BF)
    up[64:112, :] = jnp.where(lower, inner[0:WIDE, :], mine[0:WIDE, :])
    down[64:112, :] = jnp.where(lower, mine[WIDE:CTX, :], inner[WIDE:CTX, :])


def column(row):
    n = row.shape[1]
    eye = iota((n, n), 0) == iota((n, n), 1)
    return jnp.sum(jnp.where(eye, row.astype(F32), 0.0), axis=1, keepdims=True)


def plan_kernel(
    rows_in, cols_in, idx_l, ring_l, lab_l, w_fine, w_ctx, after, kron, left, digs, pick, back, labs, wide, rmat, cmat
):
    half = lax.axis_index("yh")
    row0 = (2 * lax.axis_index("x") + lax.axis_index("core")) * 32
    col0 = (2 * lax.axis_index("z") + lax.axis_index("yl")) * COLS
    rmat[...] = jnp.zeros_like(rmat)
    cmat[...] = jnp.zeros_like(cmat)
    grow = row0 + iota((10, 34), 1) - 1
    gcol = col0 + iota((10, 34), 1) - 1
    rmat[0:10, 0:34] = jnp.where((grow >= 0) & (grow < 256), rows_in[...].astype(F32), 0.0)
    cmat[0:10, 0:34] = jnp.where((gcol >= 0) & (gcol < 256), cols_in[...].astype(F32), 0.0)
    chosen = (iota((288, C), 0) >> 4) + 16 * half == iota((288, C), 1)
    side = dot_t(chosen.astype(F32).astype(BF), rmat[...].astype(BF)).astype(BF)
    spread = (iota((16, 160), 0) == iota((16, 160), 1) >> 4).astype(F32).astype(BF)
    full = dot(side, spread)
    same = (iota((288, 160), 0) & 15) == (iota((288, 160), 1) & 15)
    kron[...] = jnp.where(same, full, 0.0).astype(BF)
    cell = iota((96, C), 0)
    chosen = (cell & 31) + (cell >> 5) == iota((96, C), 1)
    left[...] = dot_t(chosen.astype(F32).astype(BF), cmat[...].astype(BF)).astype(BF)
    code = lab_l[...] + 1
    kind = iota((C, CAP), 0)
    digit = jnp.where(kind == 0, code >> 5, jnp.where(kind == 1, code & 31, 0))
    named = (idx_l[...] == iota((512, CAP), 0)).astype(F32).astype(BF)
    digs[...] = dot_t(named, digit.astype(F32).astype(BF)).astype(BF)
    slot_l = idx_l[...] + 16 * (idx_l[...] >> 5) + WIDE + 1
    slot_s = column(slot_l).astype(jnp.int32)
    ring_s = column(ring_l[...]).astype(jnp.int32)
    pick[0:CAP, :] = (slot_s == iota((CAP, EXT), 1)).astype(F32).astype(BF)
    pick[CAP:, :] = (ring_s == iota((SLOTS - CAP, EXT), 1)).astype(F32).astype(BF)
    cell = iota((EXT, CAP), 0)
    back[:, 0:CAP] = (slot_l == cell).astype(F32).astype(BF)
    back[:, CAP:] = (ring_l[...] == cell[:, :128]).astype(F32).astype(BF)
    labs[...] = column(lab_l[...]).astype(jnp.int32)
    for dy in range(3):
        lanes = slice(128 * dy, 128 * dy + 128)
        wide[0:384, lanes] = w_fine[384 * dy : 384 * dy + 384, :]
        wide[384:, lanes] = w_ctx[1536 * dy : 1536 * dy + 1536, :]


def first_conv_kernel(
    kron, left, dig, fine, west, east, mine, inner, north, south, weights,
    xc, h1, sg, last, first, digs,
    fscr, mid, block, hscr, dscr, xs, pre, spot,
):
    spot[0] = lax.axis_index("yh")
    half = spot[0]
    lower = half == 1
    for i in range(ROWS):
        at = WIDE * (i + 1) + 1
        fscr[at : at + 32, :] = fine[32 * i : 32 * i + 32, :].astype(F32)
    fscr[pl.ds(WIDE, 16, stride=WIDE), :] = west[0:16, :].astype(F32)
    fscr[pl.ds(WIDE + 33, 16, stride=WIDE), :] = east[0:16, :].astype(F32)
    above = jnp.where(lower, inner[WIDE:CTX, :], north[64:112, :])
    below = jnp.where(lower, south[64:112, :], inner[0:WIDE, :])
    fscr[0:WIDE, :] = above.astype(F32)
    fscr[17 * WIDE : 18 * WIDE, :] = below.astype(F32)
    for i in range(ROWS + 2):
        for dx in range(3):
            at = WIDE * i + dx
            xc[32 * i : 32 * i + 32, 128 * dx : 128 * dx + 128] = fscr[at : at + 32, :].astype(BF)
    xs[160:, :] = jnp.zeros((16, C), F32)
    for n, part, got in ((0, half, mine), (32, 1 - half, inner)):
        xs[0:160, :] = got[CTX:, :].astype(F32)
        for side in range(2):
            lanes = pl.ds(pl.multiple_of(256 * part + 128 * side, 128), 128)
            sl = slice(n + 16 * side, n + 16 * side + 16)
            block[0:16, lanes] = north[sl, :]
            for a in range(8):
                at = 80 * side + 10 * a
                block[16 + 16 * a : 32 + 16 * a, lanes] = xs[at : at + 16, :].astype(BF)
            block[144:160, lanes] = south[sl, :]
    mid[...] = dot(kron[...], block[...]).astype(BF)
    for i in range(ROWS + 2):
        wide = dot(left[...], mid[16 * i : 16 * i + 16, :]).astype(BF)
        for dx in range(3):
            xc[32 * i : 32 * i + 32, 384 + 512 * dx : 896 + 512 * dx] = wide[32 * dx : 32 * dx + 32]
    pre[...] = dot(xc[...], weights[...])
    acc = sum(pre[32 * dy : 32 * dy + 512, 128 * dy : 128 * dy + 128] for dy in range(3))
    s = jax.nn.sigmoid(acc)
    h = (acc * s).astype(BF)
    h1[...] = h
    hscr[0:512, :] = h.astype(F32)
    sg[...] = s * (1.0 + acc * (1.0 - s))
    dscr[0:512, :] = dig[...].astype(F32)
    digs[0:32, :] = dscr[0:32, :].astype(BF)
    digs[32:64, :] = dscr[480:512, :].astype(BF)
    for out, c0, c1, cd in ((last, COLS - 2, COLS - 1, COLS - 1), (first, 0, 1, 0)):
        out[0:16, :] = hscr[pl.ds(c0, 16, stride=COLS), :].astype(BF)
        out[16:32, :] = hscr[pl.ds(c1, 16, stride=COLS), :].astype(BF)
        out[32:48, :] = dscr[pl.ds(cd, 16, stride=COLS), :].astype(BF)


def h_rows_kernel(h1, digs, west, east, wide, inner, outer, ws, ds):
    lower = lax.axis_index("yh") == 1
    w, e = west[...].astype(F32), east[...].astype(F32)
    ws[...] = jnp.zeros_like(ws)
    ds[...] = jnp.zeros_like(ds)
    for i in range(ROWS):
        ws[WIDE * i + 2 : WIDE * i + 34, :] = h1[32 * i : 32 * i + 32, :].astype(F32)
    for col, value in ((0, w[0:16]), (1, w[16:32]), (34, e[0:16]), (35, e[16:32])):
        ws[pl.ds(col, 16, stride=WIDE), :] = value
    for n, r in ((0, 0), (1, ROWS - 1)):
        at = WIDE * n
        ds[at + 1 : at + 33, :] = digs[32 * n : 32 * n + 32, :].astype(F32)
        ds[at : at + 1, :] = w[32 + r : 33 + r, :]
        ds[at + 33 : at + 34, :] = e[32 + r : 33 + r, :]
    wide[...] = ws[0 : ROWS * WIDE, :].astype(BF)
    top, bottom = ws[0:96, :].astype(BF), ws[14 * WIDE : 16 * WIDE, :].astype(BF)
    inner[0:96, :] = jnp.where(lower, top, bottom)
    outer[0:96, :] = jnp.where(lower, bottom, top)
    top, bottom = ds[0:WIDE, :].astype(BF), ds[WIDE : 2 * WIDE, :].astype(BF)
    inner[96:144, :] = jnp.where(lower, top, bottom)
    outer[96:144, :] = jnp.where(lower, bottom, top)


def rest_kernel(
    hw, inner, outer, west, east, xc, sg1, pick, back, labs_s, cw, hid, binw,
    out,
    hp, hx, sg2, h2, rows_s, act, sgz, dl, dz, gscr, gx, g2w, g1w, pre, spot,
):
    spot[0] = lax.axis_index("core")
    spot[1] = lax.axis_index("yh")
    core, lower = spot[0], spot[1] == 1
    a, b = inner[...].astype(F32), outer[...].astype(F32)
    before, after = jnp.where(lower, a, b), jnp.where(lower, b, a)
    hp[0:96, :] = before[0:96]
    hp[96:864, :] = hw[...].astype(F32)
    hp[864:960, :] = after[0:96]
    hp[960:1000, :] = jnp.zeros((40, C), F32)
    gx[...] = jnp.zeros_like(gx)
    gx[0:WIDE, :] = before[96:144]
    gx[17 * WIDE : 18 * WIDE, :] = after[96:144]
    gx[pl.ds(WIDE, 16, stride=WIDE), :] = west[32:48, :].astype(F32)
    gx[pl.ds(WIDE + 33, 16, stride=WIDE), :] = east[32:48, :].astype(F32)
    code = dot(pick[CAP:, :], gx[0:EXT, :].astype(BF))
    lane = iota((128, C), 1)
    code = jnp.sum(jnp.where(lane == 0, 32.0 * code, jnp.where(lane == 1, code, 0.0)), axis=1, keepdims=True)
    for dx in range(3):
        hx[:, 128 * dx : 128 * dx + 128] = hp[dx : dx + 992, :].astype(BF)
    forth = jnp.concatenate([cw[384 * dy : 384 * dy + 384, :] for dy in range(3)], axis=1)
    pre[...] = dot(hx[...], forth)
    acc = sum(pre[WIDE * dy : WIDE * dy + EXT, 128 * dy : 128 * dy + 128] for dy in range(3))
    s = jax.nn.sigmoid(acc)
    h2[...] = (acc * s).astype(BF)
    sg2[...] = s * (1.0 + acc * (1.0 - s))
    rows = dot(pick[...], h2[...]).astype(BF)
    rows_s[...] = rows
    z = dot(rows, hid[...])
    s = jax.nn.sigmoid(z)
    act[...] = (z * s).astype(BF)
    sgz[...] = s * (1.0 + z * (1.0 - s))
    logits = dot(act[...], binw[...])
    peak = jnp.max(logits, axis=1, keepdims=True)
    top = peak + jnp.log(jnp.sum(jnp.exp(logits - peak), axis=1, keepdims=True))
    labs = jnp.concatenate([labs_s[...], code.astype(jnp.int32) - 1], axis=0)
    hit = labs == iota((SLOTS, BINS), 1)
    live = (labs >= 0).astype(F32)
    picked = jnp.sum(jnp.where(hit, logits, 0.0), axis=1, keepdims=True)
    loss = jnp.sum((live * (top - picked))[:CAP])
    dl[...] = ((jnp.exp(logits - top) - hit.astype(F32)) * live).astype(BF)
    dz[...] = (dot_t(dl[...], binw[...]) * sgz[...]).astype(BF)
    drows = dot_t(dz[...], hid[...])
    hi = drows.astype(BF)
    gscr[:, 0:128] = hi
    gscr[:, 128:256] = (drows - hi.astype(F32)).astype(BF)

    def put(row, value):
        out[(row // STAT) ^ core, pl.ds(row % STAT, value.shape[0]), :] = value.astype(BF)

    for n in range(4):
        put(7936 + 1024 * n, t_dot(act[0:CAP, :], dl[0:CAP, 128 * n : 128 * n + 128]))
    ghid = t_dot(rows_s[0:CAP, :], dz[0:CAP, :])
    for n in range(8):
        put(6912 + 128 * n, ghid[:, 128 * n : 128 * n + 128])
    lane = iota((1, C), 1)
    stats = jnp.where(lane == 0, loss, jnp.where(lane == 1, jnp.sum(live[:CAP]), 0.0))
    for n in range(2):
        out[n, STAT : STAT + 16, :] = stat_rows(stats, (16, C)).astype(BF)
        out[n, STAT + 16 : KEEP, :] = jnp.zeros((KEEP - STAT - 16, C), BF)
    both = dot(back[...], gscr[...])
    gx[0:EXT, :] = (both[:, :128] + both[:, 128:]) * sg2[...]

    g2w[...] = jnp.zeros_like(g2w)
    col = iota((WIDE, C), 0)
    inside = jnp.where((col >= 1) & (col <= COLS), 1.0, 0.0)
    own = (gx[WIDE : WIDE + 768, :] * jnp.concatenate([inside] * ROWS, axis=0)).astype(BF)
    for dy in range(3):
        g2w[WIDE * (1 + dy) : WIDE * (1 + dy) + 768, 128 * dy : 128 * dy + 128] = own
    for dx in range(3):
        part = t_dot(hx[0:960, 128 * dx : 128 * dx + 128], g2w[...])
        for dy in range(3):
            put(5760 + 128 * (3 * dy + dx), part[:, 128 * dy : 128 * dy + 128])

    for i in range(ROWS + 2):
        for dx in range(3):
            at = WIDE * i + 2 - dx
            hx[32 * i : 32 * i + 32, 128 * dx : 128 * dx + 128] = gx[at : at + 32, :].astype(BF)
    g1w[...] = jnp.zeros_like(g1w)
    flipped = [
        jnp.concatenate([cw[384 * dy + 128 * dx : 384 * dy + 128 * dx + 128, :] for dx in range(3)], axis=1)
        for dy in range(3)
    ]
    pre[0:576, :] = dot_t(hx[0:576, :], jnp.concatenate(flipped, axis=0))
    acc = sum(pre[64 - 32 * dy : 576 - 32 * dy, 128 * dy : 128 * dy + 128] for dy in range(3))
    g1 = (acc * sg1[...]).astype(BF)
    for dy in range(3):
        g1w[32 * dy : 32 * dy + 512, 128 * dy : 128 * dy + 128] = g1
    for dx in range(3):
        part = t_dot(xc[:, 128 * dx : 128 * dx + 128], g1w[...])
        for dy in range(3):
            put(4608 + 128 * (3 * dy + dx), part[:, 128 * dy : 128 * dy + 128])
    for dx in range(3):
        for side in range(2):
            at = 384 + 512 * dx + 256 * side
            part = t_dot(g1w[...], xc[:, at : at + 256]).astype(BF)
            for dy in range(3):
                at = 2304 * side + 256 * (3 * dy + dx)
                put(at, part[128 * dy : 128 * dy + 128, :].T)


def pair_kernel(both, got, out):
    keep = both.at[0]
    out[...] = (keep[...].astype(F32) + got[...].astype(F32)).astype(BF)
    sl = slice(STAT, STAT + 16)
    rows = keep[sl, :].astype(F32) + got[sl, :].astype(F32)
    out[sl, :] = stat_rows(jnp.sum(rows, axis=0, keepdims=True), (16, C)).astype(BF)


def spread_kernel(pieces, out, mine):
    acc = pieces[0].astype(F32)
    for i in range(1, PEERS):
        acc += pieces[i].astype(F32)
    mine[...] = acc.astype(BF)
    at = STAT % SHARD

    place = [lax.axis_index(a) for a in PLANE]
    owner = 16 * place[0] + 4 * place[1] + 2 * place[2] + place[3]

    @pl.when(owner == STAT // SHARD)
    def _():
        rows = acc[at : at + 16]
        mine[at : at + 16, :] = stat_rows(jnp.sum(rows, axis=0, keepdims=True), (16, C)).astype(BF)

    for i in range(PEERS):
        out[i] = mine[...]


def finish_kernel(second, part, *refs):
    refs = refs[5:] if second else refs
    if second:
        loss, refs = refs[5], refs[:5] + refs[6:]
    gfine, gctx, gconv, ghid, gbin, vf, vx, vc, vh, vb, sem = refs
    half = lax.axis_index("yh")
    which = lax.axis_index("core")
    which = 1 - which if second else which
    stats = jnp.sum(part[STAT : STAT + 16, :].astype(F32), axis=0, keepdims=True)
    lane = iota((1, C), 1)
    total = jnp.sum(jnp.where(lane == 1, stats, 0.0), axis=1, keepdims=True)
    scale = 1.0 / total
    if second:
        loss[...] = jnp.sum(jnp.where(lane == 0, stats, 0.0), axis=1, keepdims=True) * scale

    def get(row, n):
        at = row % STAT
        return part[at : at + n, :].astype(F32) * scale

    def send(done, view, out):
        c = pltpu.make_async_copy(view, out, sem.at[len(done)])
        c.start()
        done.append(c)

    @pl.when(which == 0)
    def _():
        done = []
        at = pl.multiple_of(half * 2304, 128)
        for n in range(9):
            sl = slice(256 * n, 256 * n + 256)
            vx[sl, :] = part[pl.ds(at + 256 * n, 256), :].astype(F32) * scale
            send(done, vx.at[sl, :], gctx.at[sl, :])
        for n in range(3):
            sl = slice(384 * n, 384 * n + 384)
            vf[sl, :] = get(4608 + 384 * n, 384)
            send(done, vf.at[sl, :], gfine.at[sl, :])
        vc[0:256, :] = get(5760, 256)
        send(done, vc.at[0:256, :], gconv.at[0:256, :])
        for c in done:
            c.wait()

    @pl.when(which == 1)
    def _():
        done = []
        for m in range(8):
            sl = slice(128 * m, 128 * m + 128)
            for n in range(4):
                vb[sl, 128 * n : 128 * n + 128] = get(7936 + 1024 * n + 128 * m, 128)
            send(done, vb.at[sl, :], gbin.at[sl, :])
        for n in range(2):
            sl = slice(256 + 448 * n, 704 + 448 * n)
            vc[sl, :] = get(6016 + 448 * n, 448)
            send(done, vc.at[sl, :], gconv.at[sl, :])
        for m in range(4):
            sl = slice(32 * m, 32 * m + 32)
            for n in range(8):
                vh[sl, 128 * n : 128 * n + 128] = get(6912 + 128 * n + 32 * m, 32)
            send(done, vh.at[sl, :], ghid.at[sl, :])
        for c in done:
            c.wait()


def sds(shape, dtype):
    return jax.ShapeDtypeStruct(shape, dtype)


def edge_cols(fine, ctx):
    return pl.pallas_call(
        edge_cols_kernel,
        out_shape=(sds((32, C), BF),) * 2 + (sds((512, C), BF), sds((64, HALF), BF)),
        in_specs=vmem(2),
        out_specs=tuple(vmem(4)),
        scratch_shapes=[pltpu.VMEM((544, C), F32), pltpu.VMEM((2, 72, C), F32)],
        compiler_params=limit(4),
        cost_estimate=BUSY,
        name="edge_cols",
    )(fine, ctx)


def edge_rows(*args):
    return pl.pallas_call(
        edge_rows_kernel,
        out_shape=sds((CTX + 160, C), BF),
        in_specs=vmem(4),
        out_specs=vmem(1)[0],
        scratch_shapes=[pltpu.VMEM((2 * WIDE, C), F32), pltpu.VMEM((176, C), F32)],
        compiler_params=limit(4),
        cost_estimate=BUSY,
        name="edge_rows",
    )(*args)


def ctx_rows(*args):
    return pl.pallas_call(
        ctx_rows_kernel,
        out_shape=(sds((112, C), BF), sds((112, C), BF)),
        in_specs=vmem(2),
        out_specs=tuple(vmem(2)),
        scratch_shapes=[pltpu.VMEM((176, C), F32)],
        compiler_params=limit(4),
        cost_estimate=BUSY,
        name="ctx_rows",
    )(*args)


def plan(*args):
    shapes = [((288, 160), BF), ((96, 16), BF), ((512, C), BF), ((SLOTS, EXT), BF), ((EXT, SLOTS), BF)]
    return pl.pallas_call(
        plan_kernel,
        out_shape=tuple(sds(*s) for s in shapes) + (sds((CAP, 1), jnp.int32), sds((1920, 384), BF)),
        in_specs=vmem(len(args)),
        out_specs=tuple(vmem(7)),
        scratch_shapes=[pltpu.VMEM((16, C), F32), pltpu.VMEM((16, C), F32)],
        compiler_params=limit(12),
        cost_estimate=BUSY,
        name="plan",
    )(*args)


def first_conv(*args):
    v = pltpu.VMEM
    edge = sds((48, C), BF)
    return pl.pallas_call(
        first_conv_kernel,
        out_shape=(sds((576, 1920), BF), sds((512, C), BF), sds((512, C), F32), edge, edge, sds((64, C), BF)),
        in_specs=vmem(len(args)),
        out_specs=tuple(vmem(6)),
        scratch_shapes=[
            v((18 * WIDE, C), F32),
            v((288, K), BF),
            v((160, K), BF),
            v((544, C), F32),
            v((544, C), F32),
            v((176, C), F32),
            v((576, 384), F32),
            pltpu.SMEM((4,), jnp.int32),
        ],
        compiler_params=limit(20),
        cost_estimate=pl.CostEstimate(flops=900_000_000, bytes_accessed=5_000_000, transcendentals=0),
        name="first_conv",
    )(*args)


def h_rows(*args):
    edge = sds((144, C), BF)
    return pl.pallas_call(
        h_rows_kernel,
        out_shape=(sds((ROWS * WIDE, C), BF), edge, edge),
        in_specs=vmem(len(args)),
        out_specs=tuple(vmem(3)),
        scratch_shapes=[pltpu.VMEM((ROWS * WIDE + WIDE, C), F32), pltpu.VMEM((2 * WIDE, C), F32)],
        compiler_params=limit(6),
        cost_estimate=BUSY,
        name="h_rows",
    )(*args)


def rest(*args):
    v = pltpu.VMEM
    return pl.pallas_call(
        rest_kernel,
        out_shape=sds((2, KEEP, C), BF),
        in_specs=vmem(len(args)),
        out_specs=vmem(1)[0],
        scratch_shapes=[
            v((1000, C), F32),
            v((992, 384), BF),
            v((EXT, C), F32),
            v((EXT, C), BF),
            v((SLOTS, C), BF),
            v((SLOTS, HID), BF),
            v((SLOTS, HID), F32),
            v((SLOTS, BINS), BF),
            v((SLOTS, HID), BF),
            v((SLOTS, 256), BF),
            v((EXT + 8, C), F32),
            v((960, 384), BF),
            v((576, 384), BF),
            v((992, 384), F32),
            pltpu.SMEM((4,), jnp.int32),
        ],
        compiler_params=limit(28),
        cost_estimate=pl.CostEstimate(flops=3_000_000_000, bytes_accessed=8_000_000, transcendentals=0),
        name="rest",
    )(*args)


def pair_sum(keep, got):
    return pl.pallas_call(
        pair_kernel,
        out_shape=sds((KEEP, C), BF),
        in_specs=vmem(2),
        out_specs=vmem(1)[0],
        compiler_params=limit(8),
        name="pair_sum",
    )(keep, got)


def spread(pieces):
    return pl.pallas_call(
        spread_kernel,
        out_shape=sds((PEERS, SHARD, C), BF),
        in_specs=vmem(1),
        out_specs=vmem(1)[0],
        scratch_shapes=[pltpu.VMEM((SHARD, C), BF)],
        compiler_params=limit(8),
        name="spread",
    )(pieces)


def finish(part, before=None):
    v = pltpu.VMEM
    shapes = [(1152, C), (2304, C), (1152, C), (C, HID), (HID, BINS)]
    second = before is not None
    more = tuple(before) if second else ()
    return pl.pallas_call(
        functools.partial(finish_kernel, second),
        out_shape=tuple(sds(s, F32) for s in shapes) + (sds((1, 1), F32),) * second,
        in_specs=vmem(1) + [ANY] * len(more),
        out_specs=(ANY,) * 5 + tuple(vmem(1)) * second,
        input_output_aliases={1 + n: n for n in range(len(more))},
        scratch_shapes=[v(s, F32) for s in shapes] + [pltpu.SemaphoreType.DMA((14,))],
        compiler_params=limit(16),
        cost_estimate=pl.CostEstimate(flops=800_000, bytes_accessed=5_000_000, transcendentals=0),
        name="finish_other" if second else "finish_own",
    )(part, *more)


def ring_cells():
    cells = [(0, c) for c in range(34)] + [(17, c) for c in range(34)]
    cells += [(r, 0) for r in range(1, 17)] + [(r, 33) for r in range(1, 17)]
    return np.array([WIDE * r + c for r, c in cells] + [-1] * 28, np.int32)


def local(
    fine,
    context,
    interp_rows,
    interp_cols,
    fine_weight,
    ctx_weight,
    conv_weight,
    hidden_weight,
    bin_weight,
    cell_index,
    counts,
    labels,
):
    idx = cell_index.reshape(1, CAP)
    live = jnp.arange(CAP, dtype=jnp.int32)[None, :] < counts
    lab = jnp.where(live, labels.reshape(1, CAP), -1)
    ring = jnp.asarray(ring_cells())

    last, first, fine, context = edge_cols(fine.reshape(512, C), context.reshape(64, HALF))
    east = shift(first, GX, 8, -1)
    west = shift(last, GX, 8, 1)
    kron, left, dig, pick, back, labs, weights = plan(
        interp_rows.T, interp_cols.T, idx, ring[None, :], lab,
        fine_weight.reshape(1152, C), ctx_weight.reshape(4608, C), last,
    )
    mine = edge_rows(fine, context, west, east)
    inner = side_swap(mine)
    down, up = ctx_rows(mine, inner)
    north = shift(down, GY, 8, 1)
    south = shift(up, GY, 8, -1)
    xc, h_one, sg1, last, first, digs = first_conv(
        kron, left, dig, fine, west, east, mine, inner, north, south, weights,
    )

    east = shift(first, GX, 8, -1)
    west = shift(last, GX, 8, 1)
    wide, inner, outer = h_rows(h_one, digs, west, east)
    outer = outer_swap(outer)
    inner = side_swap(inner)
    both = rest(
        wide, inner, outer, west, east, xc, sg1, pick, back, labs,
        conv_weight.reshape(1152, C), hidden_weight, bin_weight,
    )

    flip = [(0, 1), (1, 0)]
    pair = pair_sum(both, lax.ppermute(both[1], "core", flip))
    pieces = lax.all_to_all(pair.reshape(PEERS, SHARD, C), PLANE, 0, 0, tiled=True)
    half_sum = lax.all_to_all(spread(pieces), PLANE, 0, 0, tiled=True).reshape(KEEP, C)
    other = lax.ppermute(half_sum, "core", flip)
    outs = finish(half_sum)
    gfine, gctx, gconv, ghid, gbin, loss = finish(other, outs)
    return (
        loss.reshape(()),
        gfine.reshape(3, 3, C, C),
        gctx.reshape(3, 3, HALF, C),
        gconv.reshape(3, 3, C, C),
        ghid,
        gbin,
    )


def solution(mesh):
    devices = np.asarray(mesh.devices).reshape(4, 2, 4, 2, 2)
    split = Mesh(devices, ("x", "core", "z", "yl", "yh"))
    in_specs = (
        P(TALL, GX, None),
        P(GY, GX, "yh"),
        P(),
        P(),
        P(),
        P(),
        P(),
        P(),
        P(),
        P(TALL, GX, None),
        P(TALL, GX),
        P(TALL, GX, None),
    )
    out_specs = (P(), P(), P(None, None, "yh", None), P(), P(), P())
    return jax.shard_map(local, mesh=split, in_specs=in_specs, out_specs=out_specs, check_vma=False)
```

```python
import functools

import jax
import jax.numpy as jnp
import numpy as np
from jax import lax
from jax.experimental import pallas as pl
from jax.experimental.pallas import tpu as pltpu
from jax.sharding import Mesh
from jax.sharding import PartitionSpec as P

HID = 1024
BINS = 512
CAP = 256
ROWS = 16
COLS = 32
C = 128
K = 512
HALF = 256
SHARD = 96
PEERS = 64
BODY = 12032

GY = ("x", "core")
GX = ("z", "yl")
TALL = ("x", "core", "yh")
PLANE = ("x", "z", "yl", "yh")

BF = jnp.bfloat16
F32 = jnp.float32


def shift(x, axis, count, step):
    pairs = [(i, i + step) for i in range(count) if 0 <= i + step < count]
    return lax.ppermute(x, axis, pairs)


def side_swap(x):
    own = [(2 * t + c, 2 * t + 1 - c) for t in range(8) for c in range(2)]
    return lax.ppermute(x, TALL, own)


def outer_swap(x):
    pairs = []
    for t in range(7):
        pairs += [(2 * t + 1, 2 * t + 2), (2 * t + 2, 2 * t + 1)]
    return lax.ppermute(x, TALL, pairs)


WIDE = 48
CTX = 2 * WIDE
EXT = 896
SLOTS = 384
KEEP = PEERS * SHARD
STAT = BODY // 2
MIB = 1024 * 1024
BUSY = pl.CostEstimate(flops=5_000_000_000, bytes_accessed=1_000_000, transcendentals=0)


def limit(mib):
    return pltpu.CompilerParams(vmem_limit_bytes=mib * MIB)


def vmem(n):
    return [pl.BlockSpec(memory_space=pltpu.VMEM)] * n


ANY = pl.BlockSpec(memory_space=pl.ANY)


def dot(a, b):
    return jnp.dot(a, b, preferred_element_type=F32)


def dot_t(a, b):
    return lax.dot_general(a, b, (((1,), (1,)), ((), ())), preferred_element_type=F32)


def t_dot(a, b):
    return lax.dot_general(a, b, (((0,), (0,)), ((), ())), preferred_element_type=F32)


def iota(shape, dim):
    return lax.broadcasted_iota(jnp.int32, shape, dim)


def split3(v):
    hi = v.astype(BF)
    rest = v - hi.astype(F32)
    mid = rest.astype(BF)
    low = (rest - mid.astype(F32)).astype(BF)
    return [hi.astype(F32), mid.astype(F32), low.astype(F32)]


def stat_rows(v, like):
    hi, mid, low = split3(v)
    row = iota(like, 0)
    out = jnp.where(row == 0, hi, jnp.where(row == 1, mid, jnp.where(row == 2, low, 0.0)))
    return out


def edge_cols_kernel(fine_in, ctx_in, last, first, fine, ctx, fs, xs):
    fine[...] = fine_in[...]
    ctx[...] = ctx_in[...]
    fs[0:512, :] = fine[...].astype(F32)
    for side in range(2):
        xs[side, 0:64, :] = ctx[:, 128 * side : 128 * side + 128].astype(F32)
    for out, fc, xc in ((last, COLS - 1, 7), (first, 0, 0)):
        out[0:16, :] = fs[pl.ds(fc, 16, stride=COLS), :].astype(BF)
        sides = [xs.at[side][pl.ds(xc, 8, stride=8), :] for side in range(2)]
        out[16:32, :] = jnp.concatenate(sides, axis=0).astype(BF)


def edge_rows_kernel(fine, ctx, west, east, inner, rows, xs):
    rows[...] = jnp.zeros_like(rows)
    w, e = west[...].astype(F32), east[...].astype(F32)
    for n, r in ((0, 0), (1, ROWS - 1)):
        at = WIDE * n
        rows[at + 1 : at + 33, :] = fine[COLS * r : COLS * r + COLS, :].astype(F32)
        rows[at : at + 1, :] = w[r : r + 1, :]
        rows[at + 33 : at + 34, :] = e[r : r + 1, :]
    inner[0:CTX, :] = rows[...].astype(BF)
    for side in range(2):
        base = 80 * side
        lanes = slice(128 * side, 128 * side + 128)
        for a in range(8):
            at = base + 10 * a
            xs[at + 1 : at + 9, :] = ctx[8 * a : 8 * a + 8, lanes].astype(F32)
        xs[pl.ds(base, 8, stride=10), :] = w[16 + 8 * side : 24 + 8 * side, :]
        xs[pl.ds(base + 9, 8, stride=10), :] = e[16 + 8 * side : 24 + 8 * side, :]
    inner[CTX:, :] = xs[0:160, :].astype(BF)


def ctx_rows_kernel(mine, inner, down, up, xs):
    lower = lax.axis_index("yh") == 1
    xs[160:, :] = jnp.zeros((16, C), F32)
    for n, got in enumerate((mine, inner)):
        xs[0:160, :] = got[CTX:, :].astype(F32)
        for side in range(2):
            at, to = 80 * side, 32 * n + 16 * side
            up[to : to + 16, :] = xs[at : at + 16, :].astype(BF)
            down[to : to + 16, :] = xs[at + 70 : at + 86, :].astype(BF)
    up[64:112, :] = jnp.where(lower, inner[0:WIDE, :], mine[0:WIDE, :])
    down[64:112, :] = jnp.where(lower, mine[WIDE:CTX, :], inner[WIDE:CTX, :])


def column(row):
    n = row.shape[1]
    eye = iota((n, n), 0) == iota((n, n), 1)
    return jnp.sum(jnp.where(eye, row.astype(F32), 0.0), axis=1, keepdims=True)


def plan_kernel(
    rows_in, cols_in, idx_l, ring_l, lab_l, w_fine, w_ctx, cw, after,
    kron, left, digs, pick, back, labs, wide, forth, flipped, rmat, cmat,
):
    half = lax.axis_index("yh")
    row0 = (2 * lax.axis_index("x") + lax.axis_index("core")) * 32
    col0 = (2 * lax.axis_index("z") + lax.axis_index("yl")) * COLS
    rmat[...] = jnp.zeros_like(rmat)
    cmat[...] = jnp.zeros_like(cmat)
    grow = row0 + iota((10, 34), 1) - 1
    gcol = col0 + iota((10, 34), 1) - 1
    rmat[0:10, 0:34] = jnp.where((grow >= 0) & (grow < 256), rows_in[...].astype(F32), 0.0)
    cmat[0:10, 0:34] = jnp.where((gcol >= 0) & (gcol < 256), cols_in[...].astype(F32), 0.0)
    chosen = (iota((288, C), 0) >> 4) + 16 * half == iota((288, C), 1)
    side = dot_t(chosen.astype(F32).astype(BF), rmat[...].astype(BF)).astype(BF)
    spread = (iota((16, 160), 0) == iota((16, 160), 1) >> 4).astype(F32).astype(BF)
    full = dot(side, spread)
    same = (iota((288, 160), 0) & 15) == (iota((288, 160), 1) & 15)
    kron[...] = jnp.where(same, full, 0.0).astype(BF)
    cell = iota((96, C), 0)
    chosen = (cell & 31) + (cell >> 5) == iota((96, C), 1)
    left[...] = dot_t(chosen.astype(F32).astype(BF), cmat[...].astype(BF)).astype(BF)
    code = lab_l[...] + 1
    kind = iota((C, CAP), 0)
    digit = jnp.where(kind == 0, code >> 5, jnp.where(kind == 1, code & 31, 0))
    named = (idx_l[...] == iota((512, CAP), 0)).astype(F32).astype(BF)
    digs[...] = dot_t(named, digit.astype(F32).astype(BF)).astype(BF)
    slot_l = idx_l[...] + 16 * (idx_l[...] >> 5) + WIDE + 1
    slot_s = column(slot_l).astype(jnp.int32)
    ring_s = column(ring_l[...]).astype(jnp.int32)
    pick[0:CAP, :] = (slot_s == iota((CAP, EXT), 1)).astype(F32).astype(BF)
    pick[CAP:, :] = (ring_s == iota((SLOTS - CAP, EXT), 1)).astype(F32).astype(BF)
    cell = iota((EXT, CAP), 0)
    back[:, 0:CAP] = (slot_l == cell).astype(F32).astype(BF)
    back[:, CAP:] = (ring_l[...] == cell[:, :128]).astype(F32).astype(BF)
    labs[...] = column(lab_l[...]).astype(jnp.int32)
    for dy in range(3):
        lanes = slice(128 * dy, 128 * dy + 128)
        wide[0:384, lanes] = w_fine[384 * dy : 384 * dy + 384, :]
        wide[384:, lanes] = w_ctx[1536 * dy : 1536 * dy + 1536, :]
        forth[:, lanes] = cw[384 * dy : 384 * dy + 384, :]
        for dx in range(3):
            tap = cw[384 * dy + 128 * dx : 384 * dy + 128 * dx + 128, :]
            flipped[lanes, 128 * dx : 128 * dx + 128] = tap


def first_conv_kernel(
    kron, left, dig, fine, west, east, mine, inner, north, south, weights,
    xc, h1, sg, last, first, digs,
    fscr, mid, block, hscr, dscr, xs, pre, spot,
):
    spot[0] = lax.axis_index("yh")
    half = spot[0]
    lower = half == 1
    for i in range(ROWS):
        at = WIDE * (i + 1) + 1
        fscr[at : at + 32, :] = fine[32 * i : 32 * i + 32, :].astype(F32)
    fscr[pl.ds(WIDE, 16, stride=WIDE), :] = west[0:16, :].astype(F32)
    fscr[pl.ds(WIDE + 33, 16, stride=WIDE), :] = east[0:16, :].astype(F32)
    above = jnp.where(lower, inner[WIDE:CTX, :], north[64:112, :])
    below = jnp.where(lower, south[64:112, :], inner[0:WIDE, :])
    fscr[0:WIDE, :] = above.astype(F32)
    fscr[17 * WIDE : 18 * WIDE, :] = below.astype(F32)
    for i in range(ROWS + 2):
        for dx in range(3):
            at = WIDE * i + dx
            xc[32 * i : 32 * i + 32, 128 * dx : 128 * dx + 128] = fscr[at : at + 32, :].astype(BF)
    xs[160:, :] = jnp.zeros((16, C), F32)
    for n, part, got in ((0, half, mine), (32, 1 - half, inner)):
        xs[0:160, :] = got[CTX:, :].astype(F32)
        for side in range(2):
            lanes = pl.ds(pl.multiple_of(256 * part + 128 * side, 128), 128)
            sl = slice(n + 16 * side, n + 16 * side + 16)
            block[0:16, lanes] = north[sl, :]
            for a in range(8):
                at = 80 * side + 10 * a
                block[16 + 16 * a : 32 + 16 * a, lanes] = xs[at : at + 16, :].astype(BF)
            block[144:160, lanes] = south[sl, :]
    mid[...] = dot(kron[...], block[...]).astype(BF)
    for i in range(ROWS + 2):
        wide = dot(left[...], mid[16 * i : 16 * i + 16, :]).astype(BF)
        for dx in range(3):
            xc[32 * i : 32 * i + 32, 384 + 512 * dx : 896 + 512 * dx] = wide[32 * dx : 32 * dx + 32]
    pre[...] = dot(xc[...], weights[...])
    acc = sum(pre[32 * dy : 32 * dy + 512, 128 * dy : 128 * dy + 128] for dy in range(3))
    s = jax.nn.sigmoid(acc)
    h = (acc * s).astype(BF)
    h1[...] = h
    hscr[0:512, :] = h.astype(F32)
    sg[...] = s * (1.0 + acc * (1.0 - s))
    dscr[0:512, :] = dig[...].astype(F32)
    digs[0:32, :] = dscr[0:32, :].astype(BF)
    digs[32:64, :] = dscr[480:512, :].astype(BF)
    for out, c0, c1, cd in ((last, COLS - 2, COLS - 1, COLS - 1), (first, 0, 1, 0)):
        out[0:16, :] = hscr[pl.ds(c0, 16, stride=COLS), :].astype(BF)
        out[16:32, :] = hscr[pl.ds(c1, 16, stride=COLS), :].astype(BF)
        out[32:48, :] = dscr[pl.ds(cd, 16, stride=COLS), :].astype(BF)


def h_rows_kernel(h1, digs, west, east, wide, inner, outer, ws, ds):
    lower = lax.axis_index("yh") == 1
    w, e = west[...].astype(F32), east[...].astype(F32)
    ws[...] = jnp.zeros_like(ws)
    ds[...] = jnp.zeros_like(ds)
    for i in range(ROWS):
        ws[WIDE * i + 2 : WIDE * i + 34, :] = h1[32 * i : 32 * i + 32, :].astype(F32)
    for col, value in ((0, w[0:16]), (1, w[16:32]), (34, e[0:16]), (35, e[16:32])):
        ws[pl.ds(col, 16, stride=WIDE), :] = value
    for n, r in ((0, 0), (1, ROWS - 1)):
        at = WIDE * n
        ds[at + 1 : at + 33, :] = digs[32 * n : 32 * n + 32, :].astype(F32)
        ds[at : at + 1, :] = w[32 + r : 33 + r, :]
        ds[at + 33 : at + 34, :] = e[32 + r : 33 + r, :]
    wide[...] = ws[0 : ROWS * WIDE, :].astype(BF)
    top, bottom = ws[0:96, :].astype(BF), ws[14 * WIDE : 16 * WIDE, :].astype(BF)
    inner[0:96, :] = jnp.where(lower, top, bottom)
    outer[0:96, :] = jnp.where(lower, bottom, top)
    top, bottom = ds[0:WIDE, :].astype(BF), ds[WIDE : 2 * WIDE, :].astype(BF)
    inner[96:144, :] = jnp.where(lower, top, bottom)
    outer[96:144, :] = jnp.where(lower, bottom, top)


def rest_kernel(
    hw, inner, outer, west, east, xc, sg1, pick, back, labs_s, forth, flipped, hid, binw,
    out,
    hp, hx, sg2, h2, rows_s, act, sgz, dl, dz, gscr, gx, g2w, g1w, pre, spot,
):
    spot[0] = lax.axis_index("core")
    spot[1] = lax.axis_index("yh")
    core, lower = spot[0], spot[1] == 1
    a, b = inner[...].astype(F32), outer[...].astype(F32)
    before, after = jnp.where(lower, a, b), jnp.where(lower, b, a)
    hp[0:96, :] = before[0:96]
    hp[96:864, :] = hw[...].astype(F32)
    hp[864:960, :] = after[0:96]
    hp[960:1000, :] = jnp.zeros((40, C), F32)
    gx[...] = jnp.zeros_like(gx)
    gx[0:WIDE, :] = before[96:144]
    gx[17 * WIDE : 18 * WIDE, :] = after[96:144]
    gx[pl.ds(WIDE, 16, stride=WIDE), :] = west[32:48, :].astype(F32)
    gx[pl.ds(WIDE + 33, 16, stride=WIDE), :] = east[32:48, :].astype(F32)
    code = dot(pick[CAP:, :], gx[0:EXT, :].astype(BF))
    lane = iota((128, C), 1)
    code = jnp.sum(jnp.where(lane == 0, 32.0 * code, jnp.where(lane == 1, code, 0.0)), axis=1, keepdims=True)
    for dx in range(3):
        hx[:, 128 * dx : 128 * dx + 128] = hp[dx : dx + 992, :].astype(BF)
    pre[...] = dot(hx[...], forth[...])
    acc = sum(pre[WIDE * dy : WIDE * dy + EXT, 128 * dy : 128 * dy + 128] for dy in range(3))
    s = jax.nn.sigmoid(acc)
    h2[...] = (acc * s).astype(BF)
    sg2[...] = s * (1.0 + acc * (1.0 - s))
    rows = dot(pick[...], h2[...]).astype(BF)
    rows_s[...] = rows
    z = dot(rows, hid[...])
    s = jax.nn.sigmoid(z)
    act[...] = (z * s).astype(BF)
    sgz[...] = s * (1.0 + z * (1.0 - s))
    logits = dot(act[...], binw[...])
    peak = jnp.max(logits, axis=1, keepdims=True)
    top = peak + jnp.log(jnp.sum(jnp.exp(logits - peak), axis=1, keepdims=True))
    labs = jnp.concatenate([labs_s[...], code.astype(jnp.int32) - 1], axis=0)
    hit = labs == iota((SLOTS, BINS), 1)
    live = (labs >= 0).astype(F32)
    picked = jnp.sum(jnp.where(hit, logits, 0.0), axis=1, keepdims=True)
    loss = jnp.sum((live * (top - picked))[:CAP])
    dl[...] = ((jnp.exp(logits - top) - hit.astype(F32)) * live).astype(BF)
    dz[...] = (dot_t(dl[...], binw[...]) * sgz[...]).astype(BF)
    drows = dot_t(dz[...], hid[...])
    hi = drows.astype(BF)
    gscr[:, 0:128] = hi
    gscr[:, 128:256] = (drows - hi.astype(F32)).astype(BF)

    def put(row, value):
        out[(row // STAT) ^ core, pl.ds(row % STAT, value.shape[0]), :] = value.astype(BF)

    for n in range(4):
        put(7936 + 1024 * n, t_dot(act[0:CAP, :], dl[0:CAP, 128 * n : 128 * n + 128]))
    ghid = t_dot(rows_s[0:CAP, :], dz[0:CAP, :])
    for n in range(8):
        put(6912 + 128 * n, ghid[:, 128 * n : 128 * n + 128])
    lane = iota((1, C), 1)
    stats = jnp.where(lane == 0, loss, jnp.where(lane == 1, jnp.sum(live[:CAP]), 0.0))
    for n in range(2):
        out[n, STAT : STAT + 16, :] = stat_rows(stats, (16, C)).astype(BF)
        out[n, STAT + 16 : KEEP, :] = jnp.zeros((KEEP - STAT - 16, C), BF)
    both = dot(back[...], gscr[...])
    gx[0:EXT, :] = (both[:, :128] + both[:, 128:]) * sg2[...]

    g2w[...] = jnp.zeros_like(g2w)
    col = iota((WIDE, C), 0)
    inside = jnp.where((col >= 1) & (col <= COLS), 1.0, 0.0)
    own = (gx[WIDE : WIDE + 768, :] * jnp.concatenate([inside] * ROWS, axis=0)).astype(BF)
    for dy in range(3):
        g2w[WIDE * (1 + dy) : WIDE * (1 + dy) + 768, 128 * dy : 128 * dy + 128] = own
    for dx in range(3):
        part = t_dot(hx[0:960, 128 * dx : 128 * dx + 128], g2w[...])
        for dy in range(3):
            put(5760 + 128 * (3 * dy + dx), part[:, 128 * dy : 128 * dy + 128])

    for i in range(ROWS + 2):
        for dx in range(3):
            at = WIDE * i + 2 - dx
            hx[32 * i : 32 * i + 32, 128 * dx : 128 * dx + 128] = gx[at : at + 32, :].astype(BF)
    g1w[...] = jnp.zeros_like(g1w)
    pre[0:576, :] = dot_t(hx[0:576, :], flipped[...])
    acc = sum(pre[64 - 32 * dy : 576 - 32 * dy, 128 * dy : 128 * dy + 128] for dy in range(3))
    g1 = (acc * sg1[...]).astype(BF)
    for dy in range(3):
        g1w[32 * dy : 32 * dy + 512, 128 * dy : 128 * dy + 128] = g1
    for dx in range(3):
        part = t_dot(xc[:, 128 * dx : 128 * dx + 128], g1w[...])
        for dy in range(3):
            put(4608 + 128 * (3 * dy + dx), part[:, 128 * dy : 128 * dy + 128])
    for dx in range(3):
        for side in range(2):
            at = 384 + 512 * dx + 256 * side
            part = t_dot(g1w[...], xc[:, at : at + 256]).astype(BF)
            for dy in range(3):
                at = 2304 * side + 256 * (3 * dy + dx)
                put(at, part[128 * dy : 128 * dy + 128, :].T)


def pair_kernel(both, got, out):
    keep = both.at[0]
    out[...] = (keep[...].astype(F32) + got[...].astype(F32)).astype(BF)
    sl = slice(STAT, STAT + 16)
    rows = keep[sl, :].astype(F32) + got[sl, :].astype(F32)
    out[sl, :] = stat_rows(jnp.sum(rows, axis=0, keepdims=True), (16, C)).astype(BF)


def spread_kernel(pieces, out, mine):
    acc = pieces[0].astype(F32)
    for i in range(1, PEERS):
        acc += pieces[i].astype(F32)
    mine[...] = acc.astype(BF)
    at = STAT % SHARD

    place = [lax.axis_index(a) for a in PLANE]
    owner = 16 * place[0] + 4 * place[1] + 2 * place[2] + place[3]

    @pl.when(owner == STAT // SHARD)
    def _():
        rows = acc[at : at + 16]
        mine[at : at + 16, :] = stat_rows(jnp.sum(rows, axis=0, keepdims=True), (16, C)).astype(BF)

    for i in range(PEERS):
        out[i] = mine[...]


def finish_kernel(second, part, *refs):
    refs = refs[5:] if second else refs
    if second:
        loss, refs = refs[5], refs[:5] + refs[6:]
    gfine, gctx, gconv, ghid, gbin, vf, vx, vc, vh, vb, sem = refs
    half = lax.axis_index("yh")
    which = lax.axis_index("core")
    which = 1 - which if second else which
    stats = jnp.sum(part[STAT : STAT + 16, :].astype(F32), axis=0, keepdims=True)
    lane = iota((1, C), 1)
    total = jnp.sum(jnp.where(lane == 1, stats, 0.0), axis=1, keepdims=True)
    scale = 1.0 / total
    if second:
        loss[...] = jnp.sum(jnp.where(lane == 0, stats, 0.0), axis=1, keepdims=True) * scale

    def get(row, n):
        at = row % STAT
        return part[at : at + n, :].astype(F32) * scale

    def send(done, view, out):
        c = pltpu.make_async_copy(view, out, sem.at[len(done)])
        c.start()
        done.append(c)

    @pl.when(which == 0)
    def _():
        done = []
        at = pl.multiple_of(half * 2304, 128)
        for n in range(9):
            sl = slice(256 * n, 256 * n + 256)
            vx[sl, :] = part[pl.ds(at + 256 * n, 256), :].astype(F32) * scale
            send(done, vx.at[sl, :], gctx.at[sl, :])
        for n in range(3):
            sl = slice(384 * n, 384 * n + 384)
            vf[sl, :] = get(4608 + 384 * n, 384)
            send(done, vf.at[sl, :], gfine.at[sl, :])
        vc[0:256, :] = get(5760, 256)
        send(done, vc.at[0:256, :], gconv.at[0:256, :])
        for c in done:
            c.wait()

    @pl.when(which == 1)
    def _():
        done = []
        for m in range(8):
            sl = slice(128 * m, 128 * m + 128)
            for n in range(4):
                vb[sl, 128 * n : 128 * n + 128] = get(7936 + 1024 * n + 128 * m, 128)
            send(done, vb.at[sl, :], gbin.at[sl, :])
        for n in range(2):
            sl = slice(256 + 448 * n, 704 + 448 * n)
            vc[sl, :] = get(6016 + 448 * n, 448)
            send(done, vc.at[sl, :], gconv.at[sl, :])
        for m in range(4):
            sl = slice(32 * m, 32 * m + 32)
            for n in range(8):
                vh[sl, 128 * n : 128 * n + 128] = get(6912 + 128 * n + 32 * m, 32)
            send(done, vh.at[sl, :], ghid.at[sl, :])
        for c in done:
            c.wait()


def sds(shape, dtype):
    return jax.ShapeDtypeStruct(shape, dtype)


def edge_cols(fine, ctx):
    return pl.pallas_call(
        edge_cols_kernel,
        out_shape=(sds((32, C), BF),) * 2 + (sds((512, C), BF), sds((64, HALF), BF)),
        in_specs=vmem(2),
        out_specs=tuple(vmem(4)),
        scratch_shapes=[pltpu.VMEM((544, C), F32), pltpu.VMEM((2, 72, C), F32)],
        compiler_params=limit(4),
        cost_estimate=BUSY,
        name="edge_cols",
    )(fine, ctx)


def edge_rows(*args):
    return pl.pallas_call(
        edge_rows_kernel,
        out_shape=sds((CTX + 160, C), BF),
        in_specs=vmem(4),
        out_specs=vmem(1)[0],
        scratch_shapes=[pltpu.VMEM((2 * WIDE, C), F32), pltpu.VMEM((176, C), F32)],
        compiler_params=limit(4),
        cost_estimate=BUSY,
        name="edge_rows",
    )(*args)


def ctx_rows(*args):
    return pl.pallas_call(
        ctx_rows_kernel,
        out_shape=(sds((112, C), BF), sds((112, C), BF)),
        in_specs=vmem(2),
        out_specs=tuple(vmem(2)),
        scratch_shapes=[pltpu.VMEM((176, C), F32)],
        compiler_params=limit(4),
        cost_estimate=BUSY,
        name="ctx_rows",
    )(*args)


def plan(*args):
    shapes = [((288, 160), BF), ((96, 16), BF), ((512, C), BF), ((SLOTS, EXT), BF), ((EXT, SLOTS), BF)]
    return pl.pallas_call(
        plan_kernel,
        out_shape=tuple(sds(*s) for s in shapes) + (sds((CAP, 1), jnp.int32), sds((1920, 384), BF)) + (sds((384, 384), BF),) * 2,
        in_specs=vmem(len(args)),
        out_specs=tuple(vmem(9)),
        scratch_shapes=[pltpu.VMEM((16, C), F32), pltpu.VMEM((16, C), F32)],
        compiler_params=limit(12),
        cost_estimate=BUSY,
        name="plan",
    )(*args)


def first_conv(*args):
    v = pltpu.VMEM
    edge = sds((48, C), BF)
    return pl.pallas_call(
        first_conv_kernel,
        out_shape=(sds((576, 1920), BF), sds((512, C), BF), sds((512, C), F32), edge, edge, sds((64, C), BF)),
        in_specs=vmem(len(args)),
        out_specs=tuple(vmem(6)),
        scratch_shapes=[
            v((18 * WIDE, C), F32),
            v((288, K), BF),
            v((160, K), BF),
            v((544, C), F32),
            v((544, C), F32),
            v((176, C), F32),
            v((576, 384), F32),
            pltpu.SMEM((4,), jnp.int32),
        ],
        compiler_params=limit(20),
        cost_estimate=pl.CostEstimate(flops=900_000_000, bytes_accessed=5_000_000, transcendentals=0),
        name="first_conv",
    )(*args)


def h_rows(*args):
    edge = sds((144, C), BF)
    return pl.pallas_call(
        h_rows_kernel,
        out_shape=(sds((ROWS * WIDE, C), BF), edge, edge),
        in_specs=vmem(len(args)),
        out_specs=tuple(vmem(3)),
        scratch_shapes=[pltpu.VMEM((ROWS * WIDE + WIDE, C), F32), pltpu.VMEM((2 * WIDE, C), F32)],
        compiler_params=limit(6),
        cost_estimate=BUSY,
        name="h_rows",
    )(*args)


def rest(*args):
    v = pltpu.VMEM
    return pl.pallas_call(
        rest_kernel,
        out_shape=sds((2, KEEP, C), BF),
        in_specs=vmem(len(args)),
        out_specs=vmem(1)[0],
        scratch_shapes=[
            v((1000, C), F32),
            v((992, 384), BF),
            v((EXT, C), F32),
            v((EXT, C), BF),
            v((SLOTS, C), BF),
            v((SLOTS, HID), BF),
            v((SLOTS, HID), F32),
            v((SLOTS, BINS), BF),
            v((SLOTS, HID), BF),
            v((SLOTS, 256), BF),
            v((EXT + 8, C), F32),
            v((960, 384), BF),
            v((576, 384), BF),
            v((992, 384), F32),
            pltpu.SMEM((4,), jnp.int32),
        ],
        compiler_params=limit(28),
        cost_estimate=pl.CostEstimate(flops=3_000_000_000, bytes_accessed=8_000_000, transcendentals=0),
        name="rest",
    )(*args)


def pair_sum(keep, got):
    return pl.pallas_call(
        pair_kernel,
        out_shape=sds((KEEP, C), BF),
        in_specs=vmem(2),
        out_specs=vmem(1)[0],
        compiler_params=limit(8),
        name="pair_sum",
    )(keep, got)


def spread(pieces):
    return pl.pallas_call(
        spread_kernel,
        out_shape=sds((PEERS, SHARD, C), BF),
        in_specs=vmem(1),
        out_specs=vmem(1)[0],
        scratch_shapes=[pltpu.VMEM((SHARD, C), BF)],
        compiler_params=limit(8),
        name="spread",
    )(pieces)


def finish(part, before=None):
    v = pltpu.VMEM
    shapes = [(1152, C), (2304, C), (1152, C), (C, HID), (HID, BINS)]
    second = before is not None
    more = tuple(before) if second else ()
    return pl.pallas_call(
        functools.partial(finish_kernel, second),
        out_shape=tuple(sds(s, F32) for s in shapes) + (sds((1, 1), F32),) * second,
        in_specs=vmem(1) + [ANY] * len(more),
        out_specs=(ANY,) * 5 + tuple(vmem(1)) * second,
        input_output_aliases={1 + n: n for n in range(len(more))},
        scratch_shapes=[v(s, F32) for s in shapes] + [pltpu.SemaphoreType.DMA((14,))],
        compiler_params=limit(16),
        cost_estimate=pl.CostEstimate(flops=800_000, bytes_accessed=5_000_000, transcendentals=0),
        name="finish_other" if second else "finish_own",
    )(part, *more)


def ring_cells():
    cells = [(0, c) for c in range(34)] + [(17, c) for c in range(34)]
    cells += [(r, 0) for r in range(1, 17)] + [(r, 33) for r in range(1, 17)]
    return np.array([WIDE * r + c for r, c in cells] + [-1] * 28, np.int32)


def local(
    fine,
    context,
    interp_rows,
    interp_cols,
    fine_weight,
    ctx_weight,
    conv_weight,
    hidden_weight,
    bin_weight,
    cell_index,
    counts,
    labels,
):
    idx = cell_index.reshape(1, CAP)
    live = jnp.arange(CAP, dtype=jnp.int32)[None, :] < counts
    lab = jnp.where(live, labels.reshape(1, CAP), -1)
    ring = jnp.asarray(ring_cells())

    last, first, fine, context = edge_cols(fine.reshape(512, C), context.reshape(64, HALF))
    east = shift(first, GX, 8, -1)
    west = shift(last, GX, 8, 1)
    kron, left, dig, pick, back, labs, weights, forth, flipped = plan(
        interp_rows.T, interp_cols.T, idx, ring[None, :], lab,
        fine_weight.reshape(1152, C), ctx_weight.reshape(4608, C), conv_weight.reshape(1152, C), last,
    )
    mine = edge_rows(fine, context, west, east)
    inner = side_swap(mine)
    down, up = ctx_rows(mine, inner)
    north = shift(down, GY, 8, 1)
    south = shift(up, GY, 8, -1)
    xc, h_one, sg1, last, first, digs = first_conv(
        kron, left, dig, fine, west, east, mine, inner, north, south, weights,
    )

    east = shift(first, GX, 8, -1)
    west = shift(last, GX, 8, 1)
    wide, inner, outer = h_rows(h_one, digs, west, east)
    outer = outer_swap(outer)
    inner = side_swap(inner)
    both = rest(
        wide, inner, outer, west, east, xc, sg1, pick, back, labs,
        forth, flipped, hidden_weight, bin_weight,
    )

    flip = [(0, 1), (1, 0)]
    pair = pair_sum(both, lax.ppermute(both[1], "core", flip))
    pieces = lax.all_to_all(pair.reshape(PEERS, SHARD, C), PLANE, 0, 0, tiled=True)
    half_sum = lax.all_to_all(spread(pieces), PLANE, 0, 0, tiled=True).reshape(KEEP, C)
    other = lax.ppermute(half_sum, "core", flip)
    outs = finish(half_sum)
    gfine, gctx, gconv, ghid, gbin, loss = finish(other, outs)
    return (
        loss.reshape(()),
        gfine.reshape(3, 3, C, C),
        gctx.reshape(3, 3, HALF, C),
        gconv.reshape(3, 3, C, C),
        ghid,
        gbin,
    )


def solution(mesh):
    devices = np.asarray(mesh.devices).reshape(4, 2, 4, 2, 2)
    split = Mesh(devices, ("x", "core", "z", "yl", "yh"))
    in_specs = (
        P(TALL, GX, None),
        P(GY, GX, "yh"),
        P(),
        P(),
        P(),
        P(),
        P(),
        P(),
        P(),
        P(TALL, GX, None),
        P(TALL, GX),
        P(TALL, GX, None),
    )
    out_specs = (P(), P(), P(None, None, "yh", None), P(), P(), P())
    return jax.shard_map(local, mesh=split, in_specs=in_specs, out_specs=out_specs, check_vma=False)
```
